128 devices in a mesh: dp: 32 (over x, z, y_hi), space: 4 (over y_lo, core).
Axes of the slice: x: 4, y: 4 (y_hi: 2, y_lo: 2; y = y_hi * 2 + y_lo), z: 4, core: 2. Of those that a mesh axis runs over, the one named last changes fastest.
Arguments:
- features: bfloat16 [32, 48, 56, 1024], P('dp', 'space'), may hold values from -6 to 6
- labels: int32 [32, 48, 56], P('dp', 'space'), may hold values from 0 to 2
- w_one: bfloat16 [1024, 256], replicated, may hold values from -0.1875 to 0.1875
- w_atrous: bfloat16 [2, 3, 3, 1024, 256], replicated, may hold values from -0.0625 to 0.0625
- w_proj: bfloat16 [768, 256], replicated, may hold values from -0.21875 to 0.21875
- w_class: bfloat16 [256, 3], replicated, may hold values from -1.5 to 1.5
Outputs:
- grad_atrous: float32 [2, 3, 3, 1024, 256], P(None, None, None, ('dp', 'space'))
- grad_one: float32 [1024, 256], replicated
- grad_proj: float32 [768, 256], replicated
- grad_class: float32 [256, 3], replicated
- mean_loss: float32 [], replicated
The draws below stay inside these ranges and needn't reach their ends.
All inputs are finite; a program needn't handle non-finite values.
Results may differ from the reference program's by a relative error of at most 0.0043.
Values may be sent and summed in bfloat16 or wider, within the bound.
A program may use at most 192 MiB of HBM per device.

```python
import math
import jax
import jax.numpy as jnp
from jax import lax

IN_CH = 1024
OUT_CH = 256
CLASSES = 3
ATROUS = 2
RATE_A = 12
RATE_B = 18
WIDTH = 56
HEIGHT = 48
SAMPLES = 32
TOTAL_PIX = 86016


def place_ends(entries, rng, low, high):
    spot = [jax.random.randint(jax.random.fold_in(rng, axis), (), 0, length) for axis, length in enumerate(entries.shape)]
    widest = entries.shape.index(max(entries.shape))
    neighbour = spot[:widest] + [(spot[widest] + 1) % entries.shape[widest]] + spot[widest + 1:]
    return entries.at[tuple(spot)].set(low).at[tuple(neighbour)].set(high)


def with_spikes(array, key, source, target, parts, factor):
    def block_of(position):
        return (jnp.arange(array.shape[position]) // (array.shape[position] // parts)).reshape((-1,) + (1,) * (array.ndim - 1 - position))

    first = jax.random.permutation(key, parts)[block_of(target)]
    second = (block_of(target) + parts // 2) % parts
    return jnp.where((block_of(source) == first) | (block_of(source) == second), factor * array, array)


def block_levels(rng, extent, shards, least, top_value):
    level = 1.0
    for dim, shards_of in shards:
        heights = jax.random.uniform(jax.random.fold_in(jax.random.fold_in(rng, 6), dim), (shards_of,), jnp.float32, least / len(shards), top_value / len(shards))
        level = level * jnp.repeat(jnp.exp(heights), extent[dim] // shards_of).reshape((-1,) + (1,) * (len(extent) - 1 - dim))
    return level


def gaussian(key, shape, spread, most, pieces=(), held_as=jnp.bfloat16):
    factor_of = block_levels(key, shape, pieces, -0.22, 0.18) if pieces else 1.0
    array = jax.random.normal(key, shape, jnp.float32) * spread * factor_of
    return jnp.minimum(jnp.maximum(array, -most), most).astype(held_as)


def heavy_noise(stream_key, dims, scale, most, cuts, heavy, kind=jnp.bfloat16):
    values = scale * jax.random.normal(stream_key, dims, jnp.float32)
    if cuts:
        values = values * block_levels(stream_key, dims, cuts, -0.22, 0.18)
    return jnp.clip(with_spikes(values, jax.random.fold_in(stream_key, 3), *heavy), -most, most).astype(kind)


def setup_inputs(seed: int = 0) -> dict:
    key_of = jax.random.split(jax.random.key(seed), 7)
    features = heavy_noise(key_of[0], (SAMPLES, HEIGHT, WIDTH, IN_CH), 1.0, 6.0, ((0, 32), (1, 4)), (0, 3, 32, 2.75))
    labels = place_ends(jax.random.randint(key_of[1], (SAMPLES, HEIGHT, WIDTH), 0, CLASSES), jax.random.fold_in(key_of[1], 1), 0, CLASSES - 1).astype(jnp.int32)
    w_one = gaussian(key_of[2], (IN_CH, OUT_CH), IN_CH ** -0.5, 0.1875)
    w_atrous = gaussian(key_of[3], (ATROUS, 3, 3, IN_CH, OUT_CH), (9 * IN_CH) ** -0.5, 0.0625)
    w_proj = gaussian(key_of[4], (3 * OUT_CH, OUT_CH), (3 * OUT_CH) ** -0.5, 0.21875)
    w_class = gaussian(key_of[5], (OUT_CH, CLASSES), (OUT_CH // 16) ** -0.5, 1.5)
    return {"features": features, "labels": labels, "w_one": w_one, "w_atrous": w_atrous, "w_proj": w_proj, "w_class": w_class}


def silu_slope(pre):
    gate = jax.nn.sigmoid(pre)
    return gate * (1.0 + pre * (1.0 - gate))

def atrous_sum(padded, weights, rate, height, width, margin):
    summed = jnp.zeros((height * width, weights.shape[-1]), jnp.float32)
    for row_tap in range(3):
        for col_tap in range(3):
            top = margin + (row_tap - 1) * rate
            left = margin + (col_tap - 1) * rate
            window = padded[top:top + height, left:left + width].reshape(height * width, -1)
            summed = summed + jnp.dot(window, weights[row_tap, col_tap], preferred_element_type=jnp.float32)
    return summed

def left_product(first, second):
    return lax.dot_general(first, second, (((0,), (0,)), ((), ())), preferred_element_type=jnp.float32)

def right_product(first, second):
    return lax.dot_general(first, second, (((1,), (1,)), ((), ())), preferred_element_type=jnp.float32)

def atrous_grad(padded, branch_grad, rate, height, width, margin):
    blocks = []
    for row_tap in range(3):
        for col_tap in range(3):
            top = margin + (row_tap - 1) * rate
            left = margin + (col_tap - 1) * rate
            window = padded[top:top + height, left:left + width].reshape(height * width, -1)
            blocks.append(left_product(window, branch_grad))
    return jnp.stack(blocks).reshape(3, 3, blocks[0].shape[0], blocks[0].shape[1])

def head_terms(padded, label_map, w_one, w_atrous, w_proj, w_class, height, width, loss_scale):
    margin = RATE_B
    center = padded[margin:margin + height, margin:margin + width].reshape(height * width, -1)
    pre_list = (jnp.dot(center, w_one, preferred_element_type=jnp.float32), atrous_sum(padded, w_atrous[0], RATE_A, height, width, margin), atrous_sum(padded, w_atrous[1], RATE_B, height, width, margin))
    branch_list = tuple((jax.nn.silu(pre).astype(jnp.bfloat16) for pre in pre_list))
    joined = jnp.concatenate(branch_list, axis=1)
    pre_hidden = jnp.dot(joined, w_proj, preferred_element_type=jnp.float32)
    hidden = jax.nn.silu(pre_hidden).astype(jnp.bfloat16)
    logits = jnp.dot(hidden, w_class, preferred_element_type=jnp.float32)
    log_total = jnp.log(lax.optimization_barrier(jnp.sum(jnp.exp(logits), axis=1)))
    onehot = (label_map.reshape(-1)[:, None] == jnp.arange(logits.shape[1], dtype=jnp.int32)[None, :]).astype(jnp.float32)
    loss_sum = jnp.sum(log_total - lax.optimization_barrier(jnp.sum(onehot * logits, axis=1)))
    softmax_probs = jnp.exp(logits - log_total[:, None])
    dlogits = ((softmax_probs - onehot) * loss_scale).astype(jnp.bfloat16)
    grad_class = left_product(hidden, dlogits)
    hidden_grad = (right_product(dlogits, w_class) * silu_slope(pre_hidden)).astype(jnp.bfloat16)
    grad_proj = left_product(joined, hidden_grad)
    joined_grad = right_product(hidden_grad, w_proj)
    out_width = w_proj.shape[1]
    branch_grads = []
    for branch_index in range(3):
        block = joined_grad[:, branch_index * out_width:(branch_index + 1) * out_width]
        branch_grads.append((block * silu_slope(pre_list[branch_index])).astype(jnp.bfloat16))
    grad_one = left_product(center, branch_grads[0])
    grad_atrous = jnp.stack([atrous_grad(padded, branch_grads[1], RATE_A, height, width, margin), atrous_grad(padded, branch_grads[2], RATE_B, height, width, margin)])
    return (grad_atrous, grad_one, grad_proj, grad_class, loss_sum)

def reference(features, labels, w_one, w_atrous, w_proj, w_class):
    loss_scale = 1.0 / math.sqrt(TOTAL_PIX)

    def accumulate(carry, inputs):
        sample_image, label_map = inputs
        padded = jnp.pad(sample_image, ((RATE_B, RATE_B), (RATE_B, RATE_B), (0, 0)))
        terms = head_terms(padded, label_map, w_one, w_atrous, w_proj, w_class, HEIGHT, WIDTH, loss_scale)
        return (tuple((old + new for old, new in zip(carry, terms))), None)
    initial = (jnp.zeros((ATROUS, 3, 3, IN_CH, OUT_CH), jnp.float32), jnp.zeros((IN_CH, OUT_CH), jnp.float32), jnp.zeros((3 * OUT_CH, OUT_CH), jnp.float32), jnp.zeros((OUT_CH, CLASSES), jnp.float32), jnp.zeros((), jnp.float32))
    summed, _ = lax.scan(accumulate, initial, (features, labels))
    return (summed[0], summed[1], summed[2], summed[3], summed[4] / TOTAL_PIX)
```

```python
import math

import jax
import jax.numpy as jnp
from jax import lax
from jax.experimental import pallas as pl
from jax.experimental.pallas import tpu as pltpu
from jax.sharding import PartitionSpec as P

MESH = pl.DeviceIdType.MESH
BF = jnp.bfloat16
F32 = jnp.float32
WIDTH = 56
BLK = 6 * WIDTH
OWN = 12 * WIDTH
CHIP = 24 * WIDTH
BASE = 3
ORDERS = ("xzy", "zyx", "yxz", "zxy")
AXES = "xzy"


def slope(pre):
    gate = jax.nn.sigmoid(pre)
    return gate * (1.0 + pre * (1.0 - gate))


def silu(pre):
    return pre * jax.nn.sigmoid(pre)


def mm(first, second):
    return jnp.dot(first, second, preferred_element_type=F32)


def mm_t(first, second):
    return lax.dot_general(first, second, (((1,), (1,)), ((), ())), preferred_element_type=F32)


def t_mm(first, second):
    return lax.dot_general(first, second, (((0,), (0,)), ((), ())), preferred_element_type=F32)


def kernel(
    loss_scale,
    feat, labels, w_one_h, w_atr_h, w_proj, w_cls,
    o_atr, o_one, o_proj, o_cls,
    xbuf, xt, wbuf, wone, tacc, pre, pre0, cs, cr, joined, dh, ext, db0, raw, hraw,
    s1, r1, s2, r2, s3, r3, fin, pbuf, e1, eout, eoth, clbuf, swap,
    lsem, ssem, rsem,
):
    dp = lax.axis_index("dp")
    sp = lax.axis_index("space")
    core, s = sp % 2, sp // 2
    cx, cz, cy = dp // 8, (dp // 2) % 4, (dp % 2) * 2 + s
    here = {"x": cx, "z": cz, "y": cy}

    def place(x, z, y, c):
        return (x * 8 + z * 2 + y // 2, (y % 2) * 2 + c)

    partner = place(cx, cz, cy, 1 - core)
    across = (dp, (1 - s) * 2 + core)

    def peer(axis, d):
        at = dict(here)
        at[axis] = (at[axis] + d) % 4
        return place(at["x"], at["z"], at["y"], core)

    rate = 12 + 6 * core
    k = 2 + core

    counter = [0]

    def remote(src, dst, to):
        i = counter[0]
        counter[0] += 1
        return pltpu.make_async_remote_copy(
            src_ref=src, dst_ref=dst, send_sem=ssem.at[i], recv_sem=rsem.at[i], device_id=to, device_id_type=MESH
        )

    sends = []

    def go(copy):
        copy.start()
        sends.append(copy)
        return copy

    own_rows = pl.ds(pl.multiple_of(core * OWN, 16), OWN)
    other_rows = pl.ds(pl.multiple_of((1 - core) * OWN, 16), OWN)
    x_local = pltpu.make_async_copy(feat, xbuf.at[own_rows], lsem.at[0])
    x_local.start()
    w_local = [pltpu.make_async_copy(w_atr_h.at[core, a], wbuf.at[a], lsem.at[1 + a]) for a in range(3)]
    for copy in w_local:
        copy.start()
    one_local = pltpu.make_async_copy(w_one_h, wone, lsem.at[4])
    one_local.start()

    barrier = pltpu.get_barrier_semaphore()
    greet = [partner] + [peer(axis, d) for axis in AXES for d in (1, 2, 3)]
    for other in greet:
        pl.semaphore_signal(barrier, inc=1, device_id=other, device_id_type=MESH)
    pl.semaphore_wait(barrier, len(greet))

    x_swap = go(remote(feat, xbuf.at[own_rows], partner))

    zero = jnp.zeros((BLK, 256), BF)
    for b in range(3):
        for m in (0, 1, 2, 7, 8, 9):
            ext[b, pl.ds(m * BLK, BLK), :] = zero

    column = lax.rem(lax.broadcasted_iota(jnp.int32, (BLK, 256), 0), WIDTH)

    def from_left(value):
        return jnp.where(column >= rate, pltpu.roll(value, rate, 0), 0.0)

    def from_right(value):
        return jnp.where(column < WIDTH - rate, pltpu.roll(value, BLK - rate, 0), 0.0)

    def block(m):
        return pl.ds(pl.multiple_of(m * BLK, 16), BLK)

    x_local.wait()
    x_swap.wait_recv()
    for copy in w_local:
        copy.wait()
    cross_tap = s * 2
    cross_copies = [remote(cs.at[t], cr.at[t], across) for t in range(3)]
    for t in range(3):
        @pl.when(t < k)
        def _(t=t):
            src = jnp.where(s == 0, 4 + t - k, t)
            rows = xbuf[block(src), :]
            parts = [mm(rows, wbuf[cross_tap, b]) for b in range(3)]
            cs[t] = (parts[1] + from_left(parts[0]) + from_right(parts[2])).astype(BF)
            cross_copies[t].start()

    @pl.loop(0, 4)
    def _(i):
        rows = xbuf[block(i), :]
        for b in range(3):
            tacc[b] = mm(rows, wbuf[1, b])
        for a in (0, 2):
            src = i + (a - 1) * k

            @pl.when((src >= 0) & (src < 4))
            def _(a=a, src=src):
                shifted = xbuf[block(src), :]
                for b in range(3):
                    tacc[b] += mm(shifted, wbuf[a, b])
        pre[block(i), :] = tacc[1] + from_left(tacc[0]) + from_right(tacc[2])

    one_local.wait()

    @pl.when(core == 1)
    def _():
        @pl.loop(0, 4)
        def _(i):
            value = mm(xbuf[block(i), :], wone[...])
            pre0[block(i), :] = value
            joined[0, block(i), :] = silu(value).astype(BF)

    for t in range(3):
        @pl.when(t < k)
        def _(t=t):
            cross_copies[t].wait_recv()
            into = block(jnp.where(s == 0, 4 - k + t, t))
            pre[into, :] += cr[t].astype(F32)

    @pl.loop(0, 4)
    def _(i):
        joined[1 + core, block(i), :] = silu(pre[block(i), :]).astype(BF)

    j_copies = [remote(joined.at[b, other_rows], joined.at[b, other_rows], partner) for b in range(3)]

    @pl.when(core == 0)
    def _():
        j_copies[1].start()

    @pl.when(core == 1)
    def _():
        j_copies[0].start()
        j_copies[2].start()

    for c in range(4):
        xt[c] = xbuf[:, c * 256 : (c + 1) * 256].T

    @pl.when(core == 0)
    def _():
        j_copies[0].wait_recv()
        j_copies[2].wait_recv()

    @pl.when(core == 1)
    def _():
        j_copies[1].wait_recv()

    pre_hidden = mm(joined[0, own_rows, :], w_proj[0])
    pre_hidden += mm(joined[1, own_rows, :], w_proj[1])
    pre_hidden += mm(joined[2, own_rows, :], w_proj[2])
    hidden = silu(pre_hidden).astype(BF)
    logits = mm_t(w_cls[...], hidden)
    row = lax.broadcasted_iota(jnp.int32, logits.shape, 0)
    valid = row < 3
    top = jnp.max(jnp.where(valid, logits, -jnp.inf), axis=0, keepdims=True)
    total = jnp.sum(jnp.where(valid, jnp.exp(logits - top), 0.0), axis=0, keepdims=True)
    lse = top + jnp.log(total)
    onehot = row == labels[...]
    loss = jnp.sum(lse - jnp.sum(jnp.where(onehot, logits, 0.0), axis=0, keepdims=True), axis=1, keepdims=True)
    probs = jnp.exp(logits - lse) - jnp.where(onehot, 1.0, 0.0)
    dlogits = jnp.where(valid, probs * loss_scale, 0.0).astype(BF)
    dhidden = t_mm(dlogits, w_cls[...]) * slope(pre_hidden)
    dh[own_rows, :] = dhidden.astype(BF)
    dh_copy = go(remote(dh.at[own_rows], dh.at[own_rows], partner))

    small = mm(dlogits, hidden)
    srow = lax.broadcasted_iota(jnp.int32, small.shape, 0)
    cl_copies = []
    for n, axis in enumerate(AXES):
        cl_copies.append([remote(clbuf.at[n, here[axis]], clbuf.at[n, here[axis]], peer(axis, d)) for d in (1, 2, 3)])
    cl_copies.append([remote(clbuf.at[3, core], clbuf.at[3, core], partner)])
    clbuf[0, here["x"]] = jnp.where(srow == 3, loss, small)
    for copy in cl_copies[0]:
        go(copy)

    def small_step(n):
        for copy in cl_copies[n]:
            copy.wait_recv()
        value = clbuf[n, 0] + clbuf[n, 1]
        if n < 3:
            value = value + clbuf[n, 2] + clbuf[n, 3]
            clbuf[n + 1, core if n == 2 else here[AXES[n + 1]]] = value
            for copy in cl_copies[n + 1]:
                go(copy)
        else:
            o_cls[...] = value

    dh_copy.wait_recv()
    branch_w = w_proj[1 + core]
    raw_copies = [remote(raw.at[block(jnp.where(s == 0, 4 - k + t, t))], hraw.at[t], across) for t in range(3)]

    @pl.loop(0, 4)
    def _(i):
        value = mm_t(dh[block(i), :], branch_w) * slope(pre[block(i), :])
        raw[block(i), :] = value.astype(BF)
        to = block(BASE + i)
        rounded = value.astype(BF).astype(F32)
        ext[0, to, :] = from_right(rounded).astype(BF)
        ext[1, to, :] = rounded.astype(BF)
        ext[2, to, :] = from_left(rounded).astype(BF)

    for t in range(3):
        @pl.when(t < k)
        def _(t=t):
            raw_copies[t].start()

    def three(p, phase, buf, landing):
        axis = ORDERS[p][phase]
        left = [a for a in AXES if a in ORDERS[p][phase:]]
        spot = left.index(axis)

        def chunk(at):
            return buf.at[(slice(None),) * (1 + spot) + (at,)]

        return [remote(chunk((here[axis] + d) % 4), landing.at[d - 1], peer(axis, d)) for d in (1, 2, 3)], chunk(here[axis])

    plans = []
    for p in range(4):
        taps = 3 if p < 3 else 1
        sl = slice(3 * p, 3 * p + 3) if p < 3 else slice(9, 10)
        first = s1.at[p] if p < 3 else e1
        lead = pl.ds(sl.start, taps)
        bufs = (first, s2.at[lead], s3.at[lead])
        lands = (r1.at[:, lead], r2.at[:, lead], r3.at[:, lead])
        plan = []
        for phase in range(3):
            copies, mine = three(p, phase, bufs[phase], lands[phase])
            plan.append((copies, mine, lands[phase]))
        plans.append((plan, bufs, taps, lead))

    def send(p, phase):
        for copy in plans[p][0][phase][0]:
            go(copy)

    def settle(p, phase):
        plan, bufs, taps, lead = plans[p]
        copies, mine, landing = plan[phase]
        for copy in copies:
            copy.wait_recv()

        def one(t):
            value = mine[t].astype(F32)
            for d in range(3):
                value = value + landing[d, t].astype(F32)
            if phase < 2:
                bufs[phase + 1][t] = value.astype(BF)
            else:
                fin[lead.start + t] = value

        if taps == 1:
            one(0)
        else:
            pl.loop(0, taps)(one)
        if phase < 2:
            send(p, phase + 1)

    def proj_grad(b):
        return t_mm(joined[b], dh[...]).astype(BF).reshape(4, 4, 16, 256)

    p_copies = [remote(pbuf.at[n], e1.at[0, 2 * n], partner) for n in range(2)]

    @pl.when(core == 1)
    def _():
        for n in range(2):
            pbuf[n] = proj_grad(2 * n)
            p_copies[n].start()

        @pl.loop(0, 4)
        def _(i):
            value = mm_t(dh[block(i), :], w_proj[0]) * slope(pre0[block(i), :])
            db0[block(i), :] = value.astype(BF)

        @pl.loop(0, 4)
        def _(c):
            e1[0, c] = mm(xt[c], db0[...]).astype(BF).reshape(4, 4, 16, 256)

    @pl.when(core == 0)
    def _():
        e1[0, 1] = proj_grad(1)
        e1[0, 3] = jnp.zeros((4, 4, 16, 256), BF)
        for n in range(2):
            p_copies[n].wait_recv()

    send(3, 0)

    def part(a):
        p = jnp.where(a == 1, 0, 1 + a // 2)
        start = pl.ds(pl.multiple_of((BASE - (a - 1) * k) * BLK, 16), CHIP)

        @pl.loop(0, 4)
        def _(c):
            for b in range(3):
                s1[p, b, c] = mm(xt[c], ext[b, start, :]).astype(BF).reshape(4, 4, 16, 256)

    def outer_send(toward):
        for p in (1, 2):
            @pl.when((s == p - 1) == toward)
            def _(p=p):
                for copy in plans[p][0][0][0]:
                    copy.start()

    part(1)
    send(0, 0)
    small_step(0)
    part(2 - cross_tap)
    outer_send(False)
    settle(3, 0)

    for t in range(3):
        @pl.when(t < k)
        def _(t=t):
            raw_copies[t].wait_recv()
            to = block(jnp.where(s == 0, BASE + 4 + t, BASE - k + t))
            value = hraw[t].astype(F32)
            ext[0, to, :] = from_right(value).astype(BF)
            ext[1, to, :] = hraw[t]
            ext[2, to, :] = from_left(value).astype(BF)

    part(cross_tap)
    outer_send(True)
    for p in (1, 2):
        sends.extend(plans[p][0][0][0])
    small_step(1)
    settle(3, 1)
    settle(0, 0)
    settle(3, 2)

    spots = {"x": cx, "z": cz, "y": cy}
    eout[cx, cz, cy] = fin[9].astype(BF)

    def gather(phase):
        axis = ORDERS[3][phase]
        done = ORDERS[3][phase + 1 :]
        at = tuple(slice(None) if a in done else spots[a] for a in AXES)
        return [remote(eout.at[at], eout.at[at], peer(axis, d)) for d in (1, 2, 3)]

    gathers = [gather(phase) for phase in range(3)]
    for copy in gathers[2]:
        go(copy)
    small_step(2)
    settle(1, 0)
    for copy in gathers[2]:
        copy.wait_recv()
    for copy in gathers[1]:
        go(copy)
    settle(2, 0)
    for copy in gathers[1]:
        copy.wait_recv()
    for copy in gathers[0]:
        go(copy)
    settle(0, 1)
    small_step(3)
    settle(1, 1)
    settle(2, 1)
    for copy in gathers[0]:
        copy.wait_recv()
    e_swap = go(remote(eout, eoth, partner))
    settle(0, 2)
    settle(1, 2)
    settle(2, 2)

    give = pl.ds(pl.multiple_of((1 - core) * 8, 8), 8)
    keep = pl.ds(pl.multiple_of(core * 8, 8), 8)
    swap[0] = fin[0:9, give, :]
    f_swap = go(remote(swap.at[0], swap.at[1], partner))

    e_swap.wait_recv()

    @pl.when(core == 0)
    def _():
        o_proj[...] = eout[0:3].astype(F32).reshape(768, 256)
        o_one[...] = eoth[...].astype(F32).reshape(1024, 256)

    @pl.when(core == 1)
    def _():
        o_proj[...] = eoth[0:3].astype(F32).reshape(768, 256)
        o_one[...] = eout[...].astype(F32).reshape(1024, 256)

    f_swap.wait_recv()
    for p, a in ((0, 1), (1, 0), (2, 2)):
        for b in range(3):
            o_atr[core, a * 3 + b] = fin[3 * p + b, keep, :]
            o_atr[1 - core, a * 3 + b] = swap[1, 3 * p + b]

    for copies in (cross_copies, raw_copies):
        for t in range(3):
            @pl.when(t < k)
            def _(copy=copies[t]):
                copy.wait_send()

    @pl.when(core == 0)
    def _():
        j_copies[1].wait_send()

    @pl.when(core == 1)
    def _():
        for copy in (j_copies[0], j_copies[2], p_copies[0], p_copies[1]):
            copy.wait_send()

    for copy in sends:
        copy.wait_send()
    assert counter[0] <= COPIES


COPIES = 80


def on_device(features, labels, w_one, w_atrous, w_proj, w_class):
    total_pix = lax.axis_size("dp") * lax.axis_size("space") * OWN
    vmem = pl.BlockSpec(memory_space=pltpu.VMEM)
    hbm = pl.BlockSpec(memory_space=pl.ANY)
    scratch = [
        ((CHIP, 1024), BF),
        ((4, 256, CHIP), BF),
        ((3, 3, 1024, 256), BF),
        ((1024, 256), BF),
        ((3, BLK, 256), F32),
        ((CHIP, 256), F32),
        ((CHIP, 256), F32),
        ((3, BLK, 256), BF),
        ((3, BLK, 256), BF),
        ((3, CHIP, 256), BF),
        ((CHIP, 256), BF),
        ((3, 10 * BLK, 256), BF),
        ((CHIP, 256), BF),
        ((CHIP, 256), BF),
        ((3, BLK, 256), BF),
        ((3, 3, 4, 4, 4, 16, 256), BF),
        ((3, 10, 4, 4, 16, 256), BF),
        ((10, 4, 4, 16, 256), BF),
        ((3, 10, 4, 16, 256), BF),
        ((10, 4, 16, 256), BF),
        ((3, 10, 16, 256), BF),
        ((10, 16, 256), F32),
        ((2, 4, 4, 16, 256), BF),
        ((1, 4, 4, 4, 16, 256), BF),
        ((4, 4, 4, 16, 256), BF),
        ((4, 4, 4, 16, 256), BF),
        ((4, 4, 16, 256), F32),
        ((2, 9, 8, 256), F32),
    ]
    w_cls = jnp.pad(w_class.T, ((0, 13), (0, 0)))
    out = pl.pallas_call(
        lambda *refs: kernel(1.0 / math.sqrt(total_pix), *refs),
        out_shape=(
            jax.ShapeDtypeStruct((2, 9, 8, 256), F32),
            jax.ShapeDtypeStruct((1024, 256), F32),
            jax.ShapeDtypeStruct((768, 256), F32),
            jax.ShapeDtypeStruct((16, 256), F32),
        ),
        in_specs=[hbm, vmem, hbm, hbm, vmem, vmem],
        out_specs=(vmem, vmem, vmem, vmem),
        scratch_shapes=[pltpu.VMEM(shape, kind) for shape, kind in scratch]
        + [
            pltpu.SemaphoreType.DMA((5,)),
            pltpu.SemaphoreType.DMA((COPIES,)),
            pltpu.SemaphoreType.DMA((COPIES,)),
        ],
        compiler_params=pltpu.CompilerParams(
            collective_id=0, has_side_effects=True, vmem_limit_bytes=60 * 1024 * 1024
        ),
        name="aspp",
    )(
        features.reshape(OWN, 1024),
        labels.reshape(1, OWN),
        w_one,
        w_atrous,
        w_proj.reshape(3, 256, 256),
        w_cls,
    )
    return (
        out[0].reshape(2, 3, 3, 8, 256),
        out[1],
        out[2],
        out[3][:3].T,
        out[3][3, 0] / total_pix,
    )


def solution(mesh):
    return jax.shard_map(
        on_device,
        mesh=mesh,
        in_specs=(P("dp", "space", None, None), P("dp", "space", None), P(), P(), P(), P()),
        out_specs=(P(None, None, None, ("dp", "space"), None), P(), P(), P(), P()),
        check_vma=False,
    )
```

```python
import math

import jax
import jax.numpy as jnp
from jax import lax
from jax.experimental import pallas as pl
from jax.experimental.pallas import tpu as pltpu
from jax.sharding import PartitionSpec as P

MESH = pl.DeviceIdType.MESH
BF = jnp.bfloat16
F32 = jnp.float32
WIDTH = 56
BLK = 6 * WIDTH
OWN = 12 * WIDTH
CHIP = 24 * WIDTH
BASE = 3
ORDERS = ("xzy", "zyx", "yxz", "zxy")
AXES = "xzy"


def slope(pre):
    gate = jax.nn.sigmoid(pre)
    return gate * (1.0 + pre * (1.0 - gate))


def silu(pre):
    return pre * jax.nn.sigmoid(pre)


def mm(first, second):
    return jnp.dot(first, second, preferred_element_type=F32)


def mm_t(first, second):
    return lax.dot_general(first, second, (((1,), (1,)), ((), ())), preferred_element_type=F32)


def t_mm(first, second):
    return lax.dot_general(first, second, (((0,), (0,)), ((), ())), preferred_element_type=F32)


def kernel(
    loss_scale,
    feat, labels, w_one_h, w_atr_h, w_proj, w_cls,
    o_atr, eout, o_cls,
    xbuf, xt, wbuf, wone, tacc, pre, pre0, cs, cr, joined, dh, ext, db0, raw, hraw,
    s1, r1, s2, r2, s3, r3, fin, pbuf, e1, clbuf, swap, lab,
    lsem, ssem, rsem,
):
    dp = lax.axis_index("dp")
    sp = lax.axis_index("space")
    core, s = sp % 2, sp // 2
    cx, cz, cy = dp // 8, (dp // 2) % 4, (dp % 2) * 2 + s
    here = {"x": cx, "z": cz, "y": cy}

    def place(x, z, y, c):
        return (x * 8 + z * 2 + y // 2, (y % 2) * 2 + c)

    partner = place(cx, cz, cy, 1 - core)
    across = (dp, (1 - s) * 2 + core)

    def peer(axis, d):
        at = dict(here)
        at[axis] = (at[axis] + d) % 4
        return place(at["x"], at["z"], at["y"], core)

    rate = 12 + 6 * core
    k = 2 + core

    counter = [0]

    def remote(src, dst, to):
        i = counter[0]
        counter[0] += 1
        return pltpu.make_async_remote_copy(
            src_ref=src, dst_ref=dst, send_sem=ssem.at[i], recv_sem=rsem.at[i], device_id=to, device_id_type=MESH
        )

    sends = []

    def go(copy):
        copy.start()
        sends.append(copy)
        return copy

    own_rows = pl.ds(pl.multiple_of(core * OWN, 16), OWN)
    other_rows = pl.ds(pl.multiple_of((1 - core) * OWN, 16), OWN)
    x_local = pltpu.make_async_copy(feat, xbuf.at[own_rows], lsem.at[0])
    x_local.start()
    w_local = [pltpu.make_async_copy(w_atr_h.at[core, a], wbuf.at[a], lsem.at[1 + a]) for a in range(3)]
    for copy in w_local:
        copy.start()
    one_local = pltpu.make_async_copy(w_one_h, wone, lsem.at[4])
    one_local.start()

    barrier = pltpu.get_barrier_semaphore()
    greet = [partner] + [peer(axis, d) for axis in AXES for d in (1, 2, 3)]
    for other in greet:
        pl.semaphore_signal(barrier, inc=1, device_id=other, device_id_type=MESH)
    pl.semaphore_wait(barrier, len(greet))

    x_swap = go(remote(feat, xbuf.at[own_rows], partner))

    zero = jnp.zeros((BLK, 256), BF)
    for b in range(3):
        for m in (0, 1, 2, 7, 8, 9):
            ext[b, pl.ds(m * BLK, BLK), :] = zero

    column = lax.rem(lax.broadcasted_iota(jnp.int32, (BLK, 256), 0), WIDTH)

    def from_left(value):
        return jnp.where(column >= rate, pltpu.roll(value, rate, 0), 0.0)

    def from_right(value):
        return jnp.where(column < WIDTH - rate, pltpu.roll(value, BLK - rate, 0), 0.0)

    def block(m):
        return pl.ds(pl.multiple_of(m * BLK, 16), BLK)

    x_local.wait()
    x_swap.wait_recv()
    for copy in w_local:
        copy.wait()
    cross_tap = s * 2
    cross_copies = [remote(cs.at[t], cr.at[t], across) for t in range(3)]
    for t in range(3):
        @pl.when(t < k)
        def _(t=t):
            src = jnp.where(s == 0, 4 + t - k, t)
            rows = xbuf[block(src), :]
            parts = [mm(rows, wbuf[cross_tap, b]) for b in range(3)]
            cs[t] = (parts[1] + from_left(parts[0]) + from_right(parts[2])).astype(BF)
            cross_copies[t].start()

    @pl.loop(0, 4)
    def _(i):
        rows = xbuf[block(i), :]
        for b in range(3):
            tacc[b] = mm(rows, wbuf[1, b])
        for a in (0, 2):
            src = i + (a - 1) * k

            @pl.when((src >= 0) & (src < 4))
            def _(a=a, src=src):
                shifted = xbuf[block(src), :]
                for b in range(3):
                    tacc[b] += mm(shifted, wbuf[a, b])
        pre[block(i), :] = tacc[1] + from_left(tacc[0]) + from_right(tacc[2])

    one_local.wait()

    @pl.when(core == 1)
    def _():
        @pl.loop(0, 4)
        def _(i):
            value = mm(xbuf[block(i), :], wone[...])
            pre0[block(i), :] = value
            joined[0, block(i), :] = silu(value).astype(BF)

    for t in range(3):
        @pl.when(t < k)
        def _(t=t):
            cross_copies[t].wait_recv()
            into = block(jnp.where(s == 0, 4 - k + t, t))
            pre[into, :] += cr[t].astype(F32)

    @pl.loop(0, 4)
    def _(i):
        joined[1 + core, block(i), :] = silu(pre[block(i), :]).astype(BF)

    j_copies = [remote(joined.at[b, other_rows], joined.at[b, other_rows], partner) for b in range(3)]

    @pl.when(core == 0)
    def _():
        j_copies[1].start()

    @pl.when(core == 1)
    def _():
        j_copies[0].start()
        j_copies[2].start()

    for c in range(4):
        xt[c] = xbuf[:, c * 256 : (c + 1) * 256].T

    @pl.when(core == 0)
    def _():
        j_copies[0].wait_recv()
        j_copies[2].wait_recv()

    @pl.when(core == 1)
    def _():
        j_copies[1].wait_recv()

    pre_hidden = mm(joined[0, own_rows, :], w_proj[0])
    pre_hidden += mm(joined[1, own_rows, :], w_proj[1])
    pre_hidden += mm(joined[2, own_rows, :], w_proj[2])
    hidden = silu(pre_hidden).astype(BF)
    classes = jnp.concatenate([w_cls[...].astype(F32), jnp.zeros((13, 256), F32)]).astype(BF)
    for y in range(12):
        lab[:, y * WIDTH : (y + 1) * WIDTH] = labels[y]
    logits = mm_t(classes, hidden)
    row = lax.broadcasted_iota(jnp.int32, logits.shape, 0)
    valid = row < 3
    top = jnp.max(jnp.where(valid, logits, -jnp.inf), axis=0, keepdims=True)
    total = jnp.sum(jnp.where(valid, jnp.exp(logits - top), 0.0), axis=0, keepdims=True)
    lse = top + jnp.log(total)
    onehot = row == lab[...]
    loss = jnp.sum(lse - jnp.sum(jnp.where(onehot, logits, 0.0), axis=0, keepdims=True), axis=1, keepdims=True)
    probs = jnp.exp(logits - lse) - jnp.where(onehot, 1.0, 0.0)
    dlogits = jnp.where(valid, probs * loss_scale, 0.0).astype(BF)
    dhidden = t_mm(dlogits, classes) * slope(pre_hidden)
    dh[own_rows, :] = dhidden.astype(BF)
    dh_copy = go(remote(dh.at[own_rows], dh.at[own_rows], partner))

    small = mm(dlogits, hidden)
    srow = lax.broadcasted_iota(jnp.int32, small.shape, 0)
    cl_copies = []
    for n, axis in enumerate(AXES):
        cl_copies.append([remote(clbuf.at[n, here[axis]], clbuf.at[n, here[axis]], peer(axis, d)) for d in (1, 2, 3)])
    cl_copies.append([remote(clbuf.at[3, core], clbuf.at[3, core], partner)])
    clbuf[0, here["x"]] = jnp.where(srow == 3, loss, small)
    for copy in cl_copies[0]:
        go(copy)

    def small_step(n):
        for copy in cl_copies[n]:
            copy.wait_recv()
        value = clbuf[n, 0] + clbuf[n, 1]
        if n < 3:
            value = value + clbuf[n, 2] + clbuf[n, 3]
            clbuf[n + 1, core if n == 2 else here[AXES[n + 1]]] = value
            for copy in cl_copies[n + 1]:
                go(copy)
        else:
            o_cls[...] = value

    dh_copy.wait_recv()
    branch_w = w_proj[1 + core]
    raw_copies = [remote(raw.at[block(jnp.where(s == 0, 4 - k + t, t))], hraw.at[t], across) for t in range(3)]

    @pl.loop(0, 4)
    def _(i):
        value = mm_t(dh[block(i), :], branch_w) * slope(pre[block(i), :])
        raw[block(i), :] = value.astype(BF)
        to = block(BASE + i)
        rounded = value.astype(BF).astype(F32)
        ext[0, to, :] = from_right(rounded).astype(BF)
        ext[1, to, :] = rounded.astype(BF)
        ext[2, to, :] = from_left(rounded).astype(BF)

    for t in range(3):
        @pl.when(t < k)
        def _(t=t):
            raw_copies[t].start()

    low, high = pl.ds(0, 2), pl.ds(2, 2)

    def ring(p, phase, buf, landing):
        axis = ORDERS[p][phase]
        left = [a for a in AXES if a in ORDERS[p][phase:]]
        spot = left.index(axis)
        c = here[axis]

        def chunk(at, half=None):
            index = [slice(None)] * (1 + len(left))
            index[1 + spot] = (at + 4) % 4
            if half is not None:
                index[2 if spot == 0 else 1] = half
            return buf.at[tuple(index)]

        mine = chunk(c)
        if phase == 2:
            return mine, [remote(chunk(c + d), landing.at[d - 1], peer(axis, d)) for d in (1, 2, 3)]
        up, down = peer(axis, 1), peer(axis, 3)

        def land(slot, half):
            return landing.at[slot, :, half]

        return mine, [
            remote(chunk(c + 2, low), land(2, low), up),
            remote(chunk(c + 2, high), land(2, high), down),
            remote(chunk(c + 1, high), land(0, high), up),
            remote(chunk(c - 1, low), land(1, low), down),
            remote(chunk(c + 1, low), land(0, low), up),
            remote(chunk(c - 1, high), land(1, high), down),
        ], [(chunk(c + 1, low), land(2, low)), (chunk(c - 1, high), land(2, high))]

    plans = []
    for p in range(4):
        taps = 3 if p < 3 else 1
        lead = pl.ds(3 * p, taps)
        bufs = (s1.at[p] if p < 3 else e1, s2.at[lead], s3.at[lead])
        lands = (r1.at[:, lead], r2.at[:, lead], r3.at[:, lead])
        plans.append(([ring(p, phase, bufs[phase], lands[phase]) for phase in range(3)], bufs, lands, taps, 3 * p))

    def firsts(p, phase):
        copies = plans[p][0][phase][1]
        return copies if phase == 2 else copies[:4]

    def send(p, phase):
        for copy in firsts(p, phase):
            go(copy)

    def each_tap(taps, body):
        if taps == 1:
            body(0)
        else:
            pl.loop(0, taps)(body)

    def forward(p, phase):
        (_, copies, sums), taps = plans[p][0][phase], plans[p][3]
        for n in range(2):
            copies[n].wait_recv()
            out, got = sums[n]

            def one(t):
                out[t] = (out[t].astype(F32) + got[t].astype(F32)).astype(BF)

            each_tap(taps, one)
            go(copies[4 + n])

    def settle(p, phase):
        plan, bufs, lands, taps, at = plans[p]
        mine, copies = plan[phase][:2]
        for copy in copies if phase == 2 else copies[2:]:
            copy.wait_recv()

        def one(t):
            value = mine[t].astype(F32)
            for n in range(3 if phase == 2 else 2):
                value = value + lands[phase][n, t].astype(F32)
            if phase < 2:
                bufs[phase + 1][t] = value.astype(bufs[phase + 1].dtype)
            else:
                fin[at + t] = value

        each_tap(taps, one)
        if phase < 2:
            send(p, phase + 1)

    def proj_grad(b):
        return t_mm(joined[b], dh[...]).astype(BF).reshape(4, 4, 16, 256)

    p_copies = [remote(pbuf.at[n], e1.at[0, 2 * n], partner) for n in range(2)]

    @pl.when(core == 1)
    def _():
        for n in range(2):
            pbuf[n] = proj_grad(2 * n)
            p_copies[n].start()

        @pl.loop(0, 4)
        def _(i):
            value = mm_t(dh[block(i), :], w_proj[0]) * slope(pre0[block(i), :])
            db0[block(i), :] = value.astype(BF)

        @pl.loop(0, 4)
        def _(c):
            e1[0, c] = mm(xt[c], db0[...]).astype(BF).reshape(4, 4, 16, 256)

    @pl.when(core == 0)
    def _():
        e1[0, 1] = proj_grad(1)
        e1[0, 3] = jnp.zeros((4, 4, 16, 256), BF)
        for n in range(2):
            p_copies[n].wait_recv()

    send(3, 0)

    def part(a):
        p = jnp.where(a == 1, 0, 1 + a // 2)
        start = pl.ds(pl.multiple_of((BASE - (a - 1) * k) * BLK, 16), CHIP)

        @pl.loop(0, 4)
        def _(c):
            for b in range(3):
                s1[p, b, c] = mm(xt[c], ext[b, start, :]).astype(BF).reshape(4, 4, 16, 256)

    def outer_send(toward):
        for p in (1, 2):
            @pl.when((s == p - 1) == toward)
            def _(p=p):
                for copy in firsts(p, 0):
                    copy.start()

    part(1)
    send(0, 0)
    small_step(0)
    forward(3, 0)
    part(2 - cross_tap)
    outer_send(False)
    settle(3, 0)

    for t in range(3):
        @pl.when(t < k)
        def _(t=t):
            raw_copies[t].wait_recv()
            to = block(jnp.where(s == 0, BASE + 4 + t, BASE - k + t))
            value = hraw[t].astype(F32)
            ext[0, to, :] = from_right(value).astype(BF)
            ext[1, to, :] = hraw[t]
            ext[2, to, :] = from_left(value).astype(BF)

    part(cross_tap)
    outer_send(True)
    for p in (1, 2):
        sends.extend(firsts(p, 0))
    forward(0, 0)
    forward(3, 1)
    forward(1, 0)
    forward(2, 0)
    settle(3, 1)
    settle(0, 0)
    small_step(1)
    settle(3, 2)

    eout[core, cx, cz, cy] = fin[9].astype(BF)
    everything = slice(None)

    def around(axis, at, half):
        up, down = peer(axis, 1), peer(axis, 3)

        def view(c, n):
            index = tuple((c + 4) % 4 if a == axis else v for a, v in zip(AXES, half[n] if n is not None else at))
            return eout.at[(core,) + index]

        c = here[axis]
        first = [remote(view(c, None), view(c, None), to) for to in (up, down)]
        return first, [remote(view(c - 1, 0), view(c - 1, 0), up), remote(view(c + 1, 1), view(c + 1, 1), down)]

    mine = eout.at[core, cx, cz, cy]
    g_z = [remote(mine, mine, peer("z", d)) for d in (1, 2, 3)]
    g_y = around("y", (cx, everything, None), ((cx, low, None), (cx, high, None)))
    g_x = around("x", (None, everything, everything), ((None, low, everything), (None, high, everything)))

    def pass_on(gather):
        for n in range(2):
            gather[0][n].wait_recv()
            go(gather[1][n])

    for copy in g_z:
        go(copy)
    settle(1, 0)
    settle(2, 0)
    forward(0, 1)
    for copy in g_z:
        copy.wait_recv()
    for copy in g_y[0]:
        go(copy)
    forward(1, 1)
    forward(2, 1)
    pass_on(g_y)
    settle(0, 1)
    small_step(2)
    for copy in g_y[1]:
        copy.wait_recv()
    for copy in g_x[0]:
        go(copy)
    settle(1, 1)
    settle(2, 1)
    pass_on(g_x)
    small_step(3)
    for p in range(3):
        settle(p, 2)

    give = pl.ds(pl.multiple_of((1 - core) * 8, 8), 8)
    keep = pl.ds(pl.multiple_of(core * 8, 8), 8)
    swap[0] = fin[0:9, give, :]
    f_swap = go(remote(swap.at[0], swap.at[1], partner))
    for copy in g_x[1]:
        copy.wait_recv()
    e_swap = go(remote(eout.at[core], eout.at[core], partner))

    e_swap.wait_recv()
    f_swap.wait_recv()
    for p, a in ((0, 1), (1, 0), (2, 2)):
        for b in range(3):
            o_atr[core, a * 3 + b] = fin[3 * p + b, keep, :]
            o_atr[1 - core, a * 3 + b] = swap[1, 3 * p + b]

    for copies in (cross_copies, raw_copies):
        for t in range(3):
            @pl.when(t < k)
            def _(copy=copies[t]):
                copy.wait_send()

    @pl.when(core == 0)
    def _():
        j_copies[1].wait_send()

    @pl.when(core == 1)
    def _():
        for copy in (j_copies[0], j_copies[2], p_copies[0], p_copies[1]):
            copy.wait_send()

    for copy in sends:
        copy.wait_send()
    assert counter[0] <= COPIES


COPIES = 120


def widen(scale, shares, small, tiny, o_atr, o_one, o_proj, o_cls, o_loss):
    o_atr[...] = shares[...]
    o_proj[...] = small[0, 0:768].astype(F32)
    o_one[...] = small[1].astype(F32)
    o_cls[...] = tiny[0:3]
    o_loss[...] = tiny[3:4, 0:1] * scale


def on_device(features, labels, w_one, w_atrous, w_proj, w_class):
    total_pix = lax.axis_size("dp") * lax.axis_size("space") * OWN
    vmem = pl.BlockSpec(memory_space=pltpu.VMEM)
    hbm = pl.BlockSpec(memory_space=pl.ANY)
    scratch = [
        ((CHIP, 1024), BF),
        ((4, 256, CHIP), BF),
        ((3, 3, 1024, 256), BF),
        ((1024, 256), BF),
        ((3, BLK, 256), F32),
        ((CHIP, 256), F32),
        ((CHIP, 256), F32),
        ((3, BLK, 256), BF),
        ((3, BLK, 256), BF),
        ((3, CHIP, 256), BF),
        ((CHIP, 256), BF),
        ((3, 10 * BLK, 256), BF),
        ((CHIP, 256), BF),
        ((CHIP, 256), BF),
        ((3, BLK, 256), BF),
        ((3, 3, 4, 4, 4, 16, 256), BF),
        ((3, 10, 4, 4, 16, 256), BF),
        ((10, 4, 4, 16, 256), BF),
        ((3, 10, 4, 16, 256), BF),
        ((10, 4, 16, 256), F32),
        ((3, 10, 16, 256), F32),
        ((10, 16, 256), F32),
        ((2, 4, 4, 16, 256), BF),
        ((1, 4, 4, 4, 16, 256), BF),
        ((4, 4, 16, 256), F32),
        ((2, 9, 8, 256), F32),
        ((1, OWN), jnp.int32),
    ]
    shares, small, tiny = pl.pallas_call(
        lambda *refs: kernel(1.0 / math.sqrt(total_pix), *refs),
        out_shape=(
            jax.ShapeDtypeStruct((2, 9, 8, 256), F32),
            jax.ShapeDtypeStruct((2, 4, 4, 4, 16, 256), BF),
            jax.ShapeDtypeStruct((16, 256), F32),
        ),
        in_specs=[hbm, vmem, hbm, hbm, vmem, vmem],
        out_specs=(vmem, vmem, vmem),
        scratch_shapes=[pltpu.VMEM(shape, kind) for shape, kind in scratch]
        + [
            pltpu.SemaphoreType.DMA((5,)),
            pltpu.SemaphoreType.DMA((COPIES,)),
            pltpu.SemaphoreType.DMA((COPIES,)),
        ],
        compiler_params=pltpu.CompilerParams(
            collective_id=0, has_side_effects=True, vmem_limit_bytes=60 * 1024 * 1024
        ),
        name="aspp",
    )(
        features.reshape(OWN, 1024),
        labels.transpose(1, 0, 2),
        w_one,
        w_atrous,
        w_proj.reshape(3, 256, 256),
        w_class.T,
    )
    grad_atrous, grad_one, grad_proj, grad_class, loss = pl.pallas_call(
        lambda *refs: widen(1.0 / total_pix, *refs),
        out_shape=(
            jax.ShapeDtypeStruct((2, 9, 8, 256), F32),
            jax.ShapeDtypeStruct((1024, 256), F32),
            jax.ShapeDtypeStruct((768, 256), F32),
            jax.ShapeDtypeStruct((3, 256), F32),
            jax.ShapeDtypeStruct((1, 1), F32),
        ),
        in_specs=[vmem] * 3,
        out_specs=(vmem,) * 5,
        name="widen",
    )(shares, small.reshape(2, 1024, 256), tiny)
    return (grad_atrous.reshape(2, 3, 3, 8, 256), grad_one, grad_proj, grad_class.T, loss.reshape(()))


def solution(mesh):
    return jax.shard_map(
        on_device,
        mesh=mesh,
        in_specs=(P("dp", "space", None, None), P("dp", "space", None), P(), P(), P(), P()),
        out_specs=(P(None, None, None, ("dp", "space"), None), P(), P(), P(), P()),
        check_vma=False,
    )
```

```python
import math

import jax
import jax.numpy as jnp
from jax import lax
from jax.experimental import pallas as pl
from jax.experimental.pallas import tpu as pltpu
from jax.sharding import PartitionSpec as P

MESH = pl.DeviceIdType.MESH
BF = jnp.bfloat16
F32 = jnp.float32
WIDTH = 56
BLK = 6 * WIDTH
OWN = 12 * WIDTH
CHIP = 24 * WIDTH
BASE = 3
MIDDLE = ("xzy", "zxy", "zyx")
OUTER = ("xzy", "zxy", "yxz")
SMALL = "xzy"
AXES = "xzy"


def slope(pre):
    gate = jax.nn.sigmoid(pre)
    return gate * (1.0 + pre * (1.0 - gate))


def silu(pre):
    return pre * jax.nn.sigmoid(pre)


def mm(first, second):
    return jnp.dot(first, second, preferred_element_type=F32)


def mm_t(first, second):
    return lax.dot_general(first, second, (((1,), (1,)), ((), ())), preferred_element_type=F32)


def t_mm(first, second):
    return lax.dot_general(first, second, (((0,), (0,)), ((), ())), preferred_element_type=F32)


def kernel(
    loss_scale,
    feat, labels, w_one_h, w_atr_h, w_proj, w_cls,
    o_atr, eout, o_cls,
    xbuf, wbuf, wone, tacc, pre, pre0, cs, cr, joined, dh, ext, db0, raw, hraw,
    s1, r1, s2, r2, s3, r3, fin, pbuf, clbuf, swap, lab,
    lsem, ssem, rsem,
):
    dp = lax.axis_index("dp")
    sp = lax.axis_index("space")
    core, s = sp % 2, sp // 2
    cx, cz, cy = dp // 8, (dp // 2) % 4, (dp % 2) * 2 + s
    here = {"x": cx, "z": cz, "y": cy}

    def place(x, z, y, c):
        return (x * 8 + z * 2 + y // 2, (y % 2) * 2 + c)

    partner = place(cx, cz, cy, 1 - core)
    across = (dp, (1 - s) * 2 + core)

    def peer(axis, d):
        at = dict(here)
        at[axis] = (at[axis] + d) % 4
        return place(at["x"], at["z"], at["y"], core)

    rate = 12 + 6 * core
    k = 2 + core

    counter = [UNITS * 12 + 6]

    def remote(src, dst, to, i=None):
        if i is None:
            i = counter[0]
            counter[0] += 1
        return pltpu.make_async_remote_copy(
            src_ref=src, dst_ref=dst, send_sem=ssem.at[i], recv_sem=rsem.at[i], device_id=to, device_id_type=MESH
        )

    sends = []

    def go(copy):
        copy.start()
        sends.append(copy)
        return copy

    own_rows = pl.ds(pl.multiple_of(core * OWN, 16), OWN)
    other_rows = pl.ds(pl.multiple_of((1 - core) * OWN, 16), OWN)
    x_local = pltpu.make_async_copy(feat, xbuf.at[own_rows], lsem.at[0])
    x_local.start()
    w_local = [pltpu.make_async_copy(w_atr_h.at[core, a], wbuf.at[a], lsem.at[1 + a]) for a in range(3)]
    for a in (1, 0, 2):
        w_local[a].start()
    one_local = pltpu.make_async_copy(w_one_h, wone, lsem.at[4])
    one_local.start()

    barrier = pltpu.get_barrier_semaphore()
    greet = [partner] + [peer(axis, d) for axis in AXES for d in (1, 2, 3)]
    for other in greet:
        pl.semaphore_signal(barrier, inc=1, device_id=other, device_id_type=MESH)

    zero = jnp.zeros((BLK, 256), BF)
    for b in range(3):
        for m in (0, 1, 2, 7, 8, 9):
            ext[b, pl.ds(m * BLK, BLK), :] = zero
    tacc[...] = jnp.zeros_like(tacc)

    column = lax.rem(lax.broadcasted_iota(jnp.int32, (BLK, 256), 0), WIDTH)

    def from_left(value):
        return jnp.where(column >= rate, pltpu.roll(value, rate, 0), 0.0)

    def from_right(value):
        return jnp.where(column < WIDTH - rate, pltpu.roll(value, BLK - rate, 0), 0.0)

    def block(m):
        return pl.ds(pl.multiple_of(m * BLK, 16), BLK)

    def middle(m):
        rows = xbuf[block(m), :]
        for b in range(3):
            tacc[m, b] += mm(rows, wbuf[1, b])

    def outer(m):
        for a in (0, 2):
            to = m - (a - 1) * k

            @pl.when((to >= 0) & (to < 4))
            def _(a=a, to=to):
                rows = xbuf[block(m), :]
                for b in range(3):
                    tacc[to, b] += mm(rows, wbuf[a, b])

    def cross_copy(t):
        return remote(cs.at[t], cr.at[t], across, UNITS * 12 + t)

    cross_tap = s * 2

    def cross(m):
        @pl.when(jnp.where(s == 0, m + k >= 4, m < k))
        def _():
            t = jnp.where(s == 0, m + k - 4, m)
            rows = xbuf[block(m), :]
            parts = [mm(rows, wbuf[cross_tap, b]) for b in range(3)]
            cs[t] = (parts[1] + from_left(parts[0]) + from_right(parts[2])).astype(BF)
            cross_copy(t).start()

    mine, theirs = 2 * core, 2 * (1 - core)
    x_local.wait()
    w_local[1].wait()
    pl.loop(0, 2)(lambda q: middle(mine + q))
    pl.semaphore_wait(barrier, len(greet))
    x_swap = go(remote(feat, xbuf.at[own_rows], partner))
    w_local[0].wait()
    w_local[2].wait()
    pl.loop(0, 2)(lambda q: cross(mine + q))
    pl.loop(0, 2)(lambda q: outer(mine + q))
    x_swap.wait_recv()
    pl.loop(0, 2)(lambda q: cross(theirs + q))

    @pl.loop(0, 2)
    def _(q):
        middle(theirs + q)
        outer(theirs + q)

    @pl.loop(0, 4)
    def _(i):
        pre[block(i), :] = tacc[i, 1] + from_left(tacc[i, 0]) + from_right(tacc[i, 2])

    one_local.wait()

    @pl.when(core == 1)
    def _():
        @pl.loop(0, 4)
        def _(i):
            value = mm(xbuf[block(i), :], wone[...])
            pre0[block(i), :] = value
            joined[0, block(i), :] = silu(value).astype(BF)

    for t in range(3):
        @pl.when(t < k)
        def _(t=t):
            cross_copy(t).wait_recv()
            into = block(jnp.where(s == 0, 4 - k + t, t))
            pre[into, :] += cr[t].astype(F32)

    @pl.loop(0, 4)
    def _(i):
        joined[1 + core, block(i), :] = silu(pre[block(i), :]).astype(BF)

    j_copies = [remote(joined.at[b, other_rows], joined.at[b, other_rows], partner) for b in range(3)]

    @pl.when(core == 0)
    def _():
        j_copies[1].start()

    @pl.when(core == 1)
    def _():
        j_copies[0].start()
        j_copies[2].start()

    @pl.when(core == 0)
    def _():
        j_copies[0].wait_recv()
        j_copies[2].wait_recv()

    @pl.when(core == 1)
    def _():
        j_copies[1].wait_recv()

    pre_hidden = mm(joined[0, own_rows, :], w_proj[0])
    pre_hidden += mm(joined[1, own_rows, :], w_proj[1])
    pre_hidden += mm(joined[2, own_rows, :], w_proj[2])
    hidden = silu(pre_hidden).astype(BF)
    classes = jnp.concatenate([w_cls[...].astype(F32), jnp.zeros((13, 256), F32)]).astype(BF)
    for y in range(12):
        lab[:, y * WIDTH : (y + 1) * WIDTH] = labels[y]
    logits = mm_t(classes, hidden)
    row = lax.broadcasted_iota(jnp.int32, logits.shape, 0)
    valid = row < 3
    top = jnp.max(jnp.where(valid, logits, -jnp.inf), axis=0, keepdims=True)
    total = jnp.sum(jnp.where(valid, jnp.exp(logits - top), 0.0), axis=0, keepdims=True)
    lse = top + jnp.log(total)
    onehot = row == lab[...]
    loss = jnp.sum(lse - jnp.sum(jnp.where(onehot, logits, 0.0), axis=0, keepdims=True), axis=1, keepdims=True)
    probs = jnp.exp(logits - lse) - jnp.where(onehot, 1.0, 0.0)
    dlogits = jnp.where(valid, probs * loss_scale, 0.0).astype(BF)
    dhidden = t_mm(dlogits, classes) * slope(pre_hidden)
    dh[own_rows, :] = dhidden.astype(BF)
    dh_copy = go(remote(dh.at[own_rows], dh.at[own_rows], partner))

    small = mm(dlogits, hidden)
    srow = lax.broadcasted_iota(jnp.int32, small.shape, 0)
    cl_copies = []
    for n, axis in enumerate(AXES):
        cl_copies.append([remote(clbuf.at[n, here[axis]], clbuf.at[n, here[axis]], peer(axis, d)) for d in (1, 2, 3)])
    cl_copies.append([remote(clbuf.at[3, core], clbuf.at[3, core], partner)])
    clbuf[0, here["x"]] = jnp.where(srow == 3, loss, small)
    for copy in cl_copies[0]:
        go(copy)

    def small_step(n):
        for copy in cl_copies[n]:
            copy.wait_recv()
        value = clbuf[n, 0] + clbuf[n, 1]
        if n < 3:
            value = value + clbuf[n, 2] + clbuf[n, 3]
            clbuf[n + 1, core if n == 2 else here[AXES[n + 1]]] = value
            for copy in cl_copies[n + 1]:
                go(copy)
        else:
            o_cls[...] = value

    branch_w = w_proj[1 + core]

    def raw_copy(t):
        return remote(raw.at[block(jnp.where(s == 0, 4 - k + t, t))], hraw.at[t], across, UNITS * 12 + 3 + t)

    def branch_grad(i):
        value = mm_t(dh[block(i), :], branch_w) * slope(pre[block(i), :])
        raw[block(i), :] = value.astype(BF)

        @pl.when(jnp.where(s == 0, i >= 4 - k, i < k))
        def _():
            raw_copy(jnp.where(s == 0, i - (4 - k), i)).start()

        to = block(BASE + i)
        rounded = value.astype(BF).astype(F32)
        ext[0, to, :] = from_right(rounded).astype(BF)
        ext[1, to, :] = rounded.astype(BF)
        ext[2, to, :] = from_left(rounded).astype(BF)

    pl.loop(0, 2)(lambda q: branch_grad(mine + q))
    dh_copy.wait_recv()
    pl.loop(0, 2)(lambda q: branch_grad(theirs + q))

    low, high = pl.ds(0, 2), pl.ds(2, 2)

    def plan(u, order, ring):
        out = []
        for phase, (buf, landing) in enumerate(((s1, r1), (s2, r2), (s3, r3))):
            axis = order[phase]
            left = [a for a in AXES if a in order[phase:]]
            spot = left.index(axis)
            c = here[axis]
            base = u * 12 + (0, 6, 9)[phase]

            def chunk(at, half=None):
                index = [u] + [slice(None)] * len(left)
                index[1 + spot] = (at + 4) % 4
                if half is not None:
                    index[2 if spot == 0 else 1] = half
                return buf.at[tuple(index)]

            def land(slot, half=None):
                return landing.at[u, slot] if half is None else landing.at[u, slot, half]

            if phase or not ring:
                copies = [remote(chunk(c + d), land(d - 1), peer(axis, d), base + d - 1) for d in (2, 1, 3)]
                out.append((chunk(c), [land(n) for n in range(3)], copies, (), (), ()))
                continue
            up, down = peer(axis, 1), peer(axis, 3)
            way = [
                remote(chunk(c + 2, low), land(2, low), up, base),
                remote(chunk(c + 2, high), land(2, high), down, base + 1),
            ]
            copies = [
                remote(chunk(c + 1, high), land(0, high), up, base + 2),
                remote(chunk(c - 1, low), land(1, low), down, base + 3),
            ]
            later = [
                remote(chunk(c + 1, low), land(0, low), up, base + 4),
                remote(chunk(c - 1, high), land(1, high), down, base + 5),
            ]
            sums = [(chunk(c + 1, low), land(2, low)), (chunk(c - 1, high), land(2, high))]
            out.append((chunk(c), [land(0), land(1)], copies, way, later, sums))
        return u, out

    def send(unit, phase):
        _, _, copies, way, _, _ = unit[1][phase]
        for copy in list(way) + copies:
            go(copy)

    def forward(unit):
        _, _, _, way, later, sums = unit[1][0]
        for n in range(2):
            way[n].wait_recv()
            out, got = sums[n]
            out[...] = (out[...].astype(F32) + got[...].astype(F32)).astype(BF)
            go(later[n])

    def settle(unit, phase):
        u, phases = unit
        own, lands, copies, _, later, _ = phases[phase]
        for copy in copies + list(later):
            copy.wait_recv()
        value = own[...].astype(F32)
        for got in lands:
            value = value + got[...].astype(F32)
        if phase < 2:
            into = (s2, s3)[phase]
            into[u] = value.astype(into.dtype)
            send(unit, phase + 1)
        else:
            fin[u] = value

    mids = [plan(b, MIDDLE[b], True) for b in range(3)]
    aways = [plan(3 + 3 * (1 - s) + b, OUTER[b], True) for b in range(3)]
    towards = [plan(3 + 3 * s + b, OUTER[b], True) for b in range(3)]
    smalls = plan(9, SMALL, False)

    def proj_grad(b):
        return t_mm(joined[b], dh[...]).astype(BF).reshape(4, 4, 16, 256)

    p_copies = [remote(pbuf.at[n], s1.at[9, 2 * n], partner) for n in range(2)]

    def tap(u, rows, grad):
        for c in range(4):
            value = t_mm(xbuf[rows, c * 256 : (c + 1) * 256], grad)
            s1[u, c] = value.astype(BF).reshape(4, 4, 16, 256)

    everyone = pl.ds(0, CHIP)

    @pl.when(core == 1)
    def _():
        for n in range(2):
            pbuf[n] = proj_grad(2 * n)
            p_copies[n].start()

        @pl.loop(0, 4)
        def _(i):
            value = mm_t(dh[block(i), :], w_proj[0]) * slope(pre0[block(i), :])
            db0[block(i), :] = value.astype(BF)

        tap(9, everyone, db0[...])

    @pl.when(core == 0)
    def _():
        s1[9, 1] = proj_grad(1)
        s1[9, 3] = jnp.zeros((4, 4, 16, 256), BF)
        for n in range(2):
            p_copies[n].wait_recv()

    send(smalls, 0)

    def rows_from(m, count):
        return pl.ds(pl.multiple_of(m * BLK, 16), count * BLK)

    for b in range(3):
        tap(b, everyone, ext[b, rows_from(BASE, 4), :])
        send(mids[b], 0)
    small_step(0)
    for b in range(3):
        for n in range(2):
            @pl.when(core == n)
            def _(n=n, b=b):
                x_at = jnp.where(s == 0, 2 + n, 0)
                g_at = BASE + jnp.where(s == 0, 0, 2 + n)
                tap(aways[b][0], rows_from(x_at, 2 - n), ext[b, rows_from(g_at, 2 - n), :])
        send(aways[b], 0)

    settle(smalls, 0)
    for b in range(3):
        forward(mids[b])

    for t in range(3):
        @pl.when(t < k)
        def _(t=t):
            raw_copy(t).wait_recv()
            to = block(jnp.where(s == 0, BASE + 4 + t, BASE - k + t))
            value = hraw[t].astype(F32)
            ext[0, to, :] = from_right(value).astype(BF)
            ext[1, to, :] = hraw[t]
            ext[2, to, :] = from_left(value).astype(BF)

    for b in range(3):
        tap(towards[b][0], everyone, ext[b, rows_from(BASE - (cross_tap - 1) * k, 4), :])
        send(towards[b], 0)

    settle(smalls, 1)
    for b in range(2):
        forward(aways[b])
    for b in range(3):
        settle(mids[b], 0)
    small_step(1)
    settle(smalls, 2)

    eout[core, cx, cz, cy] = fin[9].astype(BF)
    everything = slice(None)

    def gather(axis, at):
        view = eout.at[(core,) + at]
        return [remote(view, view, peer(axis, d)) for d in (2, 1, 3)]

    gathers = [gather("z", (cx, cz, cy)), gather("y", (cx, everything, cy)), gather("x", (cx, everything, everything))]

    def gather_next(n):
        for copy in gathers[n - 1] if n else ():
            copy.wait_recv()
        for copy in gathers[n] if n < 3 else ():
            go(copy)

    gather_next(0)
    for b in range(2):
        settle(aways[b], 0)
    for b in range(2):
        forward(towards[b])
    for b in range(3):
        settle(mids[b], 1)
    gather_next(1)
    small_step(2)
    forward(aways[2])
    forward(towards[2])
    for b in range(2):
        settle(aways[b], 1)
    for b in range(2):
        settle(towards[b], 0)
    gather_next(2)
    for b in range(3):
        settle(mids[b], 2)
    settle(aways[2], 0)
    settle(towards[2], 0)
    for b in range(2):
        settle(towards[b], 1)
    for b in range(2):
        settle(aways[b], 2)
    gather_next(3)
    e_swap = go(remote(eout.at[core], eout.at[core], partner))
    small_step(3)
    settle(aways[2], 1)
    settle(towards[2], 1)
    for b in range(2):
        settle(towards[b], 2)
    settle(aways[2], 2)
    settle(towards[2], 2)

    give = pl.ds(pl.multiple_of((1 - core) * 8, 8), 8)
    keep = pl.ds(pl.multiple_of(core * 8, 8), 8)
    swap[0] = fin[0:9, give, :]
    f_swap = go(remote(swap.at[0], swap.at[1], partner))

    e_swap.wait_recv()
    f_swap.wait_recv()
    for u in range(9):
        at = u + 3 if u < 3 else u - 3 if u < 6 else u
        o_atr[core, at] = fin[u, keep, :]
        o_atr[1 - core, at] = swap[1, u]

    for t in range(3):
        @pl.when(t < k)
        def _(t=t):
            cross_copy(t).wait_send()
            raw_copy(t).wait_send()

    @pl.when(core == 0)
    def _():
        j_copies[1].wait_send()

    @pl.when(core == 1)
    def _():
        for copy in (j_copies[0], j_copies[2], p_copies[0], p_copies[1]):
            copy.wait_send()

    for copy in sends:
        copy.wait_send()
    assert counter[0] <= COPIES


COPIES = 180
UNITS = 10


def widen(scale, shares, small, tiny, o_atr, o_one, o_proj, o_cls, o_loss):
    o_atr[...] = shares[...]
    o_proj[...] = small[0, 0:768].astype(F32)
    o_one[...] = small[1].astype(F32)
    o_cls[...] = tiny[0:3]
    o_loss[...] = tiny[3:4, 0:1] * scale


def on_device(features, labels, w_one, w_atrous, w_proj, w_class):
    total_pix = lax.axis_size("dp") * lax.axis_size("space") * OWN
    vmem = pl.BlockSpec(memory_space=pltpu.VMEM)
    hbm = pl.BlockSpec(memory_space=pl.ANY)
    scratch = [
        ((CHIP, 1024), BF),
        ((3, 3, 1024, 256), BF),
        ((1024, 256), BF),
        ((4, 3, BLK, 256), F32),
        ((CHIP, 256), F32),
        ((CHIP, 256), F32),
        ((3, BLK, 256), BF),
        ((3, BLK, 256), BF),
        ((3, CHIP, 256), BF),
        ((CHIP, 256), BF),
        ((3, 10 * BLK, 256), BF),
        ((CHIP, 256), BF),
        ((CHIP, 256), BF),
        ((3, BLK, 256), BF),
        ((UNITS, 4, 4, 4, 16, 256), BF),
        ((UNITS, 3, 4, 4, 16, 256), BF),
        ((UNITS, 4, 4, 16, 256), BF),
        ((UNITS, 3, 4, 16, 256), BF),
        ((UNITS, 4, 16, 256), F32),
        ((UNITS, 3, 16, 256), F32),
        ((UNITS, 16, 256), F32),
        ((2, 4, 4, 16, 256), BF),
        ((4, 4, 16, 256), F32),
        ((2, 9, 8, 256), F32),
        ((1, OWN), jnp.int32),
    ]
    shares, small, tiny = pl.pallas_call(
        lambda *refs: kernel(1.0 / math.sqrt(total_pix), *refs),
        out_shape=(
            jax.ShapeDtypeStruct((2, 9, 8, 256), F32),
            jax.ShapeDtypeStruct((2, 4, 4, 4, 16, 256), BF),
            jax.ShapeDtypeStruct((16, 256), F32),
        ),
        in_specs=[hbm, vmem, hbm, hbm, vmem, vmem],
        out_specs=(vmem, vmem, vmem),
        scratch_shapes=[pltpu.VMEM(shape, kind) for shape, kind in scratch]
        + [
            pltpu.SemaphoreType.DMA((5,)),
            pltpu.SemaphoreType.DMA((COPIES,)),
            pltpu.SemaphoreType.DMA((COPIES,)),
        ],
        compiler_params=pltpu.CompilerParams(
            collective_id=0, has_side_effects=True, vmem_limit_bytes=60 * 1024 * 1024
        ),
        name="aspp",
    )(
        features.reshape(OWN, 1024),
        labels.transpose(1, 0, 2),
        w_one,
        w_atrous,
        w_proj.reshape(3, 256, 256),
        w_class.T,
    )
    grad_atrous, grad_one, grad_proj, grad_class, loss = pl.pallas_call(
        lambda *refs: widen(1.0 / total_pix, *refs),
        out_shape=(
            jax.ShapeDtypeStruct((2, 9, 8, 256), F32),
            jax.ShapeDtypeStruct((1024, 256), F32),
            jax.ShapeDtypeStruct((768, 256), F32),
            jax.ShapeDtypeStruct((3, 256), F32),
            jax.ShapeDtypeStruct((1, 1), F32),
        ),
        in_specs=[vmem] * 3,
        out_specs=(vmem,) * 5,
        name="widen",
    )(shares, small.reshape(2, 1024, 256), tiny)
    return (grad_atrous.reshape(2, 3, 3, 8, 256), grad_one, grad_proj, grad_class.T, loss.reshape(()))


def solution(mesh):
    return jax.shard_map(
        on_device,
        mesh=mesh,
        in_specs=(P("dp", "space", None, None), P("dp", "space", None), P(), P(), P(), P()),
        out_specs=(P(None, None, None, ("dp", "space"), None), P(), P(), P(), P()),
        check_vma=False,
    )
```

```python
import math

import jax
import jax.numpy as jnp
from jax import lax
from jax.experimental import pallas as pl
from jax.experimental.pallas import tpu as pltpu
from jax.sharding import PartitionSpec as P

MESH = pl.DeviceIdType.MESH
BF = jnp.bfloat16
F32 = jnp.float32
WIDTH = 56
BLK = 6 * WIDTH
OWN = 12 * WIDTH
CHIP = 24 * WIDTH
BASE = 1
XB = 2
ORDER = ("xzy", "zyx", "yxz")
SMALL = "yzx"
AXES = "xzy"


def slope(pre):
    gate = jax.nn.sigmoid(pre)
    return gate * (1.0 + pre * (1.0 - gate))


def silu(pre):
    return pre * jax.nn.sigmoid(pre)


def mm(first, second):
    return jnp.dot(first, second, preferred_element_type=F32)


def mm_t(first, second):
    return lax.dot_general(first, second, (((1,), (1,)), ((), ())), preferred_element_type=F32)


def t_mm(first, second):
    return lax.dot_general(first, second, (((0,), (0,)), ((), ())), preferred_element_type=F32)


def kernel(
    loss_scale,
    feat, labels, w_one_h, w_atr_h, w_proj, w_cls,
    o_atr, eout, o_cls,
    xbuf, wbuf, wone, tacc, pre, pre0, cs, cr, joined, dh, ext, db0, raw, hraw,
    s1, r1, s2, r2, s3, r3, fin, pbuf, clbuf, swap, lab,
    lsem, ssem, rsem,
):
    dp = lax.axis_index("dp")
    sp = lax.axis_index("space")
    core, s = sp % 2, sp // 2
    cx, cz, cy = dp // 8, (dp // 2) % 4, (dp % 2) * 2 + s
    here = {"x": cx, "z": cz, "y": cy}

    def place(x, z, y, c):
        return (x * 8 + z * 2 + y // 2, (y % 2) * 2 + c)

    partner = place(cx, cz, cy, 1 - core)
    across = (dp, (1 - s) * 2 + core)
    beyond = (dp, (1 - s) * 2 + 1 - core)

    def peer(axis, d):
        at = dict(here)
        at[axis] = (at[axis] + d) % 4
        return place(at["x"], at["z"], at["y"], core)

    rate = 12 + 6 * core
    k = 2 + core

    counter = [UNITS * 12 + 7]

    def remote(src, dst, to, i=None):
        if i is None:
            i = counter[0]
            counter[0] += 1
        return pltpu.make_async_remote_copy(
            src_ref=src, dst_ref=dst, send_sem=ssem.at[i], recv_sem=rsem.at[i], device_id=to, device_id_type=MESH
        )

    sends = []

    def go(copy):
        copy.start()
        sends.append(copy)
        return copy

    own_rows = pl.ds(pl.multiple_of(core * OWN, 16), OWN)
    other_rows = pl.ds(pl.multiple_of((1 - core) * OWN, 16), OWN)
    x_own = pl.ds(pl.multiple_of(XB * BLK + core * OWN, 16), OWN)
    x_local = pltpu.make_async_copy(feat, xbuf.at[x_own], lsem.at[0])
    x_local.start()
    w_local = [pltpu.make_async_copy(w_atr_h.at[core, a], wbuf.at[a], lsem.at[1 + a]) for a in range(3)]
    for a in (1, 0, 2):
        w_local[a].start()
    one_local = pltpu.make_async_copy(w_one_h, wone, lsem.at[4])
    one_local.start()

    barrier = pltpu.get_barrier_semaphore()
    greet = [partner, beyond] + [peer(axis, d) for axis in AXES for d in (1, 2, 3)]
    for other in greet:
        pl.semaphore_signal(barrier, inc=1, device_id=other, device_id_type=MESH)

    tacc[...] = jnp.zeros_like(tacc)

    column = lax.rem(lax.broadcasted_iota(jnp.int32, (BLK, 256), 0), WIDTH)

    def from_left(value):
        return jnp.where(column >= rate, pltpu.roll(value, rate, 0), 0.0)

    def from_right(value):
        return jnp.where(column < WIDTH - rate, pltpu.roll(value, BLK - rate, 0), 0.0)

    def block(m):
        return pl.ds(pl.multiple_of(m * BLK, 16), BLK)

    def middle(m):
        rows = xbuf[block(XB + m), :]
        for b in range(3):
            tacc[m, b] += mm(rows, wbuf[1, b])

    def outer(m):
        for a in (0, 2):
            to = m - (a - 1) * k

            @pl.when((to >= 0) & (to < 4))
            def _(a=a, to=to):
                rows = xbuf[block(XB + m), :]
                for b in range(3):
                    tacc[to, b] += mm(rows, wbuf[a, b])

    def cross_copy(t):
        return remote(cs.at[t], cr.at[t], across, UNITS * 12 + t)

    cross_tap = s * 2

    def cross(m):
        @pl.when(jnp.where(s == 0, m + k >= 4, m < k))
        def _():
            t = jnp.where(s == 0, m + k - 4, m)
            rows = xbuf[block(XB + m), :]
            parts = [mm(rows, wbuf[cross_tap, b]) for b in range(3)]
            cs[t] = (parts[1] + from_left(parts[0]) + from_right(parts[2])).astype(BF)
            cross_copy(t).start()

    mine, theirs = 2 * core, 2 * (1 - core)
    x_local.wait()
    w_local[1].wait()
    pl.loop(0, 2)(lambda q: middle(mine + q))
    pl.semaphore_wait(barrier, len(greet))
    x_swap = go(remote(feat, xbuf.at[x_own], partner))
    w_local[0].wait()
    w_local[2].wait()
    pl.loop(0, 2)(lambda q: cross(mine + q))
    pl.loop(0, 2)(lambda q: outer(mine + q))
    x_swap.wait_recv()
    pl.loop(0, 2)(lambda q: cross(theirs + q))

    @pl.loop(0, 2)
    def _(q):
        middle(theirs + q)
        outer(theirs + q)

    def halo(j):
        to = block(jnp.where(s == 0, j, XB + 4 + j))
        return remote(feat.at[j * BLK : (j + 1) * BLK], xbuf.at[to], (dp, (1 - s) * 2 + j), UNITS * 12 + 4 + j)

    @pl.when(core == 1 - s)
    def _():
        for j in range(2):
            halo(j).start()

    @pl.loop(0, 4)
    def _(i):
        pre[block(i), :] = tacc[i, 1] + from_left(tacc[i, 0]) + from_right(tacc[i, 2])

    one_local.wait()

    @pl.when(core == 1)
    def _():
        @pl.loop(0, 4)
        def _(i):
            value = mm(xbuf[block(XB + i), :], wone[...])
            pre0[block(i), :] = value
            joined[0, block(i), :] = silu(value).astype(BF)

    for t in range(3):
        @pl.when(t < k)
        def _(t=t):
            cross_copy(t).wait_recv()
            into = block(jnp.where(s == 0, 4 - k + t, t))
            pre[into, :] += cr[t].astype(F32)

    @pl.loop(0, 4)
    def _(i):
        joined[1 + core, block(i), :] = silu(pre[block(i), :]).astype(BF)

    j_copies = [remote(joined.at[b, other_rows], joined.at[b, other_rows], partner) for b in range(3)]

    @pl.when(core == 0)
    def _():
        j_copies[1].start()

    @pl.when(core == 1)
    def _():
        j_copies[0].start()
        j_copies[2].start()

    @pl.when(core == 0)
    def _():
        j_copies[0].wait_recv()
        j_copies[2].wait_recv()

    @pl.when(core == 1)
    def _():
        j_copies[1].wait_recv()

    pre_hidden = mm(joined[0, own_rows, :], w_proj[0])
    pre_hidden += mm(joined[1, own_rows, :], w_proj[1])
    pre_hidden += mm(joined[2, own_rows, :], w_proj[2])
    hidden = silu(pre_hidden).astype(BF)
    classes = jnp.concatenate([w_cls[...].astype(F32), jnp.zeros((13, 256), F32)]).astype(BF)
    for y in range(12):
        lab[:, y * WIDTH : (y + 1) * WIDTH] = labels[y]
    logits = mm_t(classes, hidden)
    row = lax.broadcasted_iota(jnp.int32, logits.shape, 0)
    valid = row < 3
    top = jnp.max(jnp.where(valid, logits, -jnp.inf), axis=0, keepdims=True)
    total = jnp.sum(jnp.where(valid, jnp.exp(logits - top), 0.0), axis=0, keepdims=True)
    lse = top + jnp.log(total)
    onehot = row == lab[...]
    loss = jnp.sum(lse - jnp.sum(jnp.where(onehot, logits, 0.0), axis=0, keepdims=True), axis=1, keepdims=True)
    probs = jnp.exp(logits - lse) - jnp.where(onehot, 1.0, 0.0)
    dlogits = jnp.where(valid, probs * loss_scale, 0.0).astype(BF)
    dhidden = t_mm(dlogits, classes) * slope(pre_hidden)
    dh[own_rows, :] = dhidden.astype(BF)
    dh_copy = go(remote(dh.at[own_rows], dh.at[own_rows], partner))

    small = mm(dlogits, hidden)
    srow = lax.broadcasted_iota(jnp.int32, small.shape, 0)
    cl_copies = []
    for n, axis in enumerate(AXES):
        cl_copies.append([remote(clbuf.at[n, here[axis]], clbuf.at[n, here[axis]], peer(axis, d)) for d in (1, 2, 3)])
    cl_copies.append([remote(clbuf.at[3, core], clbuf.at[3, core], partner)])
    clbuf[0, here["x"]] = jnp.where(srow == 3, loss, small)
    for copy in cl_copies[0]:
        go(copy)

    def small_step(n):
        for copy in cl_copies[n]:
            copy.wait_recv()
        value = clbuf[n, 0] + clbuf[n, 1]
        if n < 3:
            value = value + clbuf[n, 2] + clbuf[n, 3]
            clbuf[n + 1, core if n == 2 else here[AXES[n + 1]]] = value
            for copy in cl_copies[n + 1]:
                go(copy)
        else:
            o_cls[...] = value

    branch_w = w_proj[1 + core]

    raw_copy = remote(raw.at[block(jnp.where(s == 0, 3, 0))], hraw, across, UNITS * 12 + 3)

    def branch_grad(i):
        value = mm_t(dh[block(i), :], branch_w) * slope(pre[block(i), :])
        raw[block(i), :] = value.astype(BF)

        @pl.when((core == 1) & (i == jnp.where(s == 0, 3, 0)))
        def _():
            raw_copy.start()

        to = block(BASE + i)
        rounded = value.astype(BF).astype(F32)
        ext[0, to, :] = from_right(rounded).astype(BF)
        ext[1, to, :] = rounded.astype(BF)
        ext[2, to, :] = from_left(rounded).astype(BF)

    pl.loop(0, 2)(lambda q: branch_grad(mine + q))
    dh_copy.wait_recv()
    pl.loop(0, 2)(lambda q: branch_grad(theirs + q))

    low, high = pl.ds(0, 2), pl.ds(2, 2)

    def plan(u, order, ring):
        out = []
        for phase, (buf, landing) in enumerate(((s1, r1), (s2, r2), (s3, r3))):
            axis = order[phase]
            left = [a for a in AXES if a in order[phase:]]
            spot = left.index(axis)
            c = here[axis]
            base = u * 12 + (0, 6, 9)[phase]

            def chunk(at, half=None):
                index = [u] + [slice(None)] * len(left)
                index[1 + spot] = (at + 4) % 4
                if half is not None:
                    index[2 if spot == 0 else 1] = half
                return buf.at[tuple(index)]

            def land(slot, half=None):
                return landing.at[u, slot] if half is None else landing.at[u, slot, half]

            if phase or not ring:
                copies = [remote(chunk(c + d), land(d - 1), peer(axis, d), base + d - 1) for d in (2, 1, 3)]
                out.append((chunk(c), [land(n) for n in range(3)], copies, (), (), ()))
                continue
            up, down = peer(axis, 1), peer(axis, 3)
            way = [
                remote(chunk(c + 2, low), land(2, low), up, base),
                remote(chunk(c + 2, high), land(2, high), down, base + 1),
            ]
            copies = [
                remote(chunk(c + 1, high), land(0, high), up, base + 2),
                remote(chunk(c - 1, low), land(1, low), down, base + 3),
            ]
            later = [
                remote(chunk(c + 1, low), land(0, low), up, base + 4),
                remote(chunk(c - 1, high), land(1, high), down, base + 5),
            ]
            sums = [(chunk(c + 1, low), land(2, low)), (chunk(c - 1, high), land(2, high))]
            out.append((chunk(c), [land(0), land(1)], copies, way, later, sums))
        return u, out

    def send(unit, phase):
        _, _, copies, way, _, _ = unit[1][phase]
        for copy in list(way) + copies:
            go(copy)

    def forward(unit):
        _, _, _, way, later, sums = unit[1][0]
        for n in range(2):
            way[n].wait_recv()
            out, got = sums[n]
            out[...] = (out[...].astype(F32) + got[...].astype(F32)).astype(BF)
            go(later[n])

    def settle(unit, phase):
        u, phases = unit
        own, lands, copies, _, later, _ = phases[phase]
        for copy in copies + list(later):
            copy.wait_recv()
        value = own[...].astype(F32)
        for got in lands:
            value = value + got[...].astype(F32)
        if phase < 2:
            into = (s2, s3)[phase]
            into[u] = value.astype(into.dtype)
            send(unit, phase + 1)
        else:
            fin[u] = value

    mids = [plan(b, ORDER[b], True) for b in range(3)]
    outers = [plan(3 + 3 * g + b, ORDER[b], True) for b in range(3) for g in range(2)]
    nears = [plan(3 + 3 * s + b, ORDER[b], True) for b in range(3)]
    fars = [plan(3 + 3 * (1 - s) + b, ORDER[b], True) for b in range(3)]
    smalls = plan(9, SMALL, False)

    def proj_grad(b):
        return t_mm(joined[b], dh[...]).astype(BF).reshape(4, 4, 16, 256)

    p_copies = [remote(pbuf.at[n], s1.at[9, 2 * n], partner) for n in range(2)]

    def tap(u, rows, grad):
        for c in range(4):
            value = t_mm(xbuf[rows, c * 256 : (c + 1) * 256], grad)
            s1[u, c] = value.astype(BF).reshape(4, 4, 16, 256)

    everyone = pl.ds(XB * BLK, CHIP)

    @pl.when(core == 1)
    def _():
        for n in range(2):
            pbuf[n] = proj_grad(2 * n)
            p_copies[n].start()

        @pl.loop(0, 4)
        def _(i):
            value = mm_t(dh[block(i), :], w_proj[0]) * slope(pre0[block(i), :])
            db0[block(i), :] = value.astype(BF)

        tap(9, everyone, db0[...])

    @pl.when(core == 0)
    def _():
        s1[9, 1] = proj_grad(1)
        s1[9, 3] = jnp.zeros((4, 4, 16, 256), BF)
        for n in range(2):
            p_copies[n].wait_recv()

    send(smalls, 0)

    def rows_from(m, count):
        return pl.ds(pl.multiple_of(m * BLK, 16), count * BLK)

    for b in range(3):
        tap(b, everyone, ext[b, rows_from(BASE, 4), :])
        send(mids[b], 0)
    small_step(0)

    @pl.when(core == 1)
    def _():
        raw_copy.wait_recv()
        to = block(jnp.where(s == 0, BASE + 4, BASE - 1))
        value = hraw[...].astype(F32)
        ext[0, to, :] = from_right(value).astype(BF)
        ext[1, to, :] = hraw[...]
        ext[2, to, :] = from_left(value).astype(BF)

    passed_rows = block(jnp.where(s == 0, XB + 4, 0) + core)
    remote(feat.at[0:BLK], xbuf.at[passed_rows], across, UNITS * 12 + 4 + core).wait_recv()
    passed = go(remote(xbuf.at[passed_rows], xbuf.at[passed_rows], partner, UNITS * 12 + 6))

    for b in range(3):
        x_at = XB + jnp.where(s == 0, 0, 2)
        g_at = BASE + jnp.where(s == 0, k, 2 - k)
        tap(nears[b][0], rows_from(x_at, 2), ext[b, rows_from(g_at, 2), :])
        send(nears[b], 0)

    passed.wait_recv()
    for b in range(3):
        for n in range(2):
            @pl.when(core == n)
            def _(n=n, b=b):
                x_at = jnp.where(s == 0, XB + 2 + n, 0)
                g_at = BASE + jnp.where(s == 0, 0, n)
                tap(fars[b][0], rows_from(x_at, 4 - n), ext[b, rows_from(g_at, 4 - n), :])
        send(fars[b], 0)

    for unit in mids:
        forward(unit)
    settle(smalls, 0)
    for unit in outers:
        forward(unit)
    for unit in mids:
        settle(unit, 0)
    settle(smalls, 1)
    for unit in outers:
        settle(unit, 0)
    small_step(1)
    settle(smalls, 2)

    eout[core, cx, cz, cy] = fin[9].astype(BF)
    everything = slice(None)

    def gather(axis, at):
        view = eout.at[(core,) + at]
        return [remote(view, view, peer(axis, d)) for d in (2, 1, 3)]

    gathers = [gather("z", (cx, cz, cy)), gather("y", (cx, everything, cy)), gather("x", (cx, everything, everything))]

    def gather_next(n):
        for copy in gathers[n - 1] if n else ():
            copy.wait_recv()
        for copy in gathers[n] if n < 3 else ():
            go(copy)

    gather_next(0)
    for unit in mids:
        settle(unit, 1)
    gather_next(1)
    for unit in outers:
        settle(unit, 1)
    gather_next(2)
    small_step(2)
    for unit in mids:
        settle(unit, 2)
    for unit in outers:
        settle(unit, 2)

    give = pl.ds(pl.multiple_of((1 - core) * 8, 8), 8)
    keep = pl.ds(pl.multiple_of(core * 8, 8), 8)
    swap[0] = fin[0:9, give, :]
    f_swap = go(remote(swap.at[0], swap.at[1], partner))
    small_step(3)
    gather_next(3)
    e_swap = go(remote(eout.at[core], eout.at[core], partner))

    e_swap.wait_recv()
    f_swap.wait_recv()
    for u in range(9):
        at = u + 3 if u < 3 else u - 3 if u < 6 else u
        o_atr[core, at] = fin[u, keep, :]
        o_atr[1 - core, at] = swap[1, u]

    for t in range(3):
        @pl.when(t < k)
        def _(t=t):
            cross_copy(t).wait_send()

    @pl.when(core == 1 - s)
    def _():
        for j in range(2):
            halo(j).wait_send()

    @pl.when(core == 1)
    def _():
        raw_copy.wait_send()

    @pl.when(core == 0)
    def _():
        j_copies[1].wait_send()

    @pl.when(core == 1)
    def _():
        for copy in (j_copies[0], j_copies[2], p_copies[0], p_copies[1]):
            copy.wait_send()

    for copy in sends:
        copy.wait_send()
    assert counter[0] <= COPIES


COPIES = 180
UNITS = 10


def widen(scale, shares, small, tiny, o_atr, o_one, o_proj, o_cls, o_loss):
    o_atr[...] = shares[...]
    o_proj[...] = small[0, 0:768].astype(F32)
    o_one[...] = small[1].astype(F32)
    o_cls[...] = tiny[0:3]
    o_loss[...] = tiny[3:4, 0:1] * scale


def on_device(features, labels, w_one, w_atrous, w_proj, w_class):
    total_pix = lax.axis_size("dp") * lax.axis_size("space") * OWN
    vmem = pl.BlockSpec(memory_space=pltpu.VMEM)
    hbm = pl.BlockSpec(memory_space=pl.ANY)
    scratch = [
        ((8 * BLK, 1024), BF),
        ((3, 3, 1024, 256), BF),
        ((1024, 256), BF),
        ((4, 3, BLK, 256), F32),
        ((CHIP, 256), F32),
        ((CHIP, 256), F32),
        ((3, BLK, 256), BF),
        ((3, BLK, 256), BF),
        ((3, CHIP, 256), BF),
        ((CHIP, 256), BF),
        ((3, 6 * BLK, 256), BF),
        ((CHIP, 256), BF),
        ((CHIP, 256), BF),
        ((BLK, 256), BF),
        ((UNITS, 4, 4, 4, 16, 256), BF),
        ((UNITS, 3, 4, 4, 16, 256), BF),
        ((UNITS, 4, 4, 16, 256), BF),
        ((UNITS, 3, 4, 16, 256), BF),
        ((UNITS, 4, 16, 256), F32),
        ((UNITS, 3, 16, 256), F32),
        ((UNITS, 16, 256), F32),
        ((2, 4, 4, 16, 256), BF),
        ((4, 4, 16, 256), F32),
        ((2, 9, 8, 256), F32),
        ((1, OWN), jnp.int32),
    ]
    shares, small, tiny = pl.pallas_call(
        lambda *refs: kernel(1.0 / math.sqrt(total_pix), *refs),
        out_shape=(
            jax.ShapeDtypeStruct((2, 9, 8, 256), F32),
            jax.ShapeDtypeStruct((2, 4, 4, 4, 16, 256), BF),
            jax.ShapeDtypeStruct((16, 256), F32),
        ),
        in_specs=[hbm, vmem, hbm, hbm, vmem, vmem],
        out_specs=(vmem, vmem, vmem),
        scratch_shapes=[pltpu.VMEM(shape, kind) for shape, kind in scratch]
        + [
            pltpu.SemaphoreType.DMA((5,)),
            pltpu.SemaphoreType.DMA((COPIES,)),
            pltpu.SemaphoreType.DMA((COPIES,)),
        ],
        compiler_params=pltpu.CompilerParams(
            collective_id=0, has_side_effects=True, vmem_limit_bytes=60 * 1024 * 1024
        ),
        name="aspp",
    )(
        features.reshape(OWN, 1024),
        labels.transpose(1, 0, 2),
        w_one,
        w_atrous,
        w_proj.reshape(3, 256, 256),
        w_class.T,
    )
    grad_atrous, grad_one, grad_proj, grad_class, loss = pl.pallas_call(
        lambda *refs: widen(1.0 / total_pix, *refs),
        out_shape=(
            jax.ShapeDtypeStruct((2, 9, 8, 256), F32),
            jax.ShapeDtypeStruct((1024, 256), F32),
            jax.ShapeDtypeStruct((768, 256), F32),
            jax.ShapeDtypeStruct((3, 256), F32),
            jax.ShapeDtypeStruct((1, 1), F32),
        ),
        in_specs=[vmem] * 3,
        out_specs=(vmem,) * 5,
        name="widen",
    )(shares, small.reshape(2, 1024, 256), tiny)
    return (grad_atrous.reshape(2, 3, 3, 8, 256), grad_one, grad_proj, grad_class.T, loss.reshape(()))


def solution(mesh):
    return jax.shard_map(
        on_device,
        mesh=mesh,
        in_specs=(P("dp", "space", None, None), P("dp", "space", None), P(), P(), P(), P()),
        out_specs=(P(None, None, None, ("dp", "space"), None), P(), P(), P(), P()),
        check_vma=False,
    )
```

```python
import math

import jax
import jax.numpy as jnp
from jax import lax
from jax.experimental import pallas as pl
from jax.experimental.pallas import tpu as pltpu
from jax.sharding import PartitionSpec as P

MESH = pl.DeviceIdType.MESH
BF = jnp.bfloat16
F32 = jnp.float32
WIDTH = 56
BLK = 6 * WIDTH
OWN = 12 * WIDTH
CHIP = 24 * WIDTH
BASE = 1
XB = 2
ORDER = ("xzy", "zyx", "yxz")
SMALL = "yzx"
AXES = "xzy"


def slope(pre):
    gate = jax.nn.sigmoid(pre)
    return gate * (1.0 + pre * (1.0 - gate))


def silu(pre):
    return pre * jax.nn.sigmoid(pre)


def mm(first, second):
    return jnp.dot(first, second, preferred_element_type=F32)


def mm_t(first, second):
    return lax.dot_general(first, second, (((1,), (1,)), ((), ())), preferred_element_type=F32)


def t_mm(first, second):
    return lax.dot_general(first, second, (((0,), (0,)), ((), ())), preferred_element_type=F32)


def kernel(
    loss_scale,
    feat, labels, w_one_h, w_atr_h, w_proj, w_cls,
    o_atr, eout, o_cls,
    xbuf, wbuf, wtow, wone, tacc, pre, pre0, cs, cr, joined, dh, ext, db0, raw, hraw,
    s1, r1, s2, r2, s3, r3, fin, pbuf, clbuf, swap, lab,
    lsem, ssem, rsem,
):
    dp = lax.axis_index("dp")
    sp = lax.axis_index("space")
    core, s = sp % 2, sp // 2
    cx, cz, cy = dp // 8, (dp // 2) % 4, (dp % 2) * 2 + s
    here = {"x": cx, "z": cz, "y": cy}

    def place(x, z, y, c):
        return (x * 8 + z * 2 + y // 2, (y % 2) * 2 + c)

    partner = place(cx, cz, cy, 1 - core)
    across = (dp, (1 - s) * 2 + core)
    beyond = (dp, (1 - s) * 2 + 1 - core)

    def peer(axis, d):
        at = dict(here)
        at[axis] = (at[axis] + d) % 4
        return place(at["x"], at["z"], at["y"], core)

    rate = 12 + 6 * core
    k = 2 + core

    counter = [UNITS * 12 + 13]

    def remote(src, dst, to, i=None, sent=None):
        if i is None:
            i = counter[0]
            counter[0] += 1
        return pltpu.make_async_remote_copy(
            src_ref=src, dst_ref=dst, send_sem=ssem.at[i if sent is None else sent], recv_sem=rsem.at[i], device_id=to, device_id_type=MESH
        )

    sends = []

    def go(copy):
        copy.start()
        sends.append(copy)
        return copy

    own_rows = pl.ds(pl.multiple_of(core * OWN, 16), OWN)
    other_rows = pl.ds(pl.multiple_of((1 - core) * OWN, 16), OWN)
    x_own = pl.ds(pl.multiple_of(XB * BLK + core * OWN, 16), OWN)
    x_local = pltpu.make_async_copy(feat, xbuf.at[x_own], lsem.at[0])
    x_local.start()
    w_local = [pltpu.make_async_copy(w_atr_h.at[core, a], wbuf.at[a], lsem.at[1 + a]) for a in range(3)]
    cross_tap = s * 2
    tow_local = [pltpu.make_async_copy(w_atr_h.at[g, cross_tap], wtow.at[g], lsem.at[5 + g]) for g in range(2)]
    for copy in (tow_local[1], tow_local[0], w_local[1], w_local[0], w_local[2]):
        copy.start()
    one_local = pltpu.make_async_copy(w_one_h, wone, lsem.at[4])
    one_local.start()

    barrier = pltpu.get_barrier_semaphore()
    greet = [partner, beyond] + [peer(axis, d) for axis in AXES for d in (1, 2, 3)]
    for other in greet:
        pl.semaphore_signal(barrier, inc=1, device_id=other, device_id_type=MESH)

    tacc[...] = jnp.zeros_like(tacc)

    column = lax.rem(lax.broadcasted_iota(jnp.int32, (BLK, 256), 0), WIDTH)

    def from_left(value, rate=rate):
        return jnp.where(column >= rate, pltpu.roll(value, rate, 0), 0.0)

    def from_right(value, rate=rate):
        return jnp.where(column < WIDTH - rate, pltpu.roll(value, BLK - rate, 0), 0.0)

    def block(m):
        return pl.ds(pl.multiple_of(m * BLK, 16), BLK)

    def middle(m):
        rows = xbuf[block(XB + m), :]
        for b in range(3):
            tacc[m, b] += mm(rows, wbuf[1, b])

    def outer(m):
        for a in (0, 2):
            to = m - (a - 1) * k

            @pl.when((to >= 0) & (to < 4))
            def _(a=a, to=to):
                rows = xbuf[block(XB + m), :]
                for b in range(3):
                    tacc[to, b] += mm(rows, wbuf[a, b])

    def cross_copy(t, g=None):
        if g is None:
            return remote(cs.at[0, t], cr.at[t], across, UNITS * 12 + t)
        to = (dp, (1 - s) * 2 + g)
        return remote(cs.at[g, t], cr.at[t], to, UNITS * 12 + t, UNITS * 12 + 7 + 3 * g + t)

    def crossing(body):
        for g, t in ((1, 0), (1, 1), (1, 2), (0, 0), (0, 1)):
            m = jnp.where(s == 0, 2 - g + t, t)

            @pl.when(m // 2 == core)
            def _(g=g, t=t, m=m):
                body(g, t, m)

    def cross(g, t, m):
        rows = xbuf[block(XB + m), :]
        parts = [mm(rows, wtow[g, b]) for b in range(3)]
        shifted = from_left(parts[0], 12 + 6 * g) + from_right(parts[2], 12 + 6 * g)
        cs[g, t] = (parts[1] + shifted).astype(BF)

    mine, theirs = 2 * core, 2 * (1 - core)
    x_local.wait()
    for copy in tow_local:
        copy.wait()
    crossing(cross)
    pl.semaphore_wait(barrier, len(greet))
    crossing(lambda g, t, m: cross_copy(t, g).start())
    x_swap = go(remote(feat, xbuf.at[x_own], partner))
    for copy in (w_local[1], w_local[0], w_local[2]):
        copy.wait()
    pl.loop(0, 2)(lambda q: middle(mine + q))
    pl.loop(0, 2)(lambda q: outer(mine + q))
    x_swap.wait_recv()

    @pl.loop(0, 2)
    def _(q):
        middle(theirs + q)
        outer(theirs + q)

    def halo(j):
        to = block(jnp.where(s == 0, j, XB + 4 + j))
        return remote(feat.at[j * BLK : (j + 1) * BLK], xbuf.at[to], (dp, (1 - s) * 2 + j), UNITS * 12 + 4 + j)

    @pl.when(core == 1 - s)
    def _():
        for j in range(2):
            halo(j).start()

    @pl.loop(0, 4)
    def _(i):
        pre[block(i), :] = tacc[i, 1] + from_left(tacc[i, 0]) + from_right(tacc[i, 2])

    one_local.wait()

    @pl.when(core == 1)
    def _():
        @pl.loop(0, 4)
        def _(i):
            value = mm(xbuf[block(XB + i), :], wone[...])
            pre0[block(i), :] = value
            joined[0, block(i), :] = silu(value).astype(BF)

    for t in range(3):
        @pl.when(t < k)
        def _(t=t):
            cross_copy(t).wait_recv()
            into = block(jnp.where(s == 0, 4 - k + t, t))
            pre[into, :] += cr[t].astype(F32)

    @pl.loop(0, 4)
    def _(i):
        joined[1 + core, block(i), :] = silu(pre[block(i), :]).astype(BF)

    j_copies = [remote(joined.at[b, other_rows], joined.at[b, other_rows], partner) for b in range(3)]

    @pl.when(core == 0)
    def _():
        j_copies[1].start()

    @pl.when(core == 1)
    def _():
        j_copies[0].start()
        j_copies[2].start()

    @pl.when(core == 0)
    def _():
        j_copies[0].wait_recv()
        j_copies[2].wait_recv()

    @pl.when(core == 1)
    def _():
        j_copies[1].wait_recv()

    pre_hidden = mm(joined[0, own_rows, :], w_proj[0])
    pre_hidden += mm(joined[1, own_rows, :], w_proj[1])
    pre_hidden += mm(joined[2, own_rows, :], w_proj[2])
    hidden = silu(pre_hidden).astype(BF)
    classes = jnp.concatenate([w_cls[...].astype(F32), jnp.zeros((13, 256), F32)]).astype(BF)
    for y in range(12):
        lab[:, y * WIDTH : (y + 1) * WIDTH] = labels[y]
    logits = mm_t(classes, hidden)
    row = lax.broadcasted_iota(jnp.int32, logits.shape, 0)
    valid = row < 3
    top = jnp.max(jnp.where(valid, logits, -jnp.inf), axis=0, keepdims=True)
    total = jnp.sum(jnp.where(valid, jnp.exp(logits - top), 0.0), axis=0, keepdims=True)
    lse = top + jnp.log(total)
    onehot = row == lab[...]
    loss = jnp.sum(lse - jnp.sum(jnp.where(onehot, logits, 0.0), axis=0, keepdims=True), axis=1, keepdims=True)
    probs = jnp.exp(logits - lse) - jnp.where(onehot, 1.0, 0.0)
    dlogits = jnp.where(valid, probs * loss_scale, 0.0).astype(BF)
    dhidden = t_mm(dlogits, classes) * slope(pre_hidden)
    dh[own_rows, :] = dhidden.astype(BF)
    dh_copy = go(remote(dh.at[own_rows], dh.at[own_rows], partner))

    small = mm(dlogits, hidden)
    srow = lax.broadcasted_iota(jnp.int32, small.shape, 0)
    cl_copies = []
    for n, axis in enumerate(AXES):
        cl_copies.append([remote(clbuf.at[n, here[axis]], clbuf.at[n, here[axis]], peer(axis, d)) for d in (1, 2, 3)])
    cl_copies.append([remote(clbuf.at[3, core], clbuf.at[3, core], partner)])
    clbuf[0, here["x"]] = jnp.where(srow == 3, loss, small)
    for copy in cl_copies[0]:
        go(copy)

    def small_step(n):
        for copy in cl_copies[n]:
            copy.wait_recv()
        value = clbuf[n, 0] + clbuf[n, 1]
        if n < 3:
            value = value + clbuf[n, 2] + clbuf[n, 3]
            clbuf[n + 1, core if n == 2 else here[AXES[n + 1]]] = value
            for copy in cl_copies[n + 1]:
                go(copy)
        else:
            o_cls[...] = value

    branch_w = w_proj[1 + core]

    raw_copy = remote(raw.at[block(jnp.where(s == 0, 3, 0))], hraw, across, UNITS * 12 + 3)

    def branch_grad(i):
        value = mm_t(dh[block(i), :], branch_w) * slope(pre[block(i), :])
        raw[block(i), :] = value.astype(BF)

        @pl.when((core == 1) & (i == jnp.where(s == 0, 3, 0)))
        def _():
            raw_copy.start()

        to = block(BASE + i)
        rounded = value.astype(BF).astype(F32)
        ext[0, to, :] = from_right(rounded).astype(BF)
        ext[1, to, :] = rounded.astype(BF)
        ext[2, to, :] = from_left(rounded).astype(BF)

    pl.loop(0, 2)(lambda q: branch_grad(mine + q))
    dh_copy.wait_recv()
    pl.loop(0, 2)(lambda q: branch_grad(theirs + q))

    low, high = pl.ds(0, 2), pl.ds(2, 2)

    def plan(u, order, ring):
        out = []
        for phase, (buf, landing) in enumerate(((s1, r1), (s2, r2), (s3, r3))):
            axis = order[phase]
            left = [a for a in AXES if a in order[phase:]]
            spot = left.index(axis)
            c = here[axis]
            base = u * 12 + (0, 6, 9)[phase]

            def chunk(at, half=None):
                index = [u] + [slice(None)] * len(left)
                index[1 + spot] = (at + 4) % 4
                if half is not None:
                    index[2 if spot == 0 else 1] = half
                return buf.at[tuple(index)]

            def land(slot, half=None):
                return landing.at[u, slot] if half is None else landing.at[u, slot, half]

            if phase or not ring:
                copies = [remote(chunk(c + d), land(d - 1), peer(axis, d), base + d - 1) for d in (2, 1, 3)]
                out.append((chunk(c), [land(n) for n in range(3)], copies, (), (), ()))
                continue
            up, down = peer(axis, 1), peer(axis, 3)
            way = [
                remote(chunk(c + 2, low), land(2, low), up, base),
                remote(chunk(c + 2, high), land(2, high), down, base + 1),
            ]
            copies = [
                remote(chunk(c + 1, high), land(0, high), up, base + 2),
                remote(chunk(c - 1, low), land(1, low), down, base + 3),
            ]
            later = [
                remote(chunk(c + 1, low), land(0, low), up, base + 4),
                remote(chunk(c - 1, high), land(1, high), down, base + 5),
            ]
            sums = [(chunk(c + 1, low), land(2, low)), (chunk(c - 1, high), land(2, high))]
            out.append((chunk(c), [land(0), land(1)], copies, way, later, sums))
        return u, out

    def send(unit, phase):
        _, _, copies, way, _, _ = unit[1][phase]
        for copy in list(way) + copies:
            go(copy)

    def forward(unit):
        _, _, _, way, later, sums = unit[1][0]
        for n in range(2):
            way[n].wait_recv()
            out, got = sums[n]
            out[...] = (out[...].astype(F32) + got[...].astype(F32)).astype(BF)
            go(later[n])

    def settle(unit, phase):
        u, phases = unit
        own, lands, copies, _, later, _ = phases[phase]
        for copy in copies + list(later):
            copy.wait_recv()
        value = own[...].astype(F32)
        for got in lands:
            value = value + got[...].astype(F32)
        if phase < 2:
            into = (s2, s3)[phase]
            into[u] = value.astype(into.dtype)
            send(unit, phase + 1)
        else:
            fin[u] = value

    mids = [plan(b, ORDER[b], True) for b in range(3)]
    outers = [plan(3 + 3 * g + b, ORDER[b], True) for b in range(3) for g in range(2)]
    nears = [plan(3 + 3 * s + b, ORDER[b], True) for b in range(3)]
    fars = [plan(3 + 3 * (1 - s) + b, ORDER[b], True) for b in range(3)]
    smalls = plan(9, SMALL, False)

    def proj_grad(b):
        return t_mm(joined[b], dh[...]).astype(BF).reshape(4, 4, 16, 256)

    p_copies = [remote(pbuf.at[n], s1.at[9, 2 * n], partner) for n in range(2)]

    def tap(u, rows, grad):
        for c in range(4):
            value = t_mm(xbuf[rows, c * 256 : (c + 1) * 256], grad)
            s1[u, c] = value.astype(BF).reshape(4, 4, 16, 256)

    everyone = pl.ds(XB * BLK, CHIP)

    @pl.when(core == 1)
    def _():
        for n in range(2):
            pbuf[n] = proj_grad(2 * n)
            p_copies[n].start()

        @pl.loop(0, 4)
        def _(i):
            value = mm_t(dh[block(i), :], w_proj[0]) * slope(pre0[block(i), :])
            db0[block(i), :] = value.astype(BF)

        tap(9, everyone, db0[...])

    @pl.when(core == 0)
    def _():
        s1[9, 1] = proj_grad(1)
        s1[9, 3] = jnp.zeros((4, 4, 16, 256), BF)
        for n in range(2):
            p_copies[n].wait_recv()

    send(smalls, 0)

    def rows_from(m, count):
        return pl.ds(pl.multiple_of(m * BLK, 16), count * BLK)

    for b in range(3):
        tap(b, everyone, ext[b, rows_from(BASE, 4), :])
        send(mids[b], 0)
    small_step(0)

    @pl.when(core == 1)
    def _():
        raw_copy.wait_recv()
        to = block(jnp.where(s == 0, BASE + 4, BASE - 1))
        value = hraw[...].astype(F32)
        ext[0, to, :] = from_right(value).astype(BF)
        ext[1, to, :] = hraw[...]
        ext[2, to, :] = from_left(value).astype(BF)

    passed_rows = block(jnp.where(s == 0, XB + 4, 0) + core)
    remote(feat.at[0:BLK], xbuf.at[passed_rows], across, UNITS * 12 + 4 + core).wait_recv()
    passed = go(remote(xbuf.at[passed_rows], xbuf.at[passed_rows], partner, UNITS * 12 + 6))

    for b in range(3):
        x_at = XB + jnp.where(s == 0, 0, 2)
        g_at = BASE + jnp.where(s == 0, k, 2 - k)
        tap(nears[b][0], rows_from(x_at, 2), ext[b, rows_from(g_at, 2), :])
        send(nears[b], 0)

    for unit in mids:
        forward(unit)
    settle(smalls, 0)
    passed.wait_recv()
    for b in range(3):
        for n in range(2):
            @pl.when(core == n)
            def _(n=n, b=b):
                x_at = jnp.where(s == 0, XB + 2 + n, 0)
                g_at = BASE + jnp.where(s == 0, 0, n)
                tap(fars[b][0], rows_from(x_at, 4 - n), ext[b, rows_from(g_at, 4 - n), :])
        send(fars[b], 0)

    settle(smalls, 1)
    for unit in outers:
        forward(unit)
    settle(smalls, 2)

    eout[core, cx, cz, cy] = fin[9].astype(BF)
    everything = slice(None)

    def gather(axis, at):
        view = eout.at[(core,) + at]
        return [remote(view, view, peer(axis, d)) for d in (2, 1, 3)]

    gathers = [gather("z", (cx, cz, cy)), gather("y", (cx, everything, cy)), gather("x", (cx, everything, everything))]

    def gather_next(n):
        for copy in gathers[n - 1] if n else ():
            copy.wait_recv()
        for copy in gathers[n] if n < 3 else ():
            go(copy)

    gather_next(0)
    for unit in mids:
        settle(unit, 0)
    small_step(1)
    gather_next(1)
    for unit in outers:
        settle(unit, 0)
    gather_next(2)
    for unit in mids:
        settle(unit, 1)
    small_step(2)
    for unit in outers:
        settle(unit, 1)
    gather_next(3)
    e_swap = go(remote(eout.at[core], eout.at[core], partner))
    for unit in mids:
        settle(unit, 2)
    for unit in outers:
        settle(unit, 2)

    give = pl.ds(pl.multiple_of((1 - core) * 8, 8), 8)
    keep = pl.ds(pl.multiple_of(core * 8, 8), 8)
    swap[0] = fin[0:9, give, :]
    f_swap = go(remote(swap.at[0], swap.at[1], partner))
    small_step(3)

    e_swap.wait_recv()
    f_swap.wait_recv()
    for u in range(9):
        at = u + 3 if u < 3 else u - 3 if u < 6 else u
        o_atr[core, at] = fin[u, keep, :]
        o_atr[1 - core, at] = swap[1, u]

    crossing(lambda g, t, m: cross_copy(t, g).wait_send())

    @pl.when(core == 1 - s)
    def _():
        for j in range(2):
            halo(j).wait_send()

    @pl.when(core == 1)
    def _():
        raw_copy.wait_send()

    @pl.when(core == 0)
    def _():
        j_copies[1].wait_send()

    @pl.when(core == 1)
    def _():
        for copy in (j_copies[0], j_copies[2], p_copies[0], p_copies[1]):
            copy.wait_send()

    for copy in sends:
        copy.wait_send()
    assert counter[0] <= COPIES


COPIES = 180
UNITS = 10


def widen(scale, shares, small, tiny, o_atr, o_one, o_proj, o_cls, o_loss):
    o_atr[...] = shares[...]
    o_proj[...] = small[0, 0:768].astype(F32)
    o_one[...] = small[1].astype(F32)
    o_cls[...] = tiny[0:3]
    o_loss[...] = tiny[3:4, 0:1] * scale


def on_device(features, labels, w_one, w_atrous, w_proj, w_class):
    total_pix = lax.axis_size("dp") * lax.axis_size("space") * OWN
    vmem = pl.BlockSpec(memory_space=pltpu.VMEM)
    hbm = pl.BlockSpec(memory_space=pl.ANY)
    scratch = [
        ((8 * BLK, 1024), BF),
        ((3, 3, 1024, 256), BF),
        ((2, 3, 1024, 256), BF),
        ((1024, 256), BF),
        ((4, 3, BLK, 256), F32),
        ((CHIP, 256), F32),
        ((CHIP, 256), F32),
        ((2, 3, BLK, 256), BF),
        ((3, BLK, 256), BF),
        ((3, CHIP, 256), BF),
        ((CHIP, 256), BF),
        ((3, 6 * BLK, 256), BF),
        ((CHIP, 256), BF),
        ((CHIP, 256), BF),
        ((BLK, 256), BF),
        ((UNITS, 4, 4, 4, 16, 256), BF),
        ((UNITS, 3, 4, 4, 16, 256), BF),
        ((UNITS, 4, 4, 16, 256), BF),
        ((UNITS, 3, 4, 16, 256), BF),
        ((UNITS, 4, 16, 256), F32),
        ((UNITS, 3, 16, 256), F32),
        ((UNITS, 16, 256), F32),
        ((2, 4, 4, 16, 256), BF),
        ((4, 4, 16, 256), F32),
        ((2, 9, 8, 256), F32),
        ((1, OWN), jnp.int32),
    ]
    shares, small, tiny = pl.pallas_call(
        lambda *refs: kernel(1.0 / math.sqrt(total_pix), *refs),
        out_shape=(
            jax.ShapeDtypeStruct((2, 9, 8, 256), F32),
            jax.ShapeDtypeStruct((2, 4, 4, 4, 16, 256), BF),
            jax.ShapeDtypeStruct((16, 256), F32),
        ),
        in_specs=[hbm, vmem, hbm, hbm, vmem, vmem],
        out_specs=(vmem, vmem, vmem),
        scratch_shapes=[pltpu.VMEM(shape, kind) for shape, kind in scratch]
        + [
            pltpu.SemaphoreType.DMA((7,)),
            pltpu.SemaphoreType.DMA((COPIES,)),
            pltpu.SemaphoreType.DMA((COPIES,)),
        ],
        compiler_params=pltpu.CompilerParams(
            collective_id=0, has_side_effects=True, vmem_limit_bytes=60 * 1024 * 1024
        ),
        name="aspp",
    )(
        features.reshape(OWN, 1024),
        labels.transpose(1, 0, 2),
        w_one,
        w_atrous,
        w_proj.reshape(3, 256, 256),
        w_class.T,
    )
    grad_atrous, grad_one, grad_proj, grad_class, loss = pl.pallas_call(
        lambda *refs: widen(1.0 / total_pix, *refs),
        out_shape=(
            jax.ShapeDtypeStruct((2, 9, 8, 256), F32),
            jax.ShapeDtypeStruct((1024, 256), F32),
            jax.ShapeDtypeStruct((768, 256), F32),
            jax.ShapeDtypeStruct((3, 256), F32),
            jax.ShapeDtypeStruct((1, 1), F32),
        ),
        in_specs=[vmem] * 3,
        out_specs=(vmem,) * 5,
        name="widen",
    )(shares, small.reshape(2, 1024, 256), tiny)
    return (grad_atrous.reshape(2, 3, 3, 8, 256), grad_one, grad_proj, grad_class.T, loss.reshape(()))


def solution(mesh):
    return jax.shard_map(
        on_device,
        mesh=mesh,
        in_specs=(P("dp", "space", None, None), P("dp", "space", None), P(), P(), P(), P()),
        out_specs=(P(None, None, None, ("dp", "space"), None), P(), P(), P(), P()),
        check_vma=False,
    )
```

```python
import math

import jax
import jax.numpy as jnp
from jax import lax
from jax.experimental import pallas as pl
from jax.experimental.pallas import tpu as pltpu
from jax.sharding import PartitionSpec as P

MESH = pl.DeviceIdType.MESH
BF = jnp.bfloat16
F32 = jnp.float32
WIDTH = 56
BLK = 6 * WIDTH
OWN = 12 * WIDTH
CHIP = 24 * WIDTH
BASE = 1
XB = 2
ORDER = ("xzy", "zyx", "yxz")
SMALL = "yzx"
AXES = "xzy"


def slope(pre):
    gate = jax.nn.sigmoid(pre)
    return gate * (1.0 + pre * (1.0 - gate))


def silu(pre):
    return pre * jax.nn.sigmoid(pre)


def mm(first, second):
    return jnp.dot(first, second, preferred_element_type=F32)


def mm_t(first, second):
    return lax.dot_general(first, second, (((1,), (1,)), ((), ())), preferred_element_type=F32)


def t_mm(first, second):
    return lax.dot_general(first, second, (((0,), (0,)), ((), ())), preferred_element_type=F32)


def kernel(
    loss_scale,
    feat, labels, w_one_h, w_atr_h, w_proj, w_cls,
    o_atr, eout, o_cls,
    xbuf, wbuf, wtow, wone, tacc, pre, pre0, cs, cr, joined, dh, ext, db0, raw, hraw,
    s1, r1, s2, r2, s3, r3, fin, pbuf, clbuf, swap, lab,
    lsem, ssem, rsem,
):
    dp = lax.axis_index("dp")
    sp = lax.axis_index("space")
    core, s = sp % 2, sp // 2
    cx, cz, cy = dp // 8, (dp // 2) % 4, (dp % 2) * 2 + s
    here = {"x": cx, "z": cz, "y": cy}

    def place(x, z, y, c):
        return (x * 8 + z * 2 + y // 2, (y % 2) * 2 + c)

    partner = place(cx, cz, cy, 1 - core)
    across = (dp, (1 - s) * 2 + core)
    beyond = (dp, (1 - s) * 2 + 1 - core)

    def peer(axis, d):
        at = dict(here)
        at[axis] = (at[axis] + d) % 4
        return place(at["x"], at["z"], at["y"], core)

    rate = 12 + 6 * core
    k = 2 + core

    counter = [UNITS * 12 + 17]

    def remote(src, dst, to, i=None, sent=None):
        if i is None:
            i = counter[0]
            counter[0] += 1
        return pltpu.make_async_remote_copy(
            src_ref=src, dst_ref=dst, send_sem=ssem.at[i if sent is None else sent], recv_sem=rsem.at[i], device_id=to, device_id_type=MESH
        )

    sends = []

    def go(copy):
        copy.start()
        sends.append(copy)
        return copy

    own_rows = pl.ds(pl.multiple_of(core * OWN, 16), OWN)
    other_rows = pl.ds(pl.multiple_of((1 - core) * OWN, 16), OWN)
    x_own = pl.ds(pl.multiple_of(XB * BLK + core * OWN, 16), OWN)
    x_local = pltpu.make_async_copy(feat, xbuf.at[x_own], lsem.at[0])
    x_local.start()
    w_local = [pltpu.make_async_copy(w_atr_h.at[core, a], wbuf.at[a], lsem.at[1 + a]) for a in range(3)]
    cross_tap = s * 2
    tow_local = [pltpu.make_async_copy(w_atr_h.at[g, cross_tap], wtow.at[g], lsem.at[5 + g]) for g in range(2)]
    for copy in (tow_local[1], tow_local[0], w_local[1], w_local[0], w_local[2]):
        copy.start()
    one_local = pltpu.make_async_copy(w_one_h, wone, lsem.at[4])
    one_local.start()

    barrier = pltpu.get_barrier_semaphore()
    greet = [partner, beyond] + [peer(axis, d) for axis in AXES for d in (1, 2, 3)]
    for other in greet:
        pl.semaphore_signal(barrier, inc=1, device_id=other, device_id_type=MESH)

    tacc[...] = jnp.zeros_like(tacc)

    column = lax.rem(lax.broadcasted_iota(jnp.int32, (BLK, 256), 0), WIDTH)

    def from_left(value, rate=rate):
        return jnp.where(column >= rate, pltpu.roll(value, rate, 0), 0.0)

    def from_right(value, rate=rate):
        return jnp.where(column < WIDTH - rate, pltpu.roll(value, BLK - rate, 0), 0.0)

    def block(m):
        return pl.ds(pl.multiple_of(m * BLK, 16), BLK)

    def middle(m):
        rows = xbuf[block(XB + m), :]
        for b in range(3):
            tacc[m, b] += mm(rows, wbuf[1, b])

    def outer(m):
        for a in (0, 2):
            to = m - (a - 1) * k

            @pl.when((to >= 0) & (to < 4))
            def _(a=a, to=to):
                rows = xbuf[block(XB + m), :]
                for b in range(3):
                    tacc[to, b] += mm(rows, wbuf[a, b])

    def cross_copy(t, g=None):
        if g is None:
            return remote(cs.at[0, t], cr.at[t], across, UNITS * 12 + t)
        to = (dp, (1 - s) * 2 + g)
        return remote(cs.at[g, t], cr.at[t], to, UNITS * 12 + t, UNITS * 12 + 7 + 3 * g + t)

    def crossing(body):
        for g, t in ((1, 0), (1, 1), (1, 2), (0, 0), (0, 1)):
            m = jnp.where(s == 0, 2 - g + t, t)

            @pl.when(m // 2 == core)
            def _(g=g, t=t, m=m):
                body(g, t, m)

    def cross(g, t, m):
        rows = xbuf[block(XB + m), :]
        parts = [mm(rows, wtow[g, b]) for b in range(3)]
        shifted = from_left(parts[0], 12 + 6 * g) + from_right(parts[2], 12 + 6 * g)
        cs[g, t] = (parts[1] + shifted).astype(BF)

    mine, theirs = 2 * core, 2 * (1 - core)
    x_local.wait()
    for copy in tow_local:
        copy.wait()
    crossing(cross)
    pl.semaphore_wait(barrier, len(greet))
    crossing(lambda g, t, m: cross_copy(t, g).start())
    x_swap = go(remote(feat, xbuf.at[x_own], partner))
    for copy in (w_local[1], w_local[0], w_local[2]):
        copy.wait()
    pl.loop(0, 2)(lambda q: middle(mine + q))
    pl.loop(0, 2)(lambda q: outer(mine + q))
    x_swap.wait_recv()

    @pl.loop(0, 2)
    def _(q):
        middle(theirs + q)
        outer(theirs + q)

    def halo(j, h):
        rows = block(XB + jnp.where(s == 0, 2, 0) + j)
        to = block(jnp.where(s == 0, j, XB + 4 + j))
        lanes = slice(h * 512, h * 512 + 512)
        i = UNITS * 12 + 4 + h
        return remote(xbuf.at[rows, lanes], xbuf.at[to, lanes], (dp, (1 - s) * 2 + j), i, UNITS * 12 + 13 + 2 * j + h)

    def haloes(body):
        @pl.when(core == s)
        def _():
            for j, h in ((0, 0), (0, 1), (1, 0)):
                body(halo(j, h))

        @pl.when(core == 1 - s)
        def _():
            body(halo(1, 1))

    haloes(lambda copy: copy.start())

    @pl.loop(0, 4)
    def _(i):
        pre[block(i), :] = tacc[i, 1] + from_left(tacc[i, 0]) + from_right(tacc[i, 2])

    one_local.wait()

    @pl.when(core == 1)
    def _():
        @pl.loop(0, 4)
        def _(i):
            value = mm(xbuf[block(XB + i), :], wone[...])
            pre0[block(i), :] = value
            joined[0, block(i), :] = silu(value).astype(BF)

    for t in range(3):
        @pl.when(t < k)
        def _(t=t):
            cross_copy(t).wait_recv()
            into = block(jnp.where(s == 0, 4 - k + t, t))
            pre[into, :] += cr[t].astype(F32)

    @pl.loop(0, 4)
    def _(i):
        joined[1 + core, block(i), :] = silu(pre[block(i), :]).astype(BF)

    j_copies = [remote(joined.at[b, other_rows], joined.at[b, other_rows], partner) for b in range(3)]

    @pl.when(core == 0)
    def _():
        j_copies[1].start()

    @pl.when(core == 1)
    def _():
        j_copies[0].start()
        j_copies[2].start()

    @pl.when(core == 0)
    def _():
        j_copies[0].wait_recv()
        j_copies[2].wait_recv()

    @pl.when(core == 1)
    def _():
        j_copies[1].wait_recv()

    pre_hidden = mm(joined[0, own_rows, :], w_proj[0])
    pre_hidden += mm(joined[1, own_rows, :], w_proj[1])
    pre_hidden += mm(joined[2, own_rows, :], w_proj[2])
    hidden = silu(pre_hidden).astype(BF)
    classes = jnp.concatenate([w_cls[...].astype(F32), jnp.zeros((13, 256), F32)]).astype(BF)
    for y in range(12):
        lab[:, y * WIDTH : (y + 1) * WIDTH] = labels[y]
    logits = mm_t(classes, hidden)
    row = lax.broadcasted_iota(jnp.int32, logits.shape, 0)
    valid = row < 3
    top = jnp.max(jnp.where(valid, logits, -jnp.inf), axis=0, keepdims=True)
    total = jnp.sum(jnp.where(valid, jnp.exp(logits - top), 0.0), axis=0, keepdims=True)
    lse = top + jnp.log(total)
    onehot = row == lab[...]
    loss = jnp.sum(lse - jnp.sum(jnp.where(onehot, logits, 0.0), axis=0, keepdims=True), axis=1, keepdims=True)
    probs = jnp.exp(logits - lse) - jnp.where(onehot, 1.0, 0.0)
    dlogits = jnp.where(valid, probs * loss_scale, 0.0).astype(BF)
    dhidden = t_mm(dlogits, classes) * slope(pre_hidden)
    dh[own_rows, :] = dhidden.astype(BF)
    dh_copy = go(remote(dh.at[own_rows], dh.at[own_rows], partner))

    small = mm(dlogits, hidden)
    srow = lax.broadcasted_iota(jnp.int32, small.shape, 0)
    cl_copies = []
    for n, axis in enumerate(AXES):
        cl_copies.append([remote(clbuf.at[n, here[axis]], clbuf.at[n, here[axis]], peer(axis, d)) for d in (1, 2, 3)])
    cl_copies.append([remote(clbuf.at[3, core], clbuf.at[3, core], partner)])
    clbuf[0, here["x"]] = jnp.where(srow == 3, loss, small)
    for copy in cl_copies[0]:
        go(copy)

    def small_step(n):
        for copy in cl_copies[n]:
            copy.wait_recv()
        value = clbuf[n, 0] + clbuf[n, 1]
        if n < 3:
            value = value + clbuf[n, 2] + clbuf[n, 3]
            clbuf[n + 1, core if n == 2 else here[AXES[n + 1]]] = value
            for copy in cl_copies[n + 1]:
                go(copy)
        else:
            o_cls[...] = value

    branch_w = w_proj[1 + core]

    raw_copy = remote(raw.at[block(jnp.where(s == 0, 3, 0))], hraw, across, UNITS * 12 + 3)

    def branch_grad(i):
        value = mm_t(dh[block(i), :], branch_w) * slope(pre[block(i), :])
        raw[block(i), :] = value.astype(BF)

        @pl.when((core == 1) & (i == jnp.where(s == 0, 3, 0)))
        def _():
            raw_copy.start()

        to = block(BASE + i)
        rounded = value.astype(BF).astype(F32)
        ext[0, to, :] = from_right(rounded).astype(BF)
        ext[1, to, :] = rounded.astype(BF)
        ext[2, to, :] = from_left(rounded).astype(BF)

    def first_grad(first):
        @pl.when(core == 1)
        def _():
            @pl.loop(0, 2)
            def _(q):
                rows = block(first + q)
                db0[rows, :] = (mm_t(dh[rows, :], w_proj[0]) * slope(pre0[rows, :])).astype(BF)

    pl.loop(0, 2)(lambda q: branch_grad(mine + q))
    first_grad(mine)
    dh_copy.wait_recv()
    pl.loop(0, 2)(lambda q: branch_grad(theirs + q))

    low, high = pl.ds(0, 2), pl.ds(2, 2)

    def plan(u, order, ring):
        out = []
        for phase, (buf, landing) in enumerate(((s1, r1), (s2, r2), (s3, r3))):
            axis = order[phase]
            left = [a for a in AXES if a in order[phase:]]
            spot = left.index(axis)
            c = here[axis]
            base = u * 12 + (0, 6, 9)[phase]

            def chunk(at, half=None):
                index = [u] + [slice(None)] * len(left)
                index[1 + spot] = (at + 4) % 4
                if half is not None:
                    index[2 if spot == 0 else 1] = half
                return buf.at[tuple(index)]

            def land(slot, half=None):
                return landing.at[u, slot] if half is None else landing.at[u, slot, half]

            if phase or not ring:
                copies = [remote(chunk(c + d), land(d - 1), peer(axis, d), base + d - 1) for d in (2, 1, 3)]
                out.append((chunk(c), [land(n) for n in range(3)], copies, (), (), ()))
                continue
            up, down = peer(axis, 1), peer(axis, 3)
            way = [
                remote(chunk(c + 2, low), land(2, low), up, base),
                remote(chunk(c + 2, high), land(2, high), down, base + 1),
            ]
            copies = [
                remote(chunk(c + 1, high), land(0, high), up, base + 2),
                remote(chunk(c - 1, low), land(1, low), down, base + 3),
            ]
            later = [
                remote(chunk(c + 1, low), land(0, low), up, base + 4),
                remote(chunk(c - 1, high), land(1, high), down, base + 5),
            ]
            sums = [(chunk(c + 1, low), land(2, low)), (chunk(c - 1, high), land(2, high))]
            out.append((chunk(c), [land(0), land(1)], copies, way, later, sums))
        return u, out

    def send(unit, phase):
        _, _, copies, way, _, _ = unit[1][phase]
        for copy in list(way) + copies:
            go(copy)

    def forward(unit):
        _, _, _, way, later, sums = unit[1][0]
        for n in range(2):
            way[n].wait_recv()
            out, got = sums[n]
            out[...] = (out[...].astype(F32) + got[...].astype(F32)).astype(BF)
            go(later[n])

    def settle(unit, phase):
        u, phases = unit
        own, lands, copies, _, later, _ = phases[phase]
        for copy in copies + list(later):
            copy.wait_recv()
        value = own[...].astype(F32)
        for got in lands:
            value = value + got[...].astype(F32)
        if phase < 2:
            into = (s2, s3)[phase]
            into[u] = value.astype(into.dtype)
            send(unit, phase + 1)
        else:
            fin[u] = value

    mids = [plan(b, ORDER[b], True) for b in range(3)]
    nears = [plan(3 + 3 * s + b, ORDER[b], True) for b in range(3)]
    fars = [plan(3 + 3 * (1 - s) + b, ORDER[b], True) for b in range(3)]
    smalls = plan(9, SMALL, False)

    def proj_grad(b):
        return t_mm(joined[b], dh[...]).astype(BF).reshape(4, 4, 16, 256)

    p_copies = [remote(pbuf.at[n], s1.at[9, 2 * n], partner) for n in range(2)]

    def tap(u, rows, grad):
        for c in range(4):
            value = t_mm(xbuf[rows, c * 256 : (c + 1) * 256], grad)
            s1[u, c] = value.astype(BF).reshape(4, 4, 16, 256)

    everyone = pl.ds(XB * BLK, CHIP)

    first_grad(theirs)

    @pl.when(core == 1)
    def _():
        for n in range(2):
            pbuf[n] = proj_grad(2 * n)
            p_copies[n].start()

        tap(9, everyone, db0[...])

    @pl.when(core == 0)
    def _():
        s1[9, 1] = proj_grad(1)
        s1[9, 3] = jnp.zeros((4, 4, 16, 256), BF)
        for n in range(2):
            p_copies[n].wait_recv()

    send(smalls, 0)

    def rows_from(m, count):
        return pl.ds(pl.multiple_of(m * BLK, 16), count * BLK)

    for b in range(3):
        tap(b, everyone, ext[b, rows_from(BASE, 4), :])
        send(mids[b], 0)
    passed_rows = block(jnp.where(s == 0, XB + 4, 0) + core)
    for h in range(2):
        lanes = slice(h * 512, h * 512 + 512)
        remote(xbuf.at[passed_rows, lanes], xbuf.at[passed_rows, lanes], across, UNITS * 12 + 4 + h).wait_recv()
    passed = go(remote(xbuf.at[passed_rows], xbuf.at[passed_rows], partner, UNITS * 12 + 6))

    small_step(0)

    @pl.when(core == 1)
    def _():
        raw_copy.wait_recv()
        to = block(jnp.where(s == 0, BASE + 4, BASE - 1))
        value = hraw[...].astype(F32)
        ext[0, to, :] = from_right(value).astype(BF)
        ext[1, to, :] = hraw[...]
        ext[2, to, :] = from_left(value).astype(BF)

    for b in range(3):
        x_at = XB + jnp.where(s == 0, 0, 2)
        g_at = BASE + jnp.where(s == 0, k, 2 - k)
        tap(nears[b][0], rows_from(x_at, 2), ext[b, rows_from(g_at, 2), :])
        send(nears[b], 0)

    passed.wait_recv()
    for b in range(3):
        for n in range(2):
            @pl.when(core == n)
            def _(n=n, b=b):
                x_at = jnp.where(s == 0, XB + 2 + n, 0)
                g_at = BASE + jnp.where(s == 0, 0, n)
                tap(fars[b][0], rows_from(x_at, 4 - n), ext[b, rows_from(g_at, 4 - n), :])
        send(fars[b], 0)

    for unit in mids:
        forward(unit)
    settle(smalls, 0)
    for unit in nears:
        forward(unit)
    for unit in mids:
        settle(unit, 0)
    settle(smalls, 1)
    for unit in fars:
        forward(unit)
    small_step(1)
    for unit in nears:
        settle(unit, 0)
    settle(smalls, 2)

    eout[core, cx, cz, cy] = fin[9].astype(BF)
    everything = slice(None)

    def gather(axis, at):
        view = eout.at[(core,) + at]
        return [remote(view, view, peer(axis, d)) for d in (2, 1, 3)]

    gathers = [gather("z", (cx, cz, cy)), gather("y", (cx, everything, cy)), gather("x", (cx, everything, everything))]

    def gather_next(n):
        for copy in gathers[n - 1] if n else ():
            copy.wait_recv()
        for copy in gathers[n] if n < 3 else ():
            go(copy)

    gather_next(0)
    for unit in mids:
        settle(unit, 1)
    for unit in fars:
        settle(unit, 0)
    gather_next(1)
    small_step(2)
    for unit in mids:
        settle(unit, 2)
    for unit in nears:
        settle(unit, 1)
    for unit in fars:
        settle(unit, 1)
    gather_next(2)
    small_step(3)
    for unit in nears:
        settle(unit, 2)
    for unit in fars:
        settle(unit, 2)

    give = pl.ds(pl.multiple_of((1 - core) * 8, 8), 8)
    keep = pl.ds(pl.multiple_of(core * 8, 8), 8)
    swap[0] = fin[0:9, give, :]
    f_swap = go(remote(swap.at[0], swap.at[1], partner))
    gather_next(3)
    e_swap = go(remote(eout.at[core], eout.at[core], partner))

    e_swap.wait_recv()
    f_swap.wait_recv()
    for u in range(9):
        at = u + 3 if u < 3 else u - 3 if u < 6 else u
        o_atr[core, at] = fin[u, keep, :]
        o_atr[1 - core, at] = swap[1, u]

    crossing(lambda g, t, m: cross_copy(t, g).wait_send())

    haloes(lambda copy: copy.wait_send())

    @pl.when(core == 1)
    def _():
        raw_copy.wait_send()

    @pl.when(core == 0)
    def _():
        j_copies[1].wait_send()

    @pl.when(core == 1)
    def _():
        for copy in (j_copies[0], j_copies[2], p_copies[0], p_copies[1]):
            copy.wait_send()

    for copy in sends:
        copy.wait_send()
    assert counter[0] <= COPIES


COPIES = 180
UNITS = 10


def widen(scale, shares, small, tiny, o_atr, o_one, o_proj, o_cls, o_loss):
    o_atr[...] = shares[...]
    o_proj[...] = small[0, 0:768].astype(F32)
    o_one[...] = small[1].astype(F32)
    o_cls[...] = tiny[0:3]
    o_loss[...] = tiny[3:4, 0:1] * scale


def on_device(features, labels, w_one, w_atrous, w_proj, w_class):
    total_pix = lax.axis_size("dp") * lax.axis_size("space") * OWN
    vmem = pl.BlockSpec(memory_space=pltpu.VMEM)
    hbm = pl.BlockSpec(memory_space=pl.ANY)
    scratch = [
        ((8 * BLK, 1024), BF),
        ((3, 3, 1024, 256), BF),
        ((2, 3, 1024, 256), BF),
        ((1024, 256), BF),
        ((4, 3, BLK, 256), F32),
        ((CHIP, 256), F32),
        ((CHIP, 256), F32),
        ((2, 3, BLK, 256), BF),
        ((3, BLK, 256), BF),
        ((3, CHIP, 256), BF),
        ((CHIP, 256), BF),
        ((3, 6 * BLK, 256), BF),
        ((CHIP, 256), BF),
        ((CHIP, 256), BF),
        ((BLK, 256), BF),
        ((UNITS, 4, 4, 4, 16, 256), BF),
        ((UNITS, 3, 4, 4, 16, 256), BF),
        ((UNITS, 4, 4, 16, 256), BF),
        ((UNITS, 3, 4, 16, 256), BF),
        ((UNITS, 4, 16, 256), F32),
        ((UNITS, 3, 16, 256), F32),
        ((UNITS, 16, 256), F32),
        ((2, 4, 4, 16, 256), BF),
        ((4, 4, 16, 256), F32),
        ((2, 9, 8, 256), F32),
        ((1, OWN), jnp.int32),
    ]
    shares, small, tiny = pl.pallas_call(
        lambda *refs: kernel(1.0 / math.sqrt(total_pix), *refs),
        out_shape=(
            jax.ShapeDtypeStruct((2, 9, 8, 256), F32),
            jax.ShapeDtypeStruct((2, 4, 4, 4, 16, 256), BF),
            jax.ShapeDtypeStruct((16, 256), F32),
        ),
        in_specs=[hbm, vmem, hbm, hbm, vmem, vmem],
        out_specs=(vmem, vmem, vmem),
        scratch_shapes=[pltpu.VMEM(shape, kind) for shape, kind in scratch]
        + [
            pltpu.SemaphoreType.DMA((7,)),
            pltpu.SemaphoreType.DMA((COPIES,)),
            pltpu.SemaphoreType.DMA((COPIES,)),
        ],
        compiler_params=pltpu.CompilerParams(
            collective_id=0, has_side_effects=True, vmem_limit_bytes=60 * 1024 * 1024
        ),
        name="aspp",
    )(
        features.reshape(OWN, 1024),
        labels.transpose(1, 0, 2),
        w_one,
        w_atrous,
        w_proj.reshape(3, 256, 256),
        w_class.T,
    )
    grad_atrous, grad_one, grad_proj, grad_class, loss = pl.pallas_call(
        lambda *refs: widen(1.0 / total_pix, *refs),
        out_shape=(
            jax.ShapeDtypeStruct((2, 9, 8, 256), F32),
            jax.ShapeDtypeStruct((1024, 256), F32),
            jax.ShapeDtypeStruct((768, 256), F32),
            jax.ShapeDtypeStruct((3, 256), F32),
            jax.ShapeDtypeStruct((1, 1), F32),
        ),
        in_specs=[vmem] * 3,
        out_specs=(vmem,) * 5,
        name="widen",
    )(shares, small.reshape(2, 1024, 256), tiny)
    return (grad_atrous.reshape(2, 3, 3, 8, 256), grad_one, grad_proj, grad_class.T, loss.reshape(()))


def solution(mesh):
    return jax.shard_map(
        on_device,
        mesh=mesh,
        in_specs=(P("dp", "space", None, None), P("dp", "space", None), P(), P(), P(), P()),
        out_specs=(P(None, None, None, ("dp", "space"), None), P(), P(), P(), P()),
        check_vma=False,
    )
```

```python
import math

import jax
import jax.numpy as jnp
from jax import lax
from jax.experimental import pallas as pl
from jax.experimental.pallas import tpu as pltpu
from jax.sharding import PartitionSpec as P

MESH = pl.DeviceIdType.MESH
BF = jnp.bfloat16
F32 = jnp.float32
WIDTH = 56
BLK = 6 * WIDTH
OWN = 12 * WIDTH
CHIP = 24 * WIDTH
BASE = 1
XB = 2
MIDDLE = ("xzy", "zyx", "zxy")
OUTER = ("xzy", "zyx", "yxz")
SMALL = "xyz"
AXES = "xzy"


def slope(pre):
    gate = jax.nn.sigmoid(pre)
    return gate * (1.0 + pre * (1.0 - gate))


def silu(pre):
    return pre * jax.nn.sigmoid(pre)


def mm(first, second):
    return jnp.dot(first, second, preferred_element_type=F32)


def mm_t(first, second):
    return lax.dot_general(first, second, (((1,), (1,)), ((), ())), preferred_element_type=F32)


def t_mm(first, second):
    return lax.dot_general(first, second, (((0,), (0,)), ((), ())), preferred_element_type=F32)


def kernel(
    loss_scale,
    feat, labels, w_one_h, w_atr_h, w_proj, w_cls,
    o_atr, eout, o_cls,
    xbuf, wbuf, wtow, wone, tacc, pre, pre0, cs, cr, joined, dh, ext, db0, raw, hraw,
    s1, r1, s2, r2, s3, r3, fin, pbuf, clbuf, swap, lab,
    lsem, ssem, rsem,
):
    dp = lax.axis_index("dp")
    sp = lax.axis_index("space")
    core, s = sp % 2, sp // 2
    cx, cz, cy = dp // 8, (dp // 2) % 4, (dp % 2) * 2 + s
    here = {"x": cx, "z": cz, "y": cy}

    def place(x, z, y, c):
        return (x * 8 + z * 2 + y // 2, (y % 2) * 2 + c)

    partner = place(cx, cz, cy, 1 - core)
    across = (dp, (1 - s) * 2 + core)
    beyond = (dp, (1 - s) * 2 + 1 - core)

    def peer(axis, d):
        at = dict(here)
        at[axis] = (at[axis] + d) % 4
        return place(at["x"], at["z"], at["y"], core)

    rate = 12 + 6 * core
    k = 2 + core

    counter = [UNITS * 12 + 17]

    def remote(src, dst, to, i=None, sent=None):
        if i is None:
            i = counter[0]
            counter[0] += 1
        return pltpu.make_async_remote_copy(
            src_ref=src, dst_ref=dst, send_sem=ssem.at[i if sent is None else sent], recv_sem=rsem.at[i], device_id=to, device_id_type=MESH
        )

    sends = []

    def go(copy):
        copy.start()
        sends.append(copy)
        return copy

    own_rows = pl.ds(pl.multiple_of(core * OWN, 16), OWN)
    other_rows = pl.ds(pl.multiple_of((1 - core) * OWN, 16), OWN)
    x_own = pl.ds(pl.multiple_of(XB * BLK + core * OWN, 16), OWN)
    x_local = pltpu.make_async_copy(feat, xbuf.at[x_own], lsem.at[0])
    x_local.start()
    w_local = [pltpu.make_async_copy(w_atr_h.at[core, a], wbuf.at[a], lsem.at[1 + a]) for a in range(3)]
    cross_tap = s * 2
    tow_local = [pltpu.make_async_copy(w_atr_h.at[g, cross_tap], wtow.at[g], lsem.at[5 + g]) for g in range(2)]
    for copy in (tow_local[1], tow_local[0], w_local[1], w_local[0], w_local[2]):
        copy.start()
    one_local = pltpu.make_async_copy(w_one_h, wone, lsem.at[4])
    one_local.start()

    barrier = pltpu.get_barrier_semaphore()
    greet = [partner, beyond] + [peer(axis, d) for axis in AXES for d in (1, 2, 3)]
    for other in greet:
        pl.semaphore_signal(barrier, inc=1, device_id=other, device_id_type=MESH)

    tacc[...] = jnp.zeros_like(tacc)

    column = lax.rem(lax.broadcasted_iota(jnp.int32, (BLK, 256), 0), WIDTH)

    def from_left(value, rate=rate):
        return jnp.where(column >= rate, pltpu.roll(value, rate, 0), 0.0)

    def from_right(value, rate=rate):
        return jnp.where(column < WIDTH - rate, pltpu.roll(value, BLK - rate, 0), 0.0)

    def block(m):
        return pl.ds(pl.multiple_of(m * BLK, 16), BLK)

    def middle(m):
        rows = xbuf[block(XB + m), :]
        for b in range(3):
            tacc[m, b] += mm(rows, wbuf[1, b])

    def outer(m):
        for a in (0, 2):
            to = m - (a - 1) * k

            @pl.when((to >= 0) & (to < 4))
            def _(a=a, to=to):
                rows = xbuf[block(XB + m), :]
                for b in range(3):
                    tacc[to, b] += mm(rows, wbuf[a, b])

    def cross_copy(t, g=None):
        if g is None:
            return remote(cs.at[0, t], cr.at[t], across, UNITS * 12 + t)
        to = (dp, (1 - s) * 2 + g)
        return remote(cs.at[g, t], cr.at[t], to, UNITS * 12 + t, UNITS * 12 + 7 + 3 * g + t)

    def crossing(body):
        for g, t in ((1, 0), (1, 1), (1, 2), (0, 0), (0, 1)):
            m = jnp.where(s == 0, 2 - g + t, t)

            @pl.when(m // 2 == core)
            def _(g=g, t=t, m=m):
                body(g, t, m)

    def cross(g, t, m):
        rows = xbuf[block(XB + m), :]
        parts = [mm(rows, wtow[g, b]) for b in range(3)]
        shifted = from_left(parts[0], 12 + 6 * g) + from_right(parts[2], 12 + 6 * g)
        cs[g, t] = (parts[1] + shifted).astype(BF)

    mine, theirs = 2 * core, 2 * (1 - core)
    x_local.wait()
    for copy in tow_local:
        copy.wait()
    crossing(cross)
    pl.semaphore_wait(barrier, len(greet))
    crossing(lambda g, t, m: cross_copy(t, g).start())
    x_swap = go(remote(feat, xbuf.at[x_own], partner))
    for copy in (w_local[1], w_local[0], w_local[2]):
        copy.wait()
    pl.loop(0, 2)(lambda q: middle(mine + q))
    pl.loop(0, 2)(lambda q: outer(mine + q))
    x_swap.wait_recv()

    @pl.loop(0, 2)
    def _(q):
        middle(theirs + q)
        outer(theirs + q)

    def halo(j, h):
        rows = block(XB + jnp.where(s == 0, 2, 0) + j)
        to = block(jnp.where(s == 0, j, XB + 4 + j))
        lanes = slice(h * 512, h * 512 + 512)
        i = UNITS * 12 + 4 + h
        return remote(xbuf.at[rows, lanes], xbuf.at[to, lanes], (dp, (1 - s) * 2 + j), i, UNITS * 12 + 13 + 2 * j + h)

    def haloes(body):
        @pl.when(core == s)
        def _():
            for j, h in ((0, 0), (0, 1), (1, 0)):
                body(halo(j, h))

        @pl.when(core == 1 - s)
        def _():
            body(halo(1, 1))

    haloes(lambda copy: copy.start())

    @pl.loop(0, 4)
    def _(i):
        pre[block(i), :] = tacc[i, 1] + from_left(tacc[i, 0]) + from_right(tacc[i, 2])

    one_local.wait()

    @pl.when(core == 1)
    def _():
        @pl.loop(0, 4)
        def _(i):
            value = mm(xbuf[block(XB + i), :], wone[...])
            pre0[block(i), :] = value
            joined[0, block(i), :] = silu(value).astype(BF)

    for t in range(3):
        @pl.when(t < k)
        def _(t=t):
            cross_copy(t).wait_recv()
            into = block(jnp.where(s == 0, 4 - k + t, t))
            pre[into, :] += cr[t].astype(F32)

    @pl.loop(0, 4)
    def _(i):
        joined[1 + core, block(i), :] = silu(pre[block(i), :]).astype(BF)

    j_copies = [remote(joined.at[b, other_rows], joined.at[b, other_rows], partner) for b in range(3)]

    @pl.when(core == 0)
    def _():
        j_copies[1].start()

    @pl.when(core == 1)
    def _():
        j_copies[0].start()
        j_copies[2].start()

    @pl.when(core == 0)
    def _():
        j_copies[0].wait_recv()
        j_copies[2].wait_recv()

    @pl.when(core == 1)
    def _():
        j_copies[1].wait_recv()

    pre_hidden = mm(joined[0, own_rows, :], w_proj[0])
    pre_hidden += mm(joined[1, own_rows, :], w_proj[1])
    pre_hidden += mm(joined[2, own_rows, :], w_proj[2])
    hidden = silu(pre_hidden).astype(BF)
    classes = jnp.concatenate([w_cls[...].astype(F32), jnp.zeros((13, 256), F32)]).astype(BF)
    for y in range(12):
        lab[:, y * WIDTH : (y + 1) * WIDTH] = labels[y]
    logits = mm_t(classes, hidden)
    row = lax.broadcasted_iota(jnp.int32, logits.shape, 0)
    valid = row < 3
    top = jnp.max(jnp.where(valid, logits, -jnp.inf), axis=0, keepdims=True)
    total = jnp.sum(jnp.where(valid, jnp.exp(logits - top), 0.0), axis=0, keepdims=True)
    lse = top + jnp.log(total)
    onehot = row == lab[...]
    loss = jnp.sum(lse - jnp.sum(jnp.where(onehot, logits, 0.0), axis=0, keepdims=True), axis=1, keepdims=True)
    probs = jnp.exp(logits - lse) - jnp.where(onehot, 1.0, 0.0)
    dlogits = jnp.where(valid, probs * loss_scale, 0.0).astype(BF)
    dhidden = t_mm(dlogits, classes) * slope(pre_hidden)
    dh[own_rows, :] = dhidden.astype(BF)
    dh_copy = go(remote(dh.at[own_rows], dh.at[own_rows], partner))

    small = mm(dlogits, hidden)
    srow = lax.broadcasted_iota(jnp.int32, small.shape, 0)
    cl_copies = []
    for n, axis in enumerate(AXES):
        cl_copies.append([remote(clbuf.at[n, here[axis]], clbuf.at[n, here[axis]], peer(axis, d)) for d in (1, 2, 3)])
    cl_copies.append([remote(clbuf.at[3, core], clbuf.at[3, core], partner)])
    clbuf[0, here["x"]] = jnp.where(srow == 3, loss, small)
    for copy in cl_copies[0]:
        go(copy)

    def small_step(n):
        for copy in cl_copies[n]:
            copy.wait_recv()
        value = clbuf[n, 0] + clbuf[n, 1]
        if n < 3:
            value = value + clbuf[n, 2] + clbuf[n, 3]
            clbuf[n + 1, core if n == 2 else here[AXES[n + 1]]] = value
            for copy in cl_copies[n + 1]:
                go(copy)
        else:
            o_cls[...] = value

    branch_w = w_proj[1 + core]

    raw_copy = remote(raw.at[block(jnp.where(s == 0, 3, 0))], hraw, across, UNITS * 12 + 3)

    def branch_grad(i):
        value = mm_t(dh[block(i), :], branch_w) * slope(pre[block(i), :])
        raw[block(i), :] = value.astype(BF)

        @pl.when((core == 1) & (i == jnp.where(s == 0, 3, 0)))
        def _():
            raw_copy.start()

        to = block(BASE + i)
        rounded = value.astype(BF).astype(F32)
        ext[0, to, :] = from_right(rounded).astype(BF)
        ext[1, to, :] = rounded.astype(BF)
        ext[2, to, :] = from_left(rounded).astype(BF)

    def first_grad(first):
        @pl.when(core == 1)
        def _():
            @pl.loop(0, 2)
            def _(q):
                rows = block(first + q)
                db0[rows, :] = (mm_t(dh[rows, :], w_proj[0]) * slope(pre0[rows, :])).astype(BF)

    pl.loop(0, 2)(lambda q: branch_grad(mine + q))
    first_grad(mine)
    dh_copy.wait_recv()
    pl.loop(0, 2)(lambda q: branch_grad(theirs + q))

    low, high = pl.ds(0, 2), pl.ds(2, 2)

    def plan(u, order, ring):
        out = []
        for phase, (buf, landing) in enumerate(((s1, r1), (s2, r2), (s3, r3))):
            axis = order[phase]
            left = [a for a in AXES if a in order[phase:]]
            spot = left.index(axis)
            c = here[axis]
            base = u * 12 + (0, 6, 9)[phase]

            def chunk(at, half=None):
                index = [u] + [slice(None)] * len(left)
                index[1 + spot] = (at + 4) % 4
                if half is not None:
                    index[2 if spot == 0 else 1] = half
                return buf.at[tuple(index)]

            def land(slot, half=None):
                return landing.at[u, slot] if half is None else landing.at[u, slot, half]

            if phase or not ring:
                copies = [remote(chunk(c + d), land(d - 1), peer(axis, d), base + d - 1) for d in (2, 1, 3)]
                out.append((chunk(c), [land(n) for n in range(3)], copies, (), (), ()))
                continue
            up, down = peer(axis, 1), peer(axis, 3)
            way = [
                remote(chunk(c + 2, low), land(2, low), up, base),
                remote(chunk(c + 2, high), land(2, high), down, base + 1),
            ]
            copies = [
                remote(chunk(c + 1, high), land(0, high), up, base + 2),
                remote(chunk(c - 1, low), land(1, low), down, base + 3),
            ]
            later = [
                remote(chunk(c + 1, low), land(0, low), up, base + 4),
                remote(chunk(c - 1, high), land(1, high), down, base + 5),
            ]
            sums = [(chunk(c + 1, low), land(2, low)), (chunk(c - 1, high), land(2, high))]
            out.append((chunk(c), [land(0), land(1)], copies, way, later, sums))
        return u, out

    def send(unit, phase):
        _, _, copies, way, _, _ = unit[1][phase]
        for copy in list(way) + copies:
            go(copy)

    def forward(unit):
        _, _, _, way, later, sums = unit[1][0]
        for n in range(2):
            way[n].wait_recv()
            out, got = sums[n]
            out[...] = (out[...].astype(F32) + got[...].astype(F32)).astype(BF)
            go(later[n])

    def settle(unit, phase):
        u, phases = unit
        own, lands, copies, _, later, _ = phases[phase]
        for copy in copies + list(later):
            copy.wait_recv()
        value = own[...].astype(F32)
        for got in lands:
            value = value + got[...].astype(F32)
        if phase < 2:
            into = (s2, s3)[phase]
            into[u] = value.astype(into.dtype)
            send(unit, phase + 1)
        else:
            fin[u] = value

    mids = [plan(b, MIDDLE[b], True) for b in range(3)]
    nears = [plan(3 + 3 * s + b, OUTER[b], True) for b in range(3)]
    fars = [plan(3 + 3 * (1 - s) + b, OUTER[b], True) for b in range(3)]
    smalls = plan(9, SMALL, True)

    def proj_grad(b):
        return t_mm(joined[b], dh[...]).astype(BF).reshape(4, 4, 16, 256)

    p_copies = [remote(pbuf.at[n], s1.at[9, 2 * n], partner) for n in range(2)]

    def tap(u, rows, grad):
        for c in range(4):
            value = t_mm(xbuf[rows, c * 256 : (c + 1) * 256], grad)
            s1[u, c] = value.astype(BF).reshape(4, 4, 16, 256)

    everyone = pl.ds(XB * BLK, CHIP)

    def rows_from(m, count):
        return pl.ds(pl.multiple_of(m * BLK, 16), count * BLK)

    def middle_tap(b):
        tap(b, everyone, ext[b, rows_from(BASE, 4), :])
        send(mids[b], 0)

    middle_tap(0)
    first_grad(theirs)

    @pl.when(core == 1)
    def _():
        for n in range(2):
            pbuf[n] = proj_grad(2 * n)
            p_copies[n].start()

        tap(9, everyone, db0[...])

    @pl.when(core == 0)
    def _():
        s1[9, 1] = proj_grad(1)
        s1[9, 3] = jnp.zeros((4, 4, 16, 256), BF)
        for n in range(2):
            p_copies[n].wait_recv()

    send(smalls, 0)
    middle_tap(1)
    middle_tap(2)
    passed_rows = block(jnp.where(s == 0, XB + 4, 0) + core)
    for h in range(2):
        lanes = slice(h * 512, h * 512 + 512)
        remote(xbuf.at[passed_rows, lanes], xbuf.at[passed_rows, lanes], across, UNITS * 12 + 4 + h).wait_recv()
    passed = go(remote(xbuf.at[passed_rows], xbuf.at[passed_rows], partner, UNITS * 12 + 6))

    small_step(0)

    @pl.when(core == 1)
    def _():
        raw_copy.wait_recv()
        to = block(jnp.where(s == 0, BASE + 4, BASE - 1))
        value = hraw[...].astype(F32)
        ext[0, to, :] = from_right(value).astype(BF)
        ext[1, to, :] = hraw[...]
        ext[2, to, :] = from_left(value).astype(BF)

    for b in range(3):
        x_at = XB + jnp.where(s == 0, 0, 2)
        g_at = BASE + jnp.where(s == 0, k, 2 - k)
        tap(nears[b][0], rows_from(x_at, 2), ext[b, rows_from(g_at, 2), :])
        send(nears[b], 0)

    passed.wait_recv()
    for b in range(3):
        for n in range(2):
            @pl.when(core == n)
            def _(n=n, b=b):
                x_at = jnp.where(s == 0, XB + 2 + n, 0)
                g_at = BASE + jnp.where(s == 0, 0, n)
                tap(fars[b][0], rows_from(x_at, 4 - n), ext[b, rows_from(g_at, 4 - n), :])
        send(fars[b], 0)
        if b == 0:
            forward(smalls)

    for unit in mids:
        forward(unit)
    settle(smalls, 0)
    for unit in nears:
        forward(unit)
    for unit in mids:
        settle(unit, 0)
    settle(smalls, 1)
    for unit in fars:
        forward(unit)
    small_step(1)
    settle(smalls, 2)

    eout[core, cx, cz, cy] = fin[9].astype(BF)
    everything = slice(None)

    def gather(axis, at):
        view = eout.at[(core,) + at]
        return [remote(view, view, peer(axis, d)) for d in (2, 1, 3)]

    gathers = [gather("z", (cx, cz, cy)), gather("y", (cx, everything, cy)), gather("x", (cx, everything, everything))]

    def gather_next(n):
        for copy in gathers[n - 1] if n else ():
            copy.wait_recv()
        for copy in gathers[n] if n < 3 else ():
            go(copy)

    gather_next(0)
    for unit in nears:
        settle(unit, 0)
    for unit in mids:
        settle(unit, 1)
    gather_next(1)
    for unit in fars:
        settle(unit, 0)
    small_step(2)
    for unit in nears:
        settle(unit, 1)
    gather_next(2)
    for unit in mids:
        settle(unit, 2)
    for unit in fars:
        settle(unit, 1)
    small_step(3)
    gather_next(3)
    e_swap = go(remote(eout.at[core], eout.at[core], partner))
    for unit in nears:
        settle(unit, 2)
    for unit in fars:
        settle(unit, 2)

    give = pl.ds(pl.multiple_of((1 - core) * 8, 8), 8)
    keep = pl.ds(pl.multiple_of(core * 8, 8), 8)
    swap[0] = fin[0:9, give, :]
    f_swap = go(remote(swap.at[0], swap.at[1], partner))

    e_swap.wait_recv()
    f_swap.wait_recv()
    for u in range(9):
        at = u + 3 if u < 3 else u - 3 if u < 6 else u
        o_atr[core, at] = fin[u, keep, :]
        o_atr[1 - core, at] = swap[1, u]

    crossing(lambda g, t, m: cross_copy(t, g).wait_send())

    haloes(lambda copy: copy.wait_send())

    @pl.when(core == 1)
    def _():
        raw_copy.wait_send()

    @pl.when(core == 0)
    def _():
        j_copies[1].wait_send()

    @pl.when(core == 1)
    def _():
        for copy in (j_copies[0], j_copies[2], p_copies[0], p_copies[1]):
            copy.wait_send()

    for copy in sends:
        copy.wait_send()
    assert counter[0] <= COPIES


COPIES = 180
UNITS = 10


def widen(scale, shares, small, tiny, o_atr, o_one, o_proj, o_cls, o_loss):
    o_atr[...] = shares[...]
    o_proj[...] = small[0, 0:768].astype(F32)
    o_one[...] = small[1].astype(F32)
    o_cls[...] = tiny[0:3]
    o_loss[...] = tiny[3:4, 0:1] * scale


def on_device(features, labels, w_one, w_atrous, w_proj, w_class):
    total_pix = lax.axis_size("dp") * lax.axis_size("space") * OWN
    vmem = pl.BlockSpec(memory_space=pltpu.VMEM)
    hbm = pl.BlockSpec(memory_space=pl.ANY)
    scratch = [
        ((8 * BLK, 1024), BF),
        ((3, 3, 1024, 256), BF),
        ((2, 3, 1024, 256), BF),
        ((1024, 256), BF),
        ((4, 3, BLK, 256), F32),
        ((CHIP, 256), F32),
        ((CHIP, 256), F32),
        ((2, 3, BLK, 256), BF),
        ((3, BLK, 256), BF),
        ((3, CHIP, 256), BF),
        ((CHIP, 256), BF),
        ((3, 6 * BLK, 256), BF),
        ((CHIP, 256), BF),
        ((CHIP, 256), BF),
        ((BLK, 256), BF),
        ((UNITS, 4, 4, 4, 16, 256), BF),
        ((UNITS, 3, 4, 4, 16, 256), BF),
        ((UNITS, 4, 4, 16, 256), BF),
        ((UNITS, 3, 4, 16, 256), BF),
        ((UNITS, 4, 16, 256), F32),
        ((UNITS, 3, 16, 256), F32),
        ((UNITS, 16, 256), F32),
        ((2, 4, 4, 16, 256), BF),
        ((4, 4, 16, 256), F32),
        ((2, 9, 8, 256), F32),
        ((1, OWN), jnp.int32),
    ]
    shares, small, tiny = pl.pallas_call(
        lambda *refs: kernel(1.0 / math.sqrt(total_pix), *refs),
        out_shape=(
            jax.ShapeDtypeStruct((2, 9, 8, 256), F32),
            jax.ShapeDtypeStruct((2, 4, 4, 4, 16, 256), BF),
            jax.ShapeDtypeStruct((16, 256), F32),
        ),
        in_specs=[hbm, vmem, hbm, hbm, vmem, vmem],
        out_specs=(vmem, vmem, vmem),
        scratch_shapes=[pltpu.VMEM(shape, kind) for shape, kind in scratch]
        + [
            pltpu.SemaphoreType.DMA((7,)),
            pltpu.SemaphoreType.DMA((COPIES,)),
            pltpu.SemaphoreType.DMA((COPIES,)),
        ],
        compiler_params=pltpu.CompilerParams(
            collective_id=0, has_side_effects=True, vmem_limit_bytes=60 * 1024 * 1024
        ),
        name="aspp",
    )(
        features.reshape(OWN, 1024),
        labels.transpose(1, 0, 2),
        w_one,
        w_atrous,
        w_proj.reshape(3, 256, 256),
        w_class.T,
    )
    grad_atrous, grad_one, grad_proj, grad_class, loss = pl.pallas_call(
        lambda *refs: widen(1.0 / total_pix, *refs),
        out_shape=(
            jax.ShapeDtypeStruct((2, 9, 8, 256), F32),
            jax.ShapeDtypeStruct((1024, 256), F32),
            jax.ShapeDtypeStruct((768, 256), F32),
            jax.ShapeDtypeStruct((3, 256), F32),
            jax.ShapeDtypeStruct((1, 1), F32),
        ),
        in_specs=[vmem] * 3,
        out_specs=(vmem,) * 5,
        name="widen",
    )(shares, small.reshape(2, 1024, 256), tiny)
    return (grad_atrous.reshape(2, 3, 3, 8, 256), grad_one, grad_proj, grad_class.T, loss.reshape(()))


def solution(mesh):
    return jax.shard_map(
        on_device,
        mesh=mesh,
        in_specs=(P("dp", "space", None, None), P("dp", "space", None), P(), P(), P(), P()),
        out_specs=(P(None, None, None, ("dp", "space"), None), P(), P(), P(), P()),
        check_vma=False,
    )
```

```python
import math

import jax
import jax.numpy as jnp
from jax import lax
from jax.experimental import pallas as pl
from jax.experimental.pallas import tpu as pltpu
from jax.sharding import PartitionSpec as P

MESH = pl.DeviceIdType.MESH
BF = jnp.bfloat16
F32 = jnp.float32
WIDTH = 56
BLK = 6 * WIDTH
OWN = 12 * WIDTH
CHIP = 24 * WIDTH
BASE = 1
XB = 2
MIDDLE = ("xzy", "zyx", "zxy")
OUTER = ("xzy", "zyx", "yxz")
SMALL = "xyz"
AXES = "xzy"


def slope(pre):
    gate = jax.nn.sigmoid(pre)
    return gate * (1.0 + pre * (1.0 - gate))


def silu(pre):
    return pre * jax.nn.sigmoid(pre)


def mm(first, second):
    return jnp.dot(first, second, preferred_element_type=F32)


def mm_t(first, second):
    return lax.dot_general(first, second, (((1,), (1,)), ((), ())), preferred_element_type=F32)


def t_mm(first, second):
    return lax.dot_general(first, second, (((0,), (0,)), ((), ())), preferred_element_type=F32)


def kernel(
    loss_scale,
    feat, labels, w_one_h, w_atr_h, w_proj, w_cls,
    o_atr, eout, o_cls,
    xbuf, wbuf, wtow, wone, tacc, pre, pre0, cs, cr, joined, dh, ext, db0, raw, hraw,
    s1, r1, s2, r2, s3, r3, rp, fin, pbuf, clbuf, swap, lab,
    lsem, ssem, rsem,
):
    dp = lax.axis_index("dp")
    sp = lax.axis_index("space")
    core, s = sp % 2, sp // 2
    cx, cz, cy = dp // 8, (dp // 2) % 4, (dp % 2) * 2 + s
    here = {"x": cx, "z": cz, "y": cy}

    def place(x, z, y, c):
        return (x * 8 + z * 2 + y // 2, (y % 2) * 2 + c)

    partner = place(cx, cz, cy, 1 - core)
    across = (dp, (1 - s) * 2 + core)
    beyond = (dp, (1 - s) * 2 + 1 - core)

    def peer(axis, d):
        at = dict(here)
        at[axis] = (at[axis] + d) % 4
        return place(at["x"], at["z"], at["y"], core)

    rate = 12 + 6 * core
    k = 2 + core

    counter = [UNITS * 12 + 17]

    def remote(src, dst, to, i=None, sent=None):
        if i is None:
            i = counter[0]
            counter[0] += 1
        return pltpu.make_async_remote_copy(
            src_ref=src, dst_ref=dst, send_sem=ssem.at[i if sent is None else sent], recv_sem=rsem.at[i], device_id=to, device_id_type=MESH
        )

    sends = []

    def go(copy):
        copy.start()
        sends.append(copy)
        return copy

    own_rows = pl.ds(pl.multiple_of(core * OWN, 16), OWN)
    other_rows = pl.ds(pl.multiple_of((1 - core) * OWN, 16), OWN)
    x_own = pl.ds(pl.multiple_of(XB * BLK + core * OWN, 16), OWN)
    x_local = pltpu.make_async_copy(feat, xbuf.at[x_own], lsem.at[0])
    x_local.start()
    w_local = [pltpu.make_async_copy(w_atr_h.at[core, a], wbuf.at[a], lsem.at[1 + a]) for a in range(3)]
    cross_tap = s * 2
    tow_local = [pltpu.make_async_copy(w_atr_h.at[g, cross_tap], wtow.at[g], lsem.at[5 + g]) for g in range(2)]
    for copy in (tow_local[1], tow_local[0], w_local[1], w_local[0], w_local[2]):
        copy.start()
    one_local = pltpu.make_async_copy(w_one_h, wone, lsem.at[4])
    one_local.start()

    barrier = pltpu.get_barrier_semaphore()
    around = [(dz, dy) for dz in (2, 1, 3, 0) for dy in (2, 1, 3, 0) if dz or dy]

    def aside(dz, dy):
        return place(cx, (cz + dz) % 4, (cy + dy) % 4, core)

    greet = [partner, beyond] + [peer("x", d) for d in (1, 2, 3)] + [aside(*at) for at in around]
    for other in greet:
        pl.semaphore_signal(barrier, inc=1, device_id=other, device_id_type=MESH)

    tacc[...] = jnp.zeros_like(tacc)

    column = lax.rem(lax.broadcasted_iota(jnp.int32, (BLK, 256), 0), WIDTH)

    def from_left(value, rate=rate):
        return jnp.where(column >= rate, pltpu.roll(value, rate, 0), 0.0)

    def from_right(value, rate=rate):
        return jnp.where(column < WIDTH - rate, pltpu.roll(value, BLK - rate, 0), 0.0)

    def block(m):
        return pl.ds(pl.multiple_of(m * BLK, 16), BLK)

    def middle(m):
        rows = xbuf[block(XB + m), :]
        for b in range(3):
            tacc[m, b] += mm(rows, wbuf[1, b])

    def outer(m):
        for a in (0, 2):
            to = m - (a - 1) * k

            @pl.when((to >= 0) & (to < 4))
            def _(a=a, to=to):
                rows = xbuf[block(XB + m), :]
                for b in range(3):
                    tacc[to, b] += mm(rows, wbuf[a, b])

    def cross_copy(t, g=None):
        if g is None:
            return remote(cs.at[0, t], cr.at[t], across, UNITS * 12 + t)
        to = (dp, (1 - s) * 2 + g)
        return remote(cs.at[g, t], cr.at[t], to, UNITS * 12 + t, UNITS * 12 + 7 + 3 * g + t)

    def crossing(body):
        for g, t in ((1, 0), (1, 1), (1, 2), (0, 0), (0, 1)):
            m = jnp.where(s == 0, 2 - g + t, t)

            @pl.when(m // 2 == core)
            def _(g=g, t=t, m=m):
                body(g, t, m)

    def cross(g, t, m):
        rows = xbuf[block(XB + m), :]
        parts = [mm(rows, wtow[g, b]) for b in range(3)]
        shifted = from_left(parts[0], 12 + 6 * g) + from_right(parts[2], 12 + 6 * g)
        cs[g, t] = (parts[1] + shifted).astype(BF)

    mine, theirs = 2 * core, 2 * (1 - core)
    x_local.wait()
    for copy in tow_local:
        copy.wait()
    crossing(cross)
    pl.semaphore_wait(barrier, len(greet))
    crossing(lambda g, t, m: cross_copy(t, g).start())
    x_swap = go(remote(feat, xbuf.at[x_own], partner))
    for copy in (w_local[1], w_local[0], w_local[2]):
        copy.wait()
    pl.loop(0, 2)(lambda q: middle(mine + q))
    pl.loop(0, 2)(lambda q: outer(mine + q))
    x_swap.wait_recv()

    @pl.loop(0, 2)
    def _(q):
        middle(theirs + q)
        outer(theirs + q)

    def halo(j, h):
        rows = block(XB + jnp.where(s == 0, 2, 0) + j)
        to = block(jnp.where(s == 0, j, XB + 4 + j))
        lanes = slice(h * 512, h * 512 + 512)
        i = UNITS * 12 + 4 + h
        return remote(xbuf.at[rows, lanes], xbuf.at[to, lanes], (dp, (1 - s) * 2 + j), i, UNITS * 12 + 13 + 2 * j + h)

    def haloes(body):
        @pl.when(core == s)
        def _():
            for j, h in ((0, 0), (0, 1), (1, 0)):
                body(halo(j, h))

        @pl.when(core == 1 - s)
        def _():
            body(halo(1, 1))

    haloes(lambda copy: copy.start())

    @pl.loop(0, 4)
    def _(i):
        pre[block(i), :] = tacc[i, 1] + from_left(tacc[i, 0]) + from_right(tacc[i, 2])

    one_local.wait()

    @pl.when(core == 1)
    def _():
        @pl.loop(0, 4)
        def _(i):
            value = mm(xbuf[block(XB + i), :], wone[...])
            pre0[block(i), :] = value
            joined[0, block(i), :] = silu(value).astype(BF)

    for t in range(3):
        @pl.when(t < k)
        def _(t=t):
            cross_copy(t).wait_recv()
            into = block(jnp.where(s == 0, 4 - k + t, t))
            pre[into, :] += cr[t].astype(F32)

    @pl.loop(0, 4)
    def _(i):
        joined[1 + core, block(i), :] = silu(pre[block(i), :]).astype(BF)

    j_copies = [remote(joined.at[b, other_rows], joined.at[b, other_rows], partner) for b in range(3)]

    @pl.when(core == 0)
    def _():
        j_copies[1].start()

    @pl.when(core == 1)
    def _():
        j_copies[0].start()
        j_copies[2].start()

    @pl.when(core == 0)
    def _():
        j_copies[0].wait_recv()
        j_copies[2].wait_recv()

    @pl.when(core == 1)
    def _():
        j_copies[1].wait_recv()

    pre_hidden = mm(joined[0, own_rows, :], w_proj[0])
    pre_hidden += mm(joined[1, own_rows, :], w_proj[1])
    pre_hidden += mm(joined[2, own_rows, :], w_proj[2])
    hidden = silu(pre_hidden).astype(BF)
    classes = jnp.concatenate([w_cls[...].astype(F32), jnp.zeros((13, 256), F32)]).astype(BF)
    for y in range(12):
        lab[:, y * WIDTH : (y + 1) * WIDTH] = labels[y]
    logits = mm_t(classes, hidden)
    row = lax.broadcasted_iota(jnp.int32, logits.shape, 0)
    valid = row < 3
    top = jnp.max(jnp.where(valid, logits, -jnp.inf), axis=0, keepdims=True)
    total = jnp.sum(jnp.where(valid, jnp.exp(logits - top), 0.0), axis=0, keepdims=True)
    lse = top + jnp.log(total)
    onehot = row == lab[...]
    loss = jnp.sum(lse - jnp.sum(jnp.where(onehot, logits, 0.0), axis=0, keepdims=True), axis=1, keepdims=True)
    probs = jnp.exp(logits - lse) - jnp.where(onehot, 1.0, 0.0)
    dlogits = jnp.where(valid, probs * loss_scale, 0.0).astype(BF)
    dhidden = t_mm(dlogits, classes) * slope(pre_hidden)
    dh[own_rows, :] = dhidden.astype(BF)
    dh_copy = go(remote(dh.at[own_rows], dh.at[own_rows], partner))

    small = mm(dlogits, hidden)
    srow = lax.broadcasted_iota(jnp.int32, small.shape, 0)
    cl_copies = []
    for n, axis in enumerate(AXES):
        cl_copies.append([remote(clbuf.at[n, here[axis]], clbuf.at[n, here[axis]], peer(axis, d)) for d in (1, 2, 3)])
    cl_copies.append([remote(clbuf.at[3, core], clbuf.at[3, core], partner)])
    clbuf[0, here["x"]] = jnp.where(srow == 3, loss, small)
    for copy in cl_copies[0]:
        go(copy)

    def small_step(n):
        for copy in cl_copies[n]:
            copy.wait_recv()
        value = clbuf[n, 0] + clbuf[n, 1]
        if n < 3:
            value = value + clbuf[n, 2] + clbuf[n, 3]
            clbuf[n + 1, core if n == 2 else here[AXES[n + 1]]] = value
            for copy in cl_copies[n + 1]:
                go(copy)
        else:
            o_cls[...] = value

    branch_w = w_proj[1 + core]

    raw_copy = remote(raw.at[block(jnp.where(s == 0, 3, 0))], hraw, across, UNITS * 12 + 3)

    def branch_grad(i):
        value = mm_t(dh[block(i), :], branch_w) * slope(pre[block(i), :])
        raw[block(i), :] = value.astype(BF)

        @pl.when((core == 1) & (i == jnp.where(s == 0, 3, 0)))
        def _():
            raw_copy.start()

        to = block(BASE + i)
        rounded = value.astype(BF).astype(F32)
        ext[0, to, :] = from_right(rounded).astype(BF)
        ext[1, to, :] = rounded.astype(BF)
        ext[2, to, :] = from_left(rounded).astype(BF)

    def first_grad(first):
        @pl.when(core == 1)
        def _():
            @pl.loop(0, 2)
            def _(q):
                rows = block(first + q)
                db0[rows, :] = (mm_t(dh[rows, :], w_proj[0]) * slope(pre0[rows, :])).astype(BF)

    pl.loop(0, 2)(lambda q: branch_grad(mine + q))
    first_grad(mine)
    dh_copy.wait_recv()
    pl.loop(0, 2)(lambda q: branch_grad(theirs + q))

    low, high = pl.ds(0, 2), pl.ds(2, 2)

    def plan(u, order, ring):
        out = []
        for phase, (buf, landing) in enumerate(((s1, r1), (s2, r2), (s3, r3))):
            axis = order[phase]
            left = [a for a in AXES if a in order[phase:]]
            spot = left.index(axis)
            c = here[axis]
            base = u * 12 + (0, 6, 9)[phase]

            def chunk(at, half=None):
                index = [u] + [slice(None)] * len(left)
                index[1 + spot] = (at + 4) % 4
                if half is not None:
                    index[2 if spot == 0 else 1] = half
                return buf.at[tuple(index)]

            def land(slot, half=None):
                return landing.at[u, slot] if half is None else landing.at[u, slot, half]

            if phase or not ring:
                copies = [remote(chunk(c + d), land(d - 1), peer(axis, d), base + d - 1) for d in (2, 1, 3)]
                out.append((chunk(c), [land(n) for n in range(3)], copies, (), (), ()))
                continue
            up, down = peer(axis, 1), peer(axis, 3)
            way = [
                remote(chunk(c + 2, low), land(2, low), up, base),
                remote(chunk(c + 2, high), land(2, high), down, base + 1),
            ]
            copies = [
                remote(chunk(c + 1, high), land(0, high), up, base + 2),
                remote(chunk(c - 1, low), land(1, low), down, base + 3),
            ]
            later = [
                remote(chunk(c + 1, low), land(0, low), up, base + 4),
                remote(chunk(c - 1, high), land(1, high), down, base + 5),
            ]
            sums = [(chunk(c + 1, low), land(2, low)), (chunk(c - 1, high), land(2, high))]
            out.append((chunk(c), [land(0), land(1)], copies, way, later, sums))
        return u, out

    def send(unit, phase):
        _, _, copies, way, _, _ = unit[1][phase]
        for copy in list(way) + copies:
            go(copy)

    def forward(unit):
        _, _, _, way, later, sums = unit[1][0]
        for n in range(2):
            way[n].wait_recv()
            out, got = sums[n]
            out[...] = (out[...].astype(F32) + got[...].astype(F32)).astype(BF)
            go(later[n])

    def settle(unit, phase):
        u, phases = unit
        own, lands, copies, _, later, _ = phases[phase]
        for copy in copies + list(later):
            copy.wait_recv()
        value = own[...].astype(F32)
        for got in lands:
            value = value + got[...].astype(F32)
        if phase < 2:
            into = (s2, s3)[phase]
            into[u] = value.astype(into.dtype)
            if unit is smalls:
                for copy in plane:
                    go(copy)
            else:
                send(unit, phase + 1)
        else:
            fin[u] = value

    mids = [plan(b, MIDDLE[b], True) for b in range(3)]
    nears = [plan(3 + 3 * s + b, OUTER[b], True) for b in range(3)]
    fars = [plan(3 + 3 * (1 - s) + b, OUTER[b], True) for b in range(3)]
    smalls = plan(9, SMALL, True)
    plane = [
        remote(s2.at[9, (cz + dz) % 4, (cy + dy) % 4], rp.at[dz * 4 + dy - 1], aside(dz, dy)) for dz, dy in around
    ]

    def proj_grad(b):
        return t_mm(joined[b], dh[...]).astype(BF).reshape(4, 4, 16, 256)

    p_copies = [remote(pbuf.at[n], s1.at[9, 2 * n], partner) for n in range(2)]

    def tap(u, rows, grad):
        for c in range(4):
            value = t_mm(xbuf[rows, c * 256 : (c + 1) * 256], grad)
            s1[u, c] = value.astype(BF).reshape(4, 4, 16, 256)

    everyone = pl.ds(XB * BLK, CHIP)

    def rows_from(m, count):
        return pl.ds(pl.multiple_of(m * BLK, 16), count * BLK)

    def middle_tap(b):
        tap(b, everyone, ext[b, rows_from(BASE, 4), :])
        send(mids[b], 0)

    middle_tap(0)
    first_grad(theirs)

    @pl.when(core == 1)
    def _():
        for n in range(2):
            pbuf[n] = proj_grad(2 * n)
            p_copies[n].start()

        tap(9, everyone, db0[...])

    @pl.when(core == 0)
    def _():
        s1[9, 1] = proj_grad(1)
        s1[9, 3] = jnp.zeros((4, 4, 16, 256), BF)
        for n in range(2):
            p_copies[n].wait_recv()

    send(smalls, 0)
    middle_tap(1)
    middle_tap(2)
    passed_rows = block(jnp.where(s == 0, XB + 4, 0) + core)
    passed = []
    for h in range(2):
        piece = xbuf.at[passed_rows, slice(h * 512, h * 512 + 512)]
        remote(piece, piece, across, UNITS * 12 + 4 + h).wait_recv()
        passed.append(go(remote(piece, piece, partner)))

    small_step(0)

    @pl.when(core == 1)
    def _():
        raw_copy.wait_recv()
        to = block(jnp.where(s == 0, BASE + 4, BASE - 1))
        value = hraw[...].astype(F32)
        ext[0, to, :] = from_right(value).astype(BF)
        ext[1, to, :] = hraw[...]
        ext[2, to, :] = from_left(value).astype(BF)

    for b in range(3):
        x_at = XB + jnp.where(s == 0, 0, 2)
        g_at = BASE + jnp.where(s == 0, k, 2 - k)
        tap(nears[b][0], rows_from(x_at, 2), ext[b, rows_from(g_at, 2), :])
        send(nears[b], 0)

    for copy in passed:
        copy.wait_recv()
    for b in range(3):
        for n in range(2):
            @pl.when(core == n)
            def _(n=n, b=b):
                x_at = jnp.where(s == 0, XB + 2 + n, 0)
                g_at = BASE + jnp.where(s == 0, 0, n)
                tap(fars[b][0], rows_from(x_at, 4 - n), ext[b, rows_from(g_at, 4 - n), :])
        send(fars[b], 0)
        if b == 0:
            forward(smalls)

    for unit in mids:
        forward(unit)
    settle(smalls, 0)
    for unit in nears:
        forward(unit)
    for unit in mids:
        settle(unit, 0)
    for unit in fars:
        forward(unit)
    small_step(1)

    for copy in plane:
        copy.wait_recv()
    value = s2[9, cz, cy].astype(F32)
    for n in range(15):
        value = value + rp[n].astype(F32)
    eout[core, cx, cz, cy] = value.astype(BF)
    share, slab = eout.at[core, cx, cz, cy], eout.at[core, cx]
    gather_plane = [remote(share, share, aside(dz, dy)) for dz, dy in around]
    gather_x = [remote(slab, slab, peer("x", d)) for d in (2, 1, 3)]
    for copy in gather_plane:
        go(copy)
    for unit in nears:
        settle(unit, 0)
    for unit in mids:
        settle(unit, 1)
    for copy in gather_plane:
        copy.wait_recv()
    for copy in gather_x:
        go(copy)
    for unit in fars:
        settle(unit, 0)
    small_step(2)
    for unit in nears:
        settle(unit, 1)
    for unit in mids:
        settle(unit, 2)
    for unit in fars:
        settle(unit, 1)
    small_step(3)
    for copy in gather_x:
        copy.wait_recv()
    e_swap = go(remote(eout.at[core], eout.at[core], partner))
    for unit in nears:
        settle(unit, 2)
    for unit in fars:
        settle(unit, 2)

    give = pl.ds(pl.multiple_of((1 - core) * 8, 8), 8)
    keep = pl.ds(pl.multiple_of(core * 8, 8), 8)
    swap[0] = fin[0:9, give, :]
    f_swap = go(remote(swap.at[0], swap.at[1], partner))

    e_swap.wait_recv()
    f_swap.wait_recv()
    for u in range(9):
        at = u + 3 if u < 3 else u - 3 if u < 6 else u
        o_atr[core, at] = fin[u, keep, :]
        o_atr[1 - core, at] = swap[1, u]

    crossing(lambda g, t, m: cross_copy(t, g).wait_send())

    haloes(lambda copy: copy.wait_send())

    @pl.when(core == 1)
    def _():
        raw_copy.wait_send()

    @pl.when(core == 0)
    def _():
        j_copies[1].wait_send()

    @pl.when(core == 1)
    def _():
        for copy in (j_copies[0], j_copies[2], p_copies[0], p_copies[1]):
            copy.wait_send()

    for copy in sends:
        copy.wait_send()
    assert counter[0] <= COPIES


COPIES = 210
UNITS = 10


def widen(scale, shares, small, tiny, o_atr, o_one, o_proj, o_cls, o_loss):
    o_atr[...] = shares[...]
    o_proj[...] = small[0, 0:768].astype(F32)
    o_one[...] = small[1].astype(F32)
    o_cls[...] = tiny[0:3]
    o_loss[...] = tiny[3:4, 0:1] * scale


def on_device(features, labels, w_one, w_atrous, w_proj, w_class):
    total_pix = lax.axis_size("dp") * lax.axis_size("space") * OWN
    vmem = pl.BlockSpec(memory_space=pltpu.VMEM)
    hbm = pl.BlockSpec(memory_space=pl.ANY)
    scratch = [
        ((8 * BLK, 1024), BF),
        ((3, 3, 1024, 256), BF),
        ((2, 3, 1024, 256), BF),
        ((1024, 256), BF),
        ((4, 3, BLK, 256), F32),
        ((CHIP, 256), F32),
        ((CHIP, 256), F32),
        ((2, 3, BLK, 256), BF),
        ((3, BLK, 256), BF),
        ((3, CHIP, 256), BF),
        ((CHIP, 256), BF),
        ((3, 6 * BLK, 256), BF),
        ((CHIP, 256), BF),
        ((CHIP, 256), BF),
        ((BLK, 256), BF),
        ((UNITS, 4, 4, 4, 16, 256), BF),
        ((UNITS, 3, 4, 4, 16, 256), BF),
        ((UNITS, 4, 4, 16, 256), BF),
        ((UNITS, 3, 4, 16, 256), BF),
        ((UNITS, 4, 16, 256), F32),
        ((UNITS, 3, 16, 256), F32),
        ((15, 16, 256), BF),
        ((UNITS, 16, 256), F32),
        ((2, 4, 4, 16, 256), BF),
        ((4, 4, 16, 256), F32),
        ((2, 9, 8, 256), F32),
        ((1, OWN), jnp.int32),
    ]
    shares, small, tiny = pl.pallas_call(
        lambda *refs: kernel(1.0 / math.sqrt(total_pix), *refs),
        out_shape=(
            jax.ShapeDtypeStruct((2, 9, 8, 256), F32),
            jax.ShapeDtypeStruct((2, 4, 4, 4, 16, 256), BF),
            jax.ShapeDtypeStruct((16, 256), F32),
        ),
        in_specs=[hbm, vmem, hbm, hbm, vmem, vmem],
        out_specs=(vmem, vmem, vmem),
        scratch_shapes=[pltpu.VMEM(shape, kind) for shape, kind in scratch]
        + [
            pltpu.SemaphoreType.DMA((7,)),
            pltpu.SemaphoreType.DMA((COPIES,)),
            pltpu.SemaphoreType.DMA((COPIES,)),
        ],
        compiler_params=pltpu.CompilerParams(
            collective_id=0, has_side_effects=True, vmem_limit_bytes=60 * 1024 * 1024
        ),
        name="aspp",
    )(
        features.reshape(OWN, 1024),
        labels.transpose(1, 0, 2),
        w_one,
        w_atrous,
        w_proj.reshape(3, 256, 256),
        w_class.T,
    )
    grad_atrous, grad_one, grad_proj, grad_class, loss = pl.pallas_call(
        lambda *refs: widen(1.0 / total_pix, *refs),
        out_shape=(
            jax.ShapeDtypeStruct((2, 9, 8, 256), F32),
            jax.ShapeDtypeStruct((1024, 256), F32),
            jax.ShapeDtypeStruct((768, 256), F32),
            jax.ShapeDtypeStruct((3, 256), F32),
            jax.ShapeDtypeStruct((1, 1), F32),
        ),
        in_specs=[vmem] * 3,
        out_specs=(vmem,) * 5,
        name="widen",
    )(shares, small.reshape(2, 1024, 256), tiny)
    return (grad_atrous.reshape(2, 3, 3, 8, 256), grad_one, grad_proj, grad_class.T, loss.reshape(()))


def solution(mesh):
    return jax.shard_map(
        on_device,
        mesh=mesh,
        in_specs=(P("dp", "space", None, None), P("dp", "space", None), P(), P(), P(), P()),
        out_specs=(P(None, None, None, ("dp", "space"), None), P(), P(), P(), P()),
        check_vma=False,
    )
```

```python
import math

import jax
import jax.numpy as jnp
from jax import lax
from jax.experimental import pallas as pl
from jax.experimental.pallas import tpu as pltpu
from jax.sharding import PartitionSpec as P

MESH = pl.DeviceIdType.MESH
BF = jnp.bfloat16
F32 = jnp.float32
WIDTH = 56
BLK = 6 * WIDTH
OWN = 12 * WIDTH
CHIP = 24 * WIDTH
BASE = 1
XB = 2
MIDDLE = ("xzy", "zyx", "zxy")
OUTER = ("xzy", "zyx", "yxz")
SMALL = "xyz"
AXES = "xzy"


def slope(pre):
    gate = jax.nn.sigmoid(pre)
    return gate * (1.0 + pre * (1.0 - gate))


def silu(pre):
    return pre * jax.nn.sigmoid(pre)


def mm(first, second):
    return jnp.dot(first, second, preferred_element_type=F32)


def mm_t(first, second):
    return lax.dot_general(first, second, (((1,), (1,)), ((), ())), preferred_element_type=F32)


def t_mm(first, second):
    return lax.dot_general(first, second, (((0,), (0,)), ((), ())), preferred_element_type=F32)


def kernel(
    loss_scale,
    feat, labels, w_one_h, w_atr_h, w_proj, w_cls,
    o_atr, eout, o_cls,
    xbuf, wbuf, wtow, wone, tacc, pre, pre0, cs, cr, joined, dh, ext, db0, raw, hraw,
    s1, r1, s2, r2, s3, r3, fin, pbuf, clbuf, swap, lab,
    lsem, ssem, rsem,
):
    dp = lax.axis_index("dp")
    sp = lax.axis_index("space")
    core, s = sp % 2, sp // 2
    cx, cz, cy = dp // 8, (dp // 2) % 4, (dp % 2) * 2 + s
    here = {"x": cx, "z": cz, "y": cy}

    def place(x, z, y, c):
        return (x * 8 + z * 2 + y // 2, (y % 2) * 2 + c)

    partner = place(cx, cz, cy, 1 - core)
    across = (dp, (1 - s) * 2 + core)
    beyond = (dp, (1 - s) * 2 + 1 - core)

    def peer(axis, d):
        at = dict(here)
        at[axis] = (at[axis] + d) % 4
        return place(at["x"], at["z"], at["y"], core)

    rate = 12 + 6 * core
    k = 2 + core

    counter = [UNITS * 12 + 17]

    def remote(src, dst, to, i=None, sent=None):
        if i is None:
            i = counter[0]
            counter[0] += 1
        return pltpu.make_async_remote_copy(
            src_ref=src, dst_ref=dst, send_sem=ssem.at[i if sent is None else sent], recv_sem=rsem.at[i], device_id=to, device_id_type=MESH
        )

    sends = []

    def go(copy):
        copy.start()
        sends.append(copy)
        return copy

    own_rows = pl.ds(pl.multiple_of(core * OWN, 16), OWN)
    other_rows = pl.ds(pl.multiple_of((1 - core) * OWN, 16), OWN)
    x_own = pl.ds(pl.multiple_of(XB * BLK + core * OWN, 16), OWN)
    x_local = pltpu.make_async_copy(feat, xbuf.at[x_own], lsem.at[0])
    x_local.start()
    w_local = [pltpu.make_async_copy(w_atr_h.at[core, a], wbuf.at[a], lsem.at[1 + a]) for a in range(3)]
    cross_tap = s * 2
    tow_local = [pltpu.make_async_copy(w_atr_h.at[g, cross_tap], wtow.at[g], lsem.at[5 + g]) for g in range(2)]
    for copy in (tow_local[1], tow_local[0], w_local[1], w_local[0], w_local[2]):
        copy.start()
    one_local = pltpu.make_async_copy(w_one_h, wone, lsem.at[4])
    one_local.start()

    barrier = pltpu.get_barrier_semaphore()
    greet = [partner, beyond] + [peer(axis, d) for axis in AXES for d in (1, 2, 3)]
    for other in greet:
        pl.semaphore_signal(barrier, inc=1, device_id=other, device_id_type=MESH)

    tacc[...] = jnp.zeros_like(tacc)

    column = lax.rem(lax.broadcasted_iota(jnp.int32, (BLK, 256), 0), WIDTH)

    def from_left(value, rate=rate):
        return jnp.where(column >= rate, pltpu.roll(value, rate, 0), 0.0)

    def from_right(value, rate=rate):
        return jnp.where(column < WIDTH - rate, pltpu.roll(value, BLK - rate, 0), 0.0)

    def block(m):
        return pl.ds(pl.multiple_of(m * BLK, 16), BLK)

    def middle(m):
        rows = xbuf[block(XB + m), :]
        for b in range(3):
            tacc[m, b] += mm(rows, wbuf[1, b])

    def outer(m):
        for a in (0, 2):
            to = m - (a - 1) * k

            @pl.when((to >= 0) & (to < 4))
            def _(a=a, to=to):
                rows = xbuf[block(XB + m), :]
                for b in range(3):
                    tacc[to, b] += mm(rows, wbuf[a, b])

    def cross_copy(t, g=None):
        if g is None:
            return remote(cs.at[0, t], cr.at[t], across, UNITS * 12 + t)
        to = (dp, (1 - s) * 2 + g)
        return remote(cs.at[g, t], cr.at[t], to, UNITS * 12 + t, UNITS * 12 + 7 + 3 * g + t)

    def crossing(body):
        for g, t in ((1, 0), (1, 1), (1, 2), (0, 0), (0, 1)):
            m = jnp.where(s == 0, 2 - g + t, t)

            @pl.when(m // 2 == core)
            def _(g=g, t=t, m=m):
                body(g, t, m)

    def cross(g, t, m):
        rows = xbuf[block(XB + m), :]
        parts = [mm(rows, wtow[g, b]) for b in range(3)]
        shifted = from_left(parts[0], 12 + 6 * g) + from_right(parts[2], 12 + 6 * g)
        cs[g, t] = (parts[1] + shifted).astype(BF)

    mine, theirs = 2 * core, 2 * (1 - core)
    x_local.wait()
    for copy in tow_local:
        copy.wait()
    crossing(cross)
    pl.semaphore_wait(barrier, len(greet))
    crossing(lambda g, t, m: cross_copy(t, g).start())
    x_swap = go(remote(feat, xbuf.at[x_own], partner))
    for copy in (w_local[1], w_local[0], w_local[2]):
        copy.wait()
    pl.loop(0, 2)(lambda q: middle(mine + q))
    pl.loop(0, 2)(lambda q: outer(mine + q))
    x_swap.wait_recv()

    @pl.loop(0, 2)
    def _(q):
        middle(theirs + q)
        outer(theirs + q)

    def halo(j, h):
        rows = block(XB + jnp.where(s == 0, 2, 0) + j)
        to = block(jnp.where(s == 0, j, XB + 4 + j))
        lanes = slice(h * 512, h * 512 + 512)
        i = UNITS * 12 + 4 + h
        return remote(xbuf.at[rows, lanes], xbuf.at[to, lanes], (dp, (1 - s) * 2 + j), i, UNITS * 12 + 13 + 2 * j + h)

    def haloes(body):
        @pl.when(core == s)
        def _():
            for j, h in ((0, 0), (0, 1), (1, 0)):
                body(halo(j, h))

        @pl.when(core == 1 - s)
        def _():
            body(halo(1, 1))

    haloes(lambda copy: copy.start())

    @pl.loop(0, 4)
    def _(i):
        pre[block(i), :] = tacc[i, 1] + from_left(tacc[i, 0]) + from_right(tacc[i, 2])

    one_local.wait()

    @pl.when(core == 1)
    def _():
        @pl.loop(0, 4)
        def _(i):
            value = mm(xbuf[block(XB + i), :], wone[...])
            pre0[block(i), :] = value
            joined[0, block(i), :] = silu(value).astype(BF)

    for t in range(3):
        @pl.when(t < k)
        def _(t=t):
            cross_copy(t).wait_recv()
            into = block(jnp.where(s == 0, 4 - k + t, t))
            pre[into, :] += cr[t].astype(F32)

    @pl.loop(0, 4)
    def _(i):
        joined[1 + core, block(i), :] = silu(pre[block(i), :]).astype(BF)

    j_copies = [remote(joined.at[b, other_rows], joined.at[b, other_rows], partner) for b in range(3)]

    @pl.when(core == 0)
    def _():
        j_copies[1].start()

    @pl.when(core == 1)
    def _():
        j_copies[0].start()
        j_copies[2].start()

    @pl.when(core == 0)
    def _():
        j_copies[0].wait_recv()
        j_copies[2].wait_recv()

    @pl.when(core == 1)
    def _():
        j_copies[1].wait_recv()

    pre_hidden = mm(joined[0, own_rows, :], w_proj[0])
    pre_hidden += mm(joined[1, own_rows, :], w_proj[1])
    pre_hidden += mm(joined[2, own_rows, :], w_proj[2])
    hidden = silu(pre_hidden).astype(BF)
    classes = jnp.concatenate([w_cls[...].astype(F32), jnp.zeros((13, 256), F32)]).astype(BF)
    for y in range(12):
        lab[:, y * WIDTH : (y + 1) * WIDTH] = labels[y]
    logits = mm_t(classes, hidden)
    row = lax.broadcasted_iota(jnp.int32, logits.shape, 0)
    valid = row < 3
    top = jnp.max(jnp.where(valid, logits, -jnp.inf), axis=0, keepdims=True)
    total = jnp.sum(jnp.where(valid, jnp.exp(logits - top), 0.0), axis=0, keepdims=True)
    lse = top + jnp.log(total)
    onehot = row == lab[...]
    loss = jnp.sum(lse - jnp.sum(jnp.where(onehot, logits, 0.0), axis=0, keepdims=True), axis=1, keepdims=True)
    probs = jnp.exp(logits - lse) - jnp.where(onehot, 1.0, 0.0)
    dlogits = jnp.where(valid, probs * loss_scale, 0.0).astype(BF)
    dhidden = t_mm(dlogits, classes) * slope(pre_hidden)
    dh[own_rows, :] = dhidden.astype(BF)
    dh_copy = go(remote(dh.at[own_rows], dh.at[own_rows], partner))

    small = mm(dlogits, hidden)
    srow = lax.broadcasted_iota(jnp.int32, small.shape, 0)
    cl_copies = []
    for n, axis in enumerate(AXES):
        cl_copies.append([remote(clbuf.at[n, here[axis]], clbuf.at[n, here[axis]], peer(axis, d)) for d in (1, 2, 3)])
    cl_copies.append([remote(clbuf.at[3, core], clbuf.at[3, core], partner)])
    clbuf[0, here["x"]] = jnp.where(srow == 3, loss, small)
    for copy in cl_copies[0]:
        go(copy)

    def small_step(n):
        for copy in cl_copies[n]:
            copy.wait_recv()
        value = clbuf[n, 0] + clbuf[n, 1]
        if n < 3:
            value = value + clbuf[n, 2] + clbuf[n, 3]
            clbuf[n + 1, core if n == 2 else here[AXES[n + 1]]] = value
            for copy in cl_copies[n + 1]:
                go(copy)
        else:
            o_cls[...] = value

    branch_w = w_proj[1 + core]

    raw_copy = remote(raw.at[block(jnp.where(s == 0, 3, 0))], hraw, across, UNITS * 12 + 3)

    def branch_grad(i):
        value = mm_t(dh[block(i), :], branch_w) * slope(pre[block(i), :])
        raw[block(i), :] = value.astype(BF)

        @pl.when((core == 1) & (i == jnp.where(s == 0, 3, 0)))
        def _():
            raw_copy.start()

        to = block(BASE + i)
        rounded = value.astype(BF).astype(F32)
        ext[0, to, :] = from_right(rounded).astype(BF)
        ext[1, to, :] = rounded.astype(BF)
        ext[2, to, :] = from_left(rounded).astype(BF)

    def first_grad(first):
        @pl.when(core == 1)
        def _():
            @pl.loop(0, 2)
            def _(q):
                rows = block(first + q)
                db0[rows, :] = (mm_t(dh[rows, :], w_proj[0]) * slope(pre0[rows, :])).astype(BF)

    pl.loop(0, 2)(lambda q: branch_grad(mine + q))
    first_grad(mine)
    dh_copy.wait_recv()
    pl.loop(0, 2)(lambda q: branch_grad(theirs + q))

    low, high = pl.ds(0, 2), pl.ds(2, 2)

    def plan(u, order, ring):
        out = []
        for phase, (buf, landing) in enumerate(((s1, r1), (s2, r2), (s3, r3))):
            axis = order[phase]
            left = [a for a in AXES if a in order[phase:]]
            spot = left.index(axis)
            c = here[axis]
            base = u * 12 + (0, 6, 9)[phase]

            def chunk(at, half=None):
                index = [u] + [slice(None)] * len(left)
                index[1 + spot] = (at + 4) % 4
                if half is not None:
                    index[2 if spot == 0 else 1] = half
                return buf.at[tuple(index)]

            def land(slot, half=None):
                return landing.at[u, slot] if half is None else landing.at[u, slot, half]

            if phase or not ring:
                copies = [remote(chunk(c + d), land(d - 1), peer(axis, d), base + d - 1) for d in (2, 1, 3)]
                out.append((chunk(c), [land(n) for n in range(3)], copies, (), (), ()))
                continue
            up, down = peer(axis, 1), peer(axis, 3)
            way = [
                remote(chunk(c + 2, low), land(2, low), up, base),
                remote(chunk(c + 2, high), land(2, high), down, base + 1),
            ]
            copies = [
                remote(chunk(c + 1, high), land(0, high), up, base + 2),
                remote(chunk(c - 1, low), land(1, low), down, base + 3),
            ]
            later = [
                remote(chunk(c + 1, low), land(0, low), up, base + 4),
                remote(chunk(c - 1, high), land(1, high), down, base + 5),
            ]
            sums = [(chunk(c + 1, low), land(2, low)), (chunk(c - 1, high), land(2, high))]
            out.append((chunk(c), [land(0), land(1)], copies, way, later, sums))
        return u, out

    def send(unit, phase):
        _, _, copies, way, _, _ = unit[1][phase]
        for copy in list(way) + copies:
            go(copy)

    def forward(unit):
        _, _, _, way, later, sums = unit[1][0]
        for n in range(2):
            way[n].wait_recv()
            out, got = sums[n]
            out[...] = (out[...].astype(F32) + got[...].astype(F32)).astype(BF)
            go(later[n])

    def settle(unit, phase):
        u, phases = unit
        own, lands, copies, _, later, _ = phases[phase]
        for copy in copies + list(later):
            copy.wait_recv()
        value = own[...].astype(F32)
        for got in lands:
            value = value + got[...].astype(F32)
        if phase < 2:
            into = (s2, s3)[phase]
            into[u] = value.astype(into.dtype)
            send(unit, phase + 1)
        else:
            fin[u] = value

    mids = [plan(b, MIDDLE[b], True) for b in range(3)]
    nears = [plan(3 + 3 * s + b, OUTER[b], True) for b in range(3)]
    fars = [plan(3 + 3 * (1 - s) + b, OUTER[b], True) for b in range(3)]
    smalls = plan(9, SMALL, False)

    def proj_grad(b):
        return t_mm(joined[b], dh[...]).astype(BF).reshape(4, 4, 16, 256)

    p_copies = [remote(pbuf.at[n], s1.at[9, 2 * n], partner) for n in range(2)]

    def tap(u, rows, grad):
        for c in range(4):
            value = t_mm(xbuf[rows, c * 256 : (c + 1) * 256], grad)
            s1[u, c] = value.astype(BF).reshape(4, 4, 16, 256)

    everyone = pl.ds(XB * BLK, CHIP)

    def rows_from(m, count):
        return pl.ds(pl.multiple_of(m * BLK, 16), count * BLK)

    def middle_tap(b):
        tap(b, everyone, ext[b, rows_from(BASE, 4), :])
        send(mids[b], 0)

    first_grad(theirs)

    @pl.when(core == 1)
    def _():
        for n in range(2):
            pbuf[n] = proj_grad(2 * n)
            p_copies[n].start()

        tap(9, everyone, db0[...])

    @pl.when(core == 0)
    def _():
        s1[9, 1] = proj_grad(1)
        s1[9, 3] = jnp.zeros((4, 4, 16, 256), BF)
        for n in range(2):
            p_copies[n].wait_recv()

    send(smalls, 0)
    middle_tap(0)
    middle_tap(1)
    middle_tap(2)
    passed_rows = block(jnp.where(s == 0, XB + 4, 0) + core)
    for h in range(2):
        lanes = slice(h * 512, h * 512 + 512)
        remote(xbuf.at[passed_rows, lanes], xbuf.at[passed_rows, lanes], across, UNITS * 12 + 4 + h).wait_recv()
    passed = go(remote(xbuf.at[passed_rows], xbuf.at[passed_rows], partner, UNITS * 12 + 6))

    small_step(0)

    @pl.when(core == 1)
    def _():
        raw_copy.wait_recv()
        to = block(jnp.where(s == 0, BASE + 4, BASE - 1))
        value = hraw[...].astype(F32)
        ext[0, to, :] = from_right(value).astype(BF)
        ext[1, to, :] = hraw[...]
        ext[2, to, :] = from_left(value).astype(BF)

    for b in range(3):
        x_at = XB + jnp.where(s == 0, 0, 2)
        g_at = BASE + jnp.where(s == 0, k, 2 - k)
        tap(nears[b][0], rows_from(x_at, 2), ext[b, rows_from(g_at, 2), :])
        send(nears[b], 0)

    passed.wait_recv()
    for b in range(3):
        for n in range(2):
            @pl.when(core == n)
            def _(n=n, b=b):
                x_at = jnp.where(s == 0, XB + 2 + n, 0)
                g_at = BASE + jnp.where(s == 0, 0, n)
                tap(fars[b][0], rows_from(x_at, 4 - n), ext[b, rows_from(g_at, 4 - n), :])
        send(fars[b], 0)

    settle(smalls, 0)
    for unit in mids:
        forward(unit)
    for unit in nears:
        forward(unit)
    settle(smalls, 1)
    for unit in mids:
        settle(unit, 0)
    for unit in fars:
        forward(unit)
    settle(smalls, 2)

    eout[core, cx, cz, cy] = fin[9].astype(BF)
    everything = slice(None)

    def gather(axis, at):
        view = eout.at[(core,) + at]
        return [remote(view, view, peer(axis, d)) for d in (2, 1, 3)]

    gathers = [gather("z", (cx, cz, cy)), gather("y", (cx, everything, cy)), gather("x", (cx, everything, everything))]

    def gather_next(n):
        for copy in gathers[n - 1] if n else ():
            copy.wait_recv()
        for copy in gathers[n] if n < 3 else ():
            go(copy)

    gather_next(0)
    small_step(1)
    for unit in nears:
        settle(unit, 0)
    gather_next(1)
    for unit in mids:
        settle(unit, 1)
    for unit in fars:
        settle(unit, 0)
    gather_next(2)
    small_step(2)
    for unit in nears:
        settle(unit, 1)
    for unit in mids:
        settle(unit, 2)
    for unit in fars:
        settle(unit, 1)
    small_step(3)
    for unit in nears:
        settle(unit, 2)
    gather_next(3)
    e_swap = go(remote(eout.at[core], eout.at[core], partner))
    for unit in fars:
        settle(unit, 2)

    give = pl.ds(pl.multiple_of((1 - core) * 8, 8), 8)
    keep = pl.ds(pl.multiple_of(core * 8, 8), 8)
    swap[0] = fin[0:9, give, :]
    f_swap = go(remote(swap.at[0], swap.at[1], partner))

    e_swap.wait_recv()
    f_swap.wait_recv()
    for u in range(9):
        at = u + 3 if u < 3 else u - 3 if u < 6 else u
        o_atr[core, at] = fin[u, keep, :]
        o_atr[1 - core, at] = swap[1, u]

    crossing(lambda g, t, m: cross_copy(t, g).wait_send())

    haloes(lambda copy: copy.wait_send())

    @pl.when(core == 1)
    def _():
        raw_copy.wait_send()

    @pl.when(core == 0)
    def _():
        j_copies[1].wait_send()

    @pl.when(core == 1)
    def _():
        for copy in (j_copies[0], j_copies[2], p_copies[0], p_copies[1]):
            copy.wait_send()

    for copy in sends:
        copy.wait_send()
    assert counter[0] <= COPIES


COPIES = 180
UNITS = 10


def widen(scale, shares, small, tiny, o_atr, o_one, o_proj, o_cls, o_loss):
    o_atr[...] = shares[...]
    o_proj[...] = small[0, 0:768].astype(F32)
    o_one[...] = small[1].astype(F32)
    o_cls[...] = tiny[0:3]
    o_loss[...] = tiny[3:4, 0:1] * scale


def on_device(features, labels, w_one, w_atrous, w_proj, w_class):
    total_pix = lax.axis_size("dp") * lax.axis_size("space") * OWN
    vmem = pl.BlockSpec(memory_space=pltpu.VMEM)
    hbm = pl.BlockSpec(memory_space=pl.ANY)
    scratch = [
        ((8 * BLK, 1024), BF),
        ((3, 3, 1024, 256), BF),
        ((2, 3, 1024, 256), BF),
        ((1024, 256), BF),
        ((4, 3, BLK, 256), F32),
        ((CHIP, 256), F32),
        ((CHIP, 256), F32),
        ((2, 3, BLK, 256), BF),
        ((3, BLK, 256), BF),
        ((3, CHIP, 256), BF),
        ((CHIP, 256), BF),
        ((3, 6 * BLK, 256), BF),
        ((CHIP, 256), BF),
        ((CHIP, 256), BF),
        ((BLK, 256), BF),
        ((UNITS, 4, 4, 4, 16, 256), BF),
        ((UNITS, 3, 4, 4, 16, 256), BF),
        ((UNITS, 4, 4, 16, 256), BF),
        ((UNITS, 3, 4, 16, 256), BF),
        ((UNITS, 4, 16, 256), F32),
        ((UNITS, 3, 16, 256), F32),
        ((UNITS, 16, 256), F32),
        ((2, 4, 4, 16, 256), BF),
        ((4, 4, 16, 256), F32),
        ((2, 9, 8, 256), F32),
        ((1, OWN), jnp.int32),
    ]
    shares, small, tiny = pl.pallas_call(
        lambda *refs: kernel(1.0 / math.sqrt(total_pix), *refs),
        out_shape=(
            jax.ShapeDtypeStruct((2, 9, 8, 256), F32),
            jax.ShapeDtypeStruct((2, 4, 4, 4, 16, 256), BF),
            jax.ShapeDtypeStruct((16, 256), F32),
        ),
        in_specs=[hbm, vmem, hbm, hbm, vmem, vmem],
        out_specs=(vmem, vmem, vmem),
        scratch_shapes=[pltpu.VMEM(shape, kind) for shape, kind in scratch]
        + [
            pltpu.SemaphoreType.DMA((7,)),
            pltpu.SemaphoreType.DMA((COPIES,)),
            pltpu.SemaphoreType.DMA((COPIES,)),
        ],
        compiler_params=pltpu.CompilerParams(
            collective_id=0, has_side_effects=True, vmem_limit_bytes=60 * 1024 * 1024
        ),
        name="aspp",
    )(
        features.reshape(OWN, 1024),
        labels.transpose(1, 0, 2),
        w_one,
        w_atrous,
        w_proj.reshape(3, 256, 256),
        w_class.T,
    )
    grad_atrous, grad_one, grad_proj, grad_class, loss = pl.pallas_call(
        lambda *refs: widen(1.0 / total_pix, *refs),
        out_shape=(
            jax.ShapeDtypeStruct((2, 9, 8, 256), F32),
            jax.ShapeDtypeStruct((1024, 256), F32),
            jax.ShapeDtypeStruct((768, 256), F32),
            jax.ShapeDtypeStruct((3, 256), F32),
            jax.ShapeDtypeStruct((1, 1), F32),
        ),
        in_specs=[vmem] * 3,
        out_specs=(vmem,) * 5,
        name="widen",
    )(shares, small.reshape(2, 1024, 256), tiny)
    return (grad_atrous.reshape(2, 3, 3, 8, 256), grad_one, grad_proj, grad_class.T, loss.reshape(()))


def solution(mesh):
    return jax.shard_map(
        on_device,
        mesh=mesh,
        in_specs=(P("dp", "space", None, None), P("dp", "space", None), P(), P(), P(), P()),
        out_specs=(P(None, None, None, ("dp", "space"), None), P(), P(), P(), P()),
        check_vma=False,
    )
```

```python
import math

import jax
import jax.numpy as jnp
from jax import lax
from jax.experimental import pallas as pl
from jax.experimental.pallas import tpu as pltpu
from jax.sharding import PartitionSpec as P

MESH = pl.DeviceIdType.MESH
BF = jnp.bfloat16
F32 = jnp.float32
WIDTH = 56
BLK = 6 * WIDTH
OWN = 12 * WIDTH
CHIP = 24 * WIDTH
BASE = 1
XB = 2
MIDDLE = ("xzy", "zyx", "zxy")
OUTER = ("xzy", "zyx", "yxz")
SMALL = "xyz"
AXES = "xzy"


def slope(pre):
    gate = jax.nn.sigmoid(pre)
    return gate * (1.0 + pre * (1.0 - gate))


def silu(pre):
    return pre * jax.nn.sigmoid(pre)


def mm(first, second):
    return jnp.dot(first, second, preferred_element_type=F32)


def mm_t(first, second):
    return lax.dot_general(first, second, (((1,), (1,)), ((), ())), preferred_element_type=F32)


def t_mm(first, second):
    return lax.dot_general(first, second, (((0,), (0,)), ((), ())), preferred_element_type=F32)


def kernel(
    loss_scale,
    feat, labels, w_one_h, w_atr_h, w_proj, w_cls,
    o_atr, eout, o_cls,
    xbuf, wbuf, wtow, wone, tacc, pre, pre0, cs, cr, joined, dh, ext, db0, raw, hraw,
    s1, r1, s2, r2, s3, r3, fin, pbuf, clbuf, swap, lab,
    lsem, ssem, rsem,
):
    dp = lax.axis_index("dp")
    sp = lax.axis_index("space")
    core, s = sp % 2, sp // 2
    cx, cz, cy = dp // 8, (dp // 2) % 4, (dp % 2) * 2 + s
    here = {"x": cx, "z": cz, "y": cy}

    def place(x, z, y, c):
        return (x * 8 + z * 2 + y // 2, (y % 2) * 2 + c)

    partner = place(cx, cz, cy, 1 - core)
    across = (dp, (1 - s) * 2 + core)
    beyond = (dp, (1 - s) * 2 + 1 - core)

    def peer(axis, d):
        at = dict(here)
        at[axis] = (at[axis] + d) % 4
        return place(at["x"], at["z"], at["y"], core)

    rate = 12 + 6 * core
    k = 2 + core

    counter = [UNITS * 12 + 17]

    def remote(src, dst, to, i=None, sent=None):
        if i is None:
            i = counter[0]
            counter[0] += 1
        return pltpu.make_async_remote_copy(
            src_ref=src, dst_ref=dst, send_sem=ssem.at[i if sent is None else sent], recv_sem=rsem.at[i], device_id=to, device_id_type=MESH
        )

    sends = []

    def go(copy):
        copy.start()
        sends.append(copy)
        return copy

    own_rows = pl.ds(pl.multiple_of(core * OWN, 16), OWN)
    other_rows = pl.ds(pl.multiple_of((1 - core) * OWN, 16), OWN)
    x_own = pl.ds(pl.multiple_of(XB * BLK + core * OWN, 16), OWN)
    x_local = pltpu.make_async_copy(feat, xbuf.at[x_own], lsem.at[0])
    x_local.start()
    w_local = [pltpu.make_async_copy(w_atr_h.at[core, a], wbuf.at[a], lsem.at[1 + a]) for a in range(3)]
    cross_tap = s * 2
    tow_local = [pltpu.make_async_copy(w_atr_h.at[g, cross_tap], wtow.at[g], lsem.at[5 + g]) for g in range(2)]
    for copy in (tow_local[1], tow_local[0], w_local[1], w_local[0], w_local[2]):
        copy.start()
    one_local = pltpu.make_async_copy(w_one_h, wone, lsem.at[4])
    one_local.start()

    barrier = pltpu.get_barrier_semaphore()
    greet = [partner, beyond] + [peer(axis, d) for axis in AXES for d in (1, 2, 3)]
    for other in greet:
        pl.semaphore_signal(barrier, inc=1, device_id=other, device_id_type=MESH)

    tacc[...] = jnp.zeros_like(tacc)

    column = lax.rem(lax.broadcasted_iota(jnp.int32, (BLK, 256), 0), WIDTH)

    def from_left(value, rate=rate):
        return jnp.where(column >= rate, pltpu.roll(value, rate, 0), 0.0)

    def from_right(value, rate=rate):
        return jnp.where(column < WIDTH - rate, pltpu.roll(value, BLK - rate, 0), 0.0)

    def block(m):
        return pl.ds(pl.multiple_of(m * BLK, 16), BLK)

    def middle(m):
        rows = xbuf[block(XB + m), :]
        for b in range(3):
            tacc[m, b] += mm(rows, wbuf[1, b])

    def outer(m):
        for a in (0, 2):
            to = m - (a - 1) * k

            @pl.when((to >= 0) & (to < 4))
            def _(a=a, to=to):
                rows = xbuf[block(XB + m), :]
                for b in range(3):
                    tacc[to, b] += mm(rows, wbuf[a, b])

    def cross_copy(t, g=None):
        if g is None:
            return remote(cs.at[0, t], cr.at[t], across, UNITS * 12 + t)
        to = (dp, (1 - s) * 2 + g)
        return remote(cs.at[g, t], cr.at[t], to, UNITS * 12 + t, UNITS * 12 + 7 + 3 * g + t)

    def crossing(body):
        for g, t in ((1, 0), (1, 1), (1, 2), (0, 0), (0, 1)):
            m = jnp.where(s == 0, 2 - g + t, t)

            @pl.when(m // 2 == core)
            def _(g=g, t=t, m=m):
                body(g, t, m)

    def cross(g, t, m):
        rows = xbuf[block(XB + m), :]
        parts = [mm(rows, wtow[g, b]) for b in range(3)]
        shifted = from_left(parts[0], 12 + 6 * g) + from_right(parts[2], 12 + 6 * g)
        cs[g, t] = (parts[1] + shifted).astype(BF)

    mine, theirs = 2 * core, 2 * (1 - core)
    x_local.wait()
    for copy in tow_local:
        copy.wait()
    crossing(cross)
    pl.semaphore_wait(barrier, len(greet))
    crossing(lambda g, t, m: cross_copy(t, g).start())
    x_swap = go(remote(feat, xbuf.at[x_own], partner))
    for copy in (w_local[1], w_local[0], w_local[2]):
        copy.wait()
    pl.loop(0, 2)(lambda q: middle(mine + q))
    pl.loop(0, 2)(lambda q: outer(mine + q))
    x_swap.wait_recv()

    @pl.loop(0, 2)
    def _(q):
        middle(theirs + q)
        outer(theirs + q)

    def halo(j, h):
        rows = block(XB + jnp.where(s == 0, 2, 0) + j)
        to = block(jnp.where(s == 0, j, XB + 4 + j))
        lanes = slice(h * 512, h * 512 + 512)
        i = UNITS * 12 + 4 + h
        return remote(xbuf.at[rows, lanes], xbuf.at[to, lanes], (dp, (1 - s) * 2 + j), i, UNITS * 12 + 13 + 2 * j + h)

    def haloes(body):
        @pl.when(core == s)
        def _():
            for j, h in ((0, 0), (0, 1), (1, 0)):
                body(halo(j, h))

        @pl.when(core == 1 - s)
        def _():
            body(halo(1, 1))

    haloes(lambda copy: copy.start())

    @pl.loop(0, 4)
    def _(i):
        pre[block(i), :] = tacc[i, 1] + from_left(tacc[i, 0]) + from_right(tacc[i, 2])

    one_local.wait()

    @pl.when(core == 1)
    def _():
        @pl.loop(0, 4)
        def _(i):
            value = mm(xbuf[block(XB + i), :], wone[...])
            pre0[block(i), :] = value
            joined[0, block(i), :] = silu(value).astype(BF)

    for t in range(3):
        @pl.when(t < k)
        def _(t=t):
            cross_copy(t).wait_recv()
            into = block(jnp.where(s == 0, 4 - k + t, t))
            pre[into, :] += cr[t].astype(F32)

    @pl.loop(0, 4)
    def _(i):
        joined[1 + core, block(i), :] = silu(pre[block(i), :]).astype(BF)

    j_copies = [remote(joined.at[b, other_rows], joined.at[b, other_rows], partner) for b in range(3)]

    @pl.when(core == 0)
    def _():
        j_copies[1].start()

    @pl.when(core == 1)
    def _():
        j_copies[0].start()
        j_copies[2].start()

    @pl.when(core == 0)
    def _():
        j_copies[0].wait_recv()
        j_copies[2].wait_recv()

    @pl.when(core == 1)
    def _():
        j_copies[1].wait_recv()

    pre_hidden = mm(joined[0, own_rows, :], w_proj[0])
    pre_hidden += mm(joined[1, own_rows, :], w_proj[1])
    pre_hidden += mm(joined[2, own_rows, :], w_proj[2])
    hidden = silu(pre_hidden).astype(BF)
    classes = jnp.concatenate([w_cls[...].astype(F32), jnp.zeros((13, 256), F32)]).astype(BF)
    for y in range(12):
        lab[:, y * WIDTH : (y + 1) * WIDTH] = labels[y]
    logits = mm_t(classes, hidden)
    row = lax.broadcasted_iota(jnp.int32, logits.shape, 0)
    valid = row < 3
    top = jnp.max(jnp.where(valid, logits, -jnp.inf), axis=0, keepdims=True)
    total = jnp.sum(jnp.where(valid, jnp.exp(logits - top), 0.0), axis=0, keepdims=True)
    lse = top + jnp.log(total)
    onehot = row == lab[...]
    loss = jnp.sum(lse - jnp.sum(jnp.where(onehot, logits, 0.0), axis=0, keepdims=True), axis=1, keepdims=True)
    probs = jnp.exp(logits - lse) - jnp.where(onehot, 1.0, 0.0)
    dlogits = jnp.where(valid, probs * loss_scale, 0.0).astype(BF)
    dhidden = t_mm(dlogits, classes) * slope(pre_hidden)
    dh[own_rows, :] = dhidden.astype(BF)
    dh_copy = go(remote(dh.at[own_rows], dh.at[own_rows], partner))

    small = mm(dlogits, hidden)
    srow = lax.broadcasted_iota(jnp.int32, small.shape, 0)
    cl_copies = []
    for n, axis in enumerate(AXES):
        cl_copies.append([remote(clbuf.at[n, here[axis]], clbuf.at[n, here[axis]], peer(axis, d)) for d in (1, 2, 3)])
    cl_copies.append([remote(clbuf.at[3, core], clbuf.at[3, core], partner)])
    clbuf[0, here["x"]] = jnp.where(srow == 3, loss, small)
    for copy in cl_copies[0]:
        go(copy)

    def small_step(n):
        for copy in cl_copies[n]:
            copy.wait_recv()
        value = clbuf[n, 0] + clbuf[n, 1]
        if n < 3:
            value = value + clbuf[n, 2] + clbuf[n, 3]
            clbuf[n + 1, core if n == 2 else here[AXES[n + 1]]] = value
            for copy in cl_copies[n + 1]:
                go(copy)
        else:
            o_cls[...] = value

    branch_w = w_proj[1 + core]

    raw_copy = remote(raw.at[block(jnp.where(s == 0, 3, 0))], hraw, across, UNITS * 12 + 3)

    def branch_grad(i):
        value = mm_t(dh[block(i), :], branch_w) * slope(pre[block(i), :])
        raw[block(i), :] = value.astype(BF)

        @pl.when((core == 1) & (i == jnp.where(s == 0, 3, 0)))
        def _():
            raw_copy.start()

        to = block(BASE + i)
        rounded = value.astype(BF).astype(F32)
        ext[0, to, :] = from_right(rounded).astype(BF)
        ext[1, to, :] = rounded.astype(BF)
        ext[2, to, :] = from_left(rounded).astype(BF)

    def first_grad(first):
        @pl.when(core == 1)
        def _():
            @pl.loop(0, 2)
            def _(q):
                rows = block(first + q)
                db0[rows, :] = (mm_t(dh[rows, :], w_proj[0]) * slope(pre0[rows, :])).astype(BF)

    pl.loop(0, 2)(lambda q: branch_grad(mine + q))
    first_grad(mine)
    dh_copy.wait_recv()
    pl.loop(0, 2)(lambda q: branch_grad(theirs + q))

    low, high = pl.ds(0, 2), pl.ds(2, 2)

    def plan(u, order, ring):
        out = []
        for phase, (buf, landing) in enumerate(((s1, r1), (s2, r2), (s3, r3))):
            axis = order[phase]
            left = [a for a in AXES if a in order[phase:]]
            spot = left.index(axis)
            c = here[axis]
            base = u * 12 + (0, 6, 9)[phase]

            def chunk(at, half=None):
                index = [u] + [slice(None)] * len(left)
                index[1 + spot] = (at + 4) % 4
                if half is not None:
                    index[2 if spot == 0 else 1] = half
                return buf.at[tuple(index)]

            def land(slot, half=None):
                return landing.at[u, slot] if half is None else landing.at[u, slot, half]

            if phase or not ring:
                copies = [remote(chunk(c + d), land(d - 1), peer(axis, d), base + d - 1) for d in (2, 1, 3)]
                out.append((chunk(c), [land(n) for n in range(3)], copies, (), (), ()))
                continue
            up, down = peer(axis, 1), peer(axis, 3)
            way = [
                remote(chunk(c + 2, low), land(2, low), up, base),
                remote(chunk(c + 2, high), land(2, high), down, base + 1),
            ]
            copies = [
                remote(chunk(c + 1, high), land(0, high), up, base + 2),
                remote(chunk(c - 1, low), land(1, low), down, base + 3),
            ]
            later = [
                remote(chunk(c + 1, low), land(0, low), up, base + 4),
                remote(chunk(c - 1, high), land(1, high), down, base + 5),
            ]
            sums = [(chunk(c + 1, low), land(2, low)), (chunk(c - 1, high), land(2, high))]
            out.append((chunk(c), [land(0), land(1)], copies, way, later, sums))
        return u, out

    def send(unit, phase):
        _, _, copies, way, _, _ = unit[1][phase]
        for copy in list(way) + copies:
            go(copy)

    def forward(unit):
        _, _, _, way, later, sums = unit[1][0]
        for n in range(2):
            way[n].wait_recv()
            out, got = sums[n]
            out[...] = (out[...].astype(F32) + got[...].astype(F32)).astype(BF)
            go(later[n])

    def settle(unit, phase):
        u, phases = unit
        own, lands, copies, _, later, _ = phases[phase]
        for copy in copies + list(later):
            copy.wait_recv()
        value = own[...].astype(F32)
        for got in lands:
            value = value + got[...].astype(F32)
        if phase < 2:
            into = (s2, s3)[phase]
            into[u] = value.astype(into.dtype)
            send(unit, phase + 1)
        else:
            fin[u] = value

    mids = [plan(b, MIDDLE[b], True) for b in range(3)]
    nears = [plan(3 + 3 * s + b, OUTER[b], True) for b in range(3)]
    fars = [plan(3 + 3 * (1 - s) + b, OUTER[b], True) for b in range(3)]
    smalls = plan(9, SMALL, False)

    def proj_grad(b):
        return t_mm(joined[b], dh[...]).astype(BF).reshape(4, 4, 16, 256)

    p_copies = [remote(pbuf.at[n], s1.at[9, 2 * n], partner) for n in range(2)]

    def tap(u, rows, grad):
        for c in range(4):
            value = t_mm(xbuf[rows, c * 256 : (c + 1) * 256], grad)
            s1[u, c] = value.astype(BF).reshape(4, 4, 16, 256)

    everyone = pl.ds(XB * BLK, CHIP)

    def rows_from(m, count):
        return pl.ds(pl.multiple_of(m * BLK, 16), count * BLK)

    def middle_tap(b):
        tap(b, everyone, ext[b, rows_from(BASE, 4), :])
        send(mids[b], 0)

    @pl.when(core == 1)
    def _():
        for n in range(2):
            pbuf[n] = proj_grad(2 * n)
            p_copies[n].start()
        first_grad(theirs)
        tap(9, everyone, db0[...])

    @pl.when(core == 0)
    def _():
        s1[9, 1] = proj_grad(1)
        s1[9, 3] = jnp.zeros((4, 4, 16, 256), BF)
        for n in range(2):
            p_copies[n].wait_recv()

    send(smalls, 0)
    middle_tap(0)
    middle_tap(1)
    middle_tap(2)
    passed_rows = block(jnp.where(s == 0, XB + 4, 0) + core)
    passed = []
    for h in range(2):
        piece = xbuf.at[passed_rows, slice(h * 512, h * 512 + 512)]
        remote(piece, piece, across, UNITS * 12 + 4 + h).wait_recv()
        passed.append(go(remote(piece, piece, partner)))

    small_step(0)

    @pl.when(core == 1)
    def _():
        raw_copy.wait_recv()
        to = block(jnp.where(s == 0, BASE + 4, BASE - 1))
        value = hraw[...].astype(F32)
        ext[0, to, :] = from_right(value).astype(BF)
        ext[1, to, :] = hraw[...]
        ext[2, to, :] = from_left(value).astype(BF)

    for b in range(3):
        x_at = XB + jnp.where(s == 0, 0, 2)
        g_at = BASE + jnp.where(s == 0, k, 2 - k)
        tap(nears[b][0], rows_from(x_at, 2), ext[b, rows_from(g_at, 2), :])
        send(nears[b], 0)

    for copy in passed:
        copy.wait_recv()
    for b in range(3):
        for n in range(2):
            @pl.when(core == n)
            def _(n=n, b=b):
                x_at = jnp.where(s == 0, XB + 2 + n, 0)
                g_at = BASE + jnp.where(s == 0, 0, n)
                tap(fars[b][0], rows_from(x_at, 4 - n), ext[b, rows_from(g_at, 4 - n), :])
        send(fars[b], 0)

    settle(smalls, 0)
    for unit in mids:
        forward(unit)
    for unit in nears:
        forward(unit)
    settle(smalls, 1)
    for unit in mids:
        settle(unit, 0)
    for unit in fars:
        forward(unit)
    settle(smalls, 2)

    eout[core, cx, cz, cy] = fin[9].astype(BF)
    everything = slice(None)

    def gather(axis, at):
        view = eout.at[(core,) + at]
        return [remote(view, view, peer(axis, d)) for d in (2, 1, 3)]

    gathers = [gather("z", (cx, cz, cy)), gather("y", (cx, everything, cy)), gather("x", (cx, everything, everything))]

    def gather_next(n):
        for copy in gathers[n - 1] if n else ():
            copy.wait_recv()
        for copy in gathers[n] if n < 3 else ():
            go(copy)

    gather_next(0)
    small_step(1)
    for unit in nears:
        settle(unit, 0)
    gather_next(1)
    for unit in mids:
        settle(unit, 1)
    for unit in fars:
        settle(unit, 0)
    gather_next(2)
    small_step(2)
    for unit in nears:
        settle(unit, 1)
    for unit in mids:
        settle(unit, 2)
    for unit in fars:
        settle(unit, 1)
    small_step(3)
    for unit in nears:
        settle(unit, 2)
    gather_next(3)
    e_swap = go(remote(eout.at[core], eout.at[core], partner))
    for unit in fars:
        settle(unit, 2)

    give = pl.ds(pl.multiple_of((1 - core) * 8, 8), 8)
    keep = pl.ds(pl.multiple_of(core * 8, 8), 8)
    swap[0] = fin[0:9, give, :]
    f_swap = go(remote(swap.at[0], swap.at[1], partner))

    e_swap.wait_recv()
    f_swap.wait_recv()
    for u in range(9):
        at = u + 3 if u < 3 else u - 3 if u < 6 else u
        o_atr[core, at] = fin[u, keep, :]
        o_atr[1 - core, at] = swap[1, u]

    crossing(lambda g, t, m: cross_copy(t, g).wait_send())

    haloes(lambda copy: copy.wait_send())

    @pl.when(core == 1)
    def _():
        raw_copy.wait_send()

    @pl.when(core == 0)
    def _():
        j_copies[1].wait_send()

    @pl.when(core == 1)
    def _():
        for copy in (j_copies[0], j_copies[2], p_copies[0], p_copies[1]):
            copy.wait_send()

    for copy in sends:
        copy.wait_send()
    assert counter[0] <= COPIES


COPIES = 180
UNITS = 10


def widen(scale, shares, small, tiny, o_atr, o_one, o_proj, o_cls, o_loss):
    o_atr[...] = shares[...]
    o_proj[...] = small[0, 0:768].astype(F32)
    o_one[...] = small[1].astype(F32)
    o_cls[...] = tiny[0:3]
    o_loss[...] = tiny[3:4, 0:1] * scale


def on_device(features, labels, w_one, w_atrous, w_proj, w_class):
    total_pix = lax.axis_size("dp") * lax.axis_size("space") * OWN
    vmem = pl.BlockSpec(memory_space=pltpu.VMEM)
    hbm = pl.BlockSpec(memory_space=pl.ANY)
    scratch = [
        ((8 * BLK, 1024), BF),
        ((3, 3, 1024, 256), BF),
        ((2, 3, 1024, 256), BF),
        ((1024, 256), BF),
        ((4, 3, BLK, 256), F32),
        ((CHIP, 256), F32),
        ((CHIP, 256), F32),
        ((2, 3, BLK, 256), BF),
        ((3, BLK, 256), BF),
        ((3, CHIP, 256), BF),
        ((CHIP, 256), BF),
        ((3, 6 * BLK, 256), BF),
        ((CHIP, 256), BF),
        ((CHIP, 256), BF),
        ((BLK, 256), BF),
        ((UNITS, 4, 4, 4, 16, 256), BF),
        ((UNITS, 3, 4, 4, 16, 256), BF),
        ((UNITS, 4, 4, 16, 256), BF),
        ((UNITS, 3, 4, 16, 256), BF),
        ((UNITS, 4, 16, 256), F32),
        ((UNITS, 3, 16, 256), F32),
        ((UNITS, 16, 256), F32),
        ((2, 4, 4, 16, 256), BF),
        ((4, 4, 16, 256), F32),
        ((2, 9, 8, 256), F32),
        ((1, OWN), jnp.int32),
    ]
    shares, small, tiny = pl.pallas_call(
        lambda *refs: kernel(1.0 / math.sqrt(total_pix), *refs),
        out_shape=(
            jax.ShapeDtypeStruct((2, 9, 8, 256), F32),
            jax.ShapeDtypeStruct((2, 4, 4, 4, 16, 256), BF),
            jax.ShapeDtypeStruct((16, 256), F32),
        ),
        in_specs=[hbm, vmem, hbm, hbm, vmem, vmem],
        out_specs=(vmem, vmem, vmem),
        scratch_shapes=[pltpu.VMEM(shape, kind) for shape, kind in scratch]
        + [
            pltpu.SemaphoreType.DMA((7,)),
            pltpu.SemaphoreType.DMA((COPIES,)),
            pltpu.SemaphoreType.DMA((COPIES,)),
        ],
        compiler_params=pltpu.CompilerParams(
            collective_id=0, has_side_effects=True, vmem_limit_bytes=60 * 1024 * 1024
        ),
        name="aspp",
    )(
        features.reshape(OWN, 1024),
        labels.transpose(1, 0, 2),
        w_one,
        w_atrous,
        w_proj.reshape(3, 256, 256),
        w_class.T,
    )
    grad_atrous, grad_one, grad_proj, grad_class, loss = pl.pallas_call(
        lambda *refs: widen(1.0 / total_pix, *refs),
        out_shape=(
            jax.ShapeDtypeStruct((2, 9, 8, 256), F32),
            jax.ShapeDtypeStruct((1024, 256), F32),
            jax.ShapeDtypeStruct((768, 256), F32),
            jax.ShapeDtypeStruct((3, 256), F32),
            jax.ShapeDtypeStruct((1, 1), F32),
        ),
        in_specs=[vmem] * 3,
        out_specs=(vmem,) * 5,
        name="widen",
    )(shares, small.reshape(2, 1024, 256), tiny)
    return (grad_atrous.reshape(2, 3, 3, 8, 256), grad_one, grad_proj, grad_class.T, loss.reshape(()))


def solution(mesh):
    return jax.shard_map(
        on_device,
        mesh=mesh,
        in_specs=(P("dp", "space", None, None), P("dp", "space", None), P(), P(), P(), P()),
        out_specs=(P(None, None, None, ("dp", "space"), None), P(), P(), P(), P()),
        check_vma=False,
    )
```
